512 devices in a mesh: fsdp: 64 (over y, z_hi, core), vocab: 8 (over x, z_lo).
Axes of the slice: x: 4, y: 8, z: 8 (z_hi: 4, z_lo: 2; z = z_hi * 2 + z_lo), core: 2. Of those that a mesh axis runs over, the one named last changes fastest.
Arguments:
- hidden: bfloat16 [4, 128, 8192], P(None, 'fsdp', 'vocab'), may hold values from -6 to 6
- norm_gain: float32 [8192], P('vocab'), may hold values from 0.25 to 1.75
- head: bfloat16 [8192, 32000], P('vocab', 'fsdp'), may hold values from -8 to 8
- targets: int32 [128], P('vocab'), may hold values from 0 to 31999
- scale_index: int32 [4, 128], P(None, 'vocab'), may hold values from 0 to 3
- layer_act: bfloat16 [128, 28672], P('vocab', 'fsdp'), may hold values from -6 to 6
- down_weight: bfloat16 [28672, 8192], P('fsdp', 'vocab'), may hold values from -0.03125 to 0.03125
Outputs:
- loss: float32 [], replicated
- grad_hidden: bfloat16 [4, 128, 8192], P(None, 'fsdp', 'vocab')
- grad_head: bfloat16 [8192, 32000], P('vocab', 'fsdp')
- grad_gain: float32 [8192], P('vocab')
- grad_act: bfloat16 [128, 28672], P('vocab', 'fsdp')
- grad_down: bfloat16 [28672, 8192], P('fsdp', 'vocab')
The draws below stay inside these ranges and needn't reach their ends.
All inputs are finite; a program needn't handle non-finite values.
Results may differ from the reference program's by a relative error of at most 0.0053.
Values may be sent and summed in bfloat16 or wider, within the bound.
A program may use at most 64 MiB of HBM per device.

```python
import math
import jax
import jax.numpy as jnp
import numpy as np
from jax import lax

D = 8192
V = 32000
FF = 28672
EXITS = 4
TOKENS = 128


STRENGTHS = (0.45, 0.65, 0.88)


PAIR_SHIFT = 0.011


HALF_WIDTH = 1.7320508


PLANT_SCORE = 260.0


def drawn(key):
    key = jax.random.fold_in(key, 71)
    key_direction, key_twin, key_columns, key_rows = jax.random.split(key, 4)
    direction = jax.random.uniform(key_direction, (3, D), jnp.float32, -HALF_WIDTH, HALF_WIDTH)
    twin_part = jax.random.uniform(key_twin, (3, D), jnp.float32, -HALF_WIDTH, HALF_WIDTH)
    col_span = V // 6
    columns = jnp.arange(6, dtype=jnp.int32) * col_span + jax.random.randint(key_columns, (6,), 0, col_span, dtype=jnp.int32)
    row_stride = TOKENS // 3
    row_ids = jnp.arange(3, dtype=jnp.int32)[None, :] * row_stride + jax.random.randint(key_rows, (EXITS, 3), 0, row_stride, dtype=jnp.int32)
    return (direction, twin_part, columns, row_ids)


def draw_head(key, part):
    own_key = jax.random.fold_in(key, 5)
    column_scale = (D / 9.0) ** (-0.5)
    direction, twin_part, columns, row_ids = drawn(key)
    clip_bound = min(6.0, 1.0 / column_scale)
    matrix = jax.random.truncated_normal(own_key, -clip_bound, clip_bound, (D, V), jnp.float32) * column_scale
    plant_scale = PLANT_SCORE / D
    lead_cols = columns[0::2]
    pair_cols = columns[1::2]
    matrix = matrix.at[:, lead_cols].set((direction * plant_scale).T)
    matrix = matrix.at[:, pair_cols].set((((1.0 - PAIR_SHIFT) * direction + 0.1 * twin_part) * plant_scale).T)
    return matrix.astype(jnp.bfloat16)


def draw_hidden(key, part):
    own_key = jax.random.fold_in(key, 9)
    direction, twin_part, columns, row_ids = drawn(key)
    key_base = jax.random.fold_in(own_key, 0)
    key_rest = jax.random.fold_in(own_key, 2)
    sample = jax.random.truncated_normal(key_base, -6.0, 6.0, (EXITS, TOKENS, D), jnp.float32)
    strengths = jnp.array(STRENGTHS, jnp.float32)
    others = jnp.sqrt(1.0 - strengths * strengths)
    fresh_noise = jax.random.uniform(key_rest, (EXITS, 3, D), jnp.float32, -HALF_WIDTH, HALF_WIDTH)
    aligned = strengths[None, :, None] * direction[None] + others[None, :, None] * fresh_noise
    exit_ids = jnp.broadcast_to(jnp.arange(EXITS, dtype=jnp.int32)[:, None], (EXITS, 3))
    sample = sample.at[exit_ids, row_ids].set(aligned)
    return sample.astype(jnp.bfloat16)


def draw_scale_index(key, part):
    key = jax.random.fold_in(key, 13)
    base = jax.random.randint(key, (EXITS, TOKENS), 0, 2, dtype=jnp.int32)
    position = jnp.arange(TOKENS, dtype=jnp.int32)
    ramp = 3 * (TOKENS - 1 - position) // TOKENS
    return jnp.minimum(base + ramp[None, :], 3).astype(jnp.int32)


def touch_ends(values, stream_key, low, largest):
    shape = values.shape
    place = [jax.random.randint(jax.random.fold_in(stream_key, axis), (), 0, shape[axis]) for axis in range(len(shape))]
    values = values.at[tuple(place)].set(low)
    longest = shape.index(max(shape))
    place[longest] = (place[longest] + 1) % shape[longest]
    return values.at[tuple(place)].set(largest)


def steps_of(key, shape, cuts, least, top_value):
    level, own = 1.0, jax.random.fold_in(key, 6)
    for dim, shards_of in cuts:
        steps = jnp.exp(jax.random.uniform(jax.random.fold_in(own, dim), (shards_of,), jnp.float32, least / len(cuts), top_value / len(cuts)))
        level = level * jnp.repeat(steps, shape[dim] // shards_of).reshape([-1 if axis == dim else 1 for axis in range(len(shape))])
    return level


def rank_bounds(amount, skew):
    loads = [(1 << 20) // math.isqrt(rank ** skew) + 1 for rank in range(1, amount + 1)]
    scale = 1 + sum(loads) // (1 << 30)
    return np.cumsum(np.array([max(1, weight // scale) for weight in loads]))


def skewed_ids(key, shape, count, lean):
    grid = rank_bounds(count, lean)
    lot = jax.random.randint(jax.random.fold_in(key, 1), shape, 0, int(grid[count - 1]))
    standing = jnp.searchsorted(jnp.asarray(grid, jnp.int32), lot, side="right")
    return jax.random.permutation(jax.random.fold_in(key, 2), count)[standing].astype(jnp.int32)


def scatter_about(key, dims, scale, bound, pieces=(), kind=jnp.bfloat16):
    entries = scale * jax.random.normal(key, dims, jnp.float32)
    if pieces:
        entries = entries * steps_of(key, dims, pieces, -0.22, 0.18)
    return jnp.clip(entries, -bound, bound).astype(kind)


def setup_inputs(seed: int = 0) -> dict:
    seeds = jax.random.split(jax.random.key(seed), 8)
    return {
        "hidden": draw_hidden(jax.random.fold_in(seeds[7], 71), 0),
        "norm_gain": jnp.clip(1.0 + 0.15 * jax.random.normal(seeds[1], (D,), jnp.float32), 0.25, 1.75),
        "head": draw_head(jax.random.fold_in(seeds[7], 71), 0),
        "targets": touch_ends(skewed_ids(seeds[3], (TOKENS,), V, 2), jax.random.fold_in(seeds[3], 3), 0, V - 1).astype(jnp.int32),
        "scale_index": draw_scale_index(jax.random.fold_in(seeds[7], 71), 0),
        "layer_act": scatter_about(seeds[5], (TOKENS, FF), 1.0, 6.0, ((0, 8), (1, 64))),
        "down_weight": scatter_about(seeds[6], (FF, D), FF ** -0.5, 0.03125, ((0, 64), (1, 8))),
    }


EPS = 1e-05

def reference(hidden, norm_gain, head, targets, scale_index, layer_act, down_weight):
    exits, tokens, width = hidden.shape
    h32 = hidden.astype(jnp.float32)
    scale = lax.rsqrt(lax.optimization_barrier(jnp.mean(h32 * h32, axis=-1)) + EPS)
    normed = (h32 * scale[..., None] * norm_gain).astype(jnp.bfloat16)
    flat = normed.reshape(exits * tokens, width)
    logits = jnp.dot(flat, head, preferred_element_type=jnp.float32).reshape(exits, tokens, -1)
    peak = lax.optimization_barrier(jnp.max(logits, axis=-1))
    lse = peak + jnp.log(lax.optimization_barrier(jnp.sum(jnp.exp(logits - peak[..., None]), axis=-1)))
    columns = lax.iota(jnp.int32, logits.shape[-1])
    onehot = columns[None, None, :] == targets[None, :, None]
    picked = lax.optimization_barrier(jnp.sum(jnp.where(onehot, logits, 0.0), axis=-1))
    weights = jnp.exp2((4 - scale_index).astype(jnp.float32))
    loss = jnp.sum(weights * (lse - picked)) / (exits * tokens)
    prob = jnp.exp(logits - lse[..., None])
    dlogits = (weights[..., None] * (prob - onehot.astype(jnp.float32))).astype(jnp.bfloat16)
    dflat = dlogits.reshape(exits * tokens, -1)
    grad_head = lax.dot_general(flat, dflat, (((0,), (0,)), ((), ())), preferred_element_type=jnp.float32).astype(jnp.bfloat16)
    grad_normed = lax.dot_general(dflat, head, (((1,), (1,)), ((), ())), preferred_element_type=jnp.float32).reshape(exits, tokens, width)
    grad_gain = lax.optimization_barrier(jnp.sum(grad_normed * h32 * scale[..., None], axis=(0, 1)))
    gated = grad_normed * norm_gain
    inner = lax.optimization_barrier(jnp.sum(gated * h32, axis=-1))
    cubed = scale * scale * scale
    grad_hidden = (scale[..., None] * gated - h32 * (cubed * inner / width)[..., None]).astype(jnp.bfloat16)
    last_rows = grad_hidden[exits - 1]
    grad_down = lax.dot_general(layer_act, last_rows, (((0,), (0,)), ((), ())), preferred_element_type=jnp.float32).astype(jnp.bfloat16)
    grad_act = lax.dot_general(last_rows, down_weight, (((1,), (1,)), ((), ())), preferred_element_type=jnp.float32).astype(jnp.bfloat16)
    return (loss, grad_hidden, grad_head, grad_gain, grad_act, grad_down)
```

```python
import functools

import jax
import jax.numpy as jnp
from jax import lax
from jax.experimental import pallas as pl
from jax.experimental.pallas import tpu as pltpu
from jax.sharding import PartitionSpec as P

MESH = pl.DeviceIdType.MESH
EPS = 1e-05
F32 = jnp.float32
BF16 = jnp.bfloat16
EXITS = 4
OWN = 8
VP = 512


def send_all(n, me, dev, src, dst, sems):
    def one(j, _):
        p = lax.rem(me + j, n)
        pltpu.make_async_remote_copy(
            src_ref=src(p), dst_ref=dst, send_sem=sems.at[0, j], recv_sem=sems.at[1, me],
            device_id=dev(p), device_id_type=MESH,
        ).start()
        return 0

    lax.fori_loop(1, n, one, 0)


def recv_all(n, me, dev, slot, sems, then=None):
    def one(j, _):
        p = lax.rem(me + j, n)
        pltpu.make_async_remote_copy(
            src_ref=slot(p), dst_ref=slot(p), send_sem=sems.at[0, j], recv_sem=sems.at[1, p],
            device_id=dev(p), device_id_type=MESH,
        ).wait_recv()
        if then is not None:
            then(p)
        return 0

    lax.fori_loop(1, n, one, 0)


def sent_all(n, me, dev, src, sems):
    def one(j, _):
        p = lax.rem(me + j, n)
        pltpu.make_async_remote_copy(
            src_ref=src(p), dst_ref=src(p), send_sem=sems.at[0, j], recv_sem=sems.at[1, p],
            device_id=dev(p), device_id_type=MESH,
        ).wait_send()
        return 0

    lax.fori_loop(1, n, one, 0)


def split3(x):
    hi = x.astype(BF16).astype(F32)
    rest = x - hi
    mid = rest.astype(BF16).astype(F32)
    return hi, mid, rest - mid


def stack(x):
    q = x.shape[1] // 2
    return jnp.concatenate([x[:, :q], x[:, q:]], axis=0)


def kernel(
    ny, nz, nv, vc,
    hid_ref, gain_ref, head_ref, tgt_ref, si_ref, act_ref, dw_ref,
    loss_ref, gh_ref, ghead_ref, ggain_ref, gact_ref, gdown_ref,
    hown, ga1, ga2, act, headp, hr, hg, ssum, lg, rb, st1, st2, df, rowv,
    po, pm, rc, d1, d2, rd1, rd2, d1b, d2b, rd1b, rd2b, ghs, erow, e1, gg1, gg2, lry, lr, fp, rf,
    s_act, s_a1, s_a2, s_a3, s_a4, s_c1, s_c2, s_b, s_s1, s_s2, s_c, s_dc, s_d1, s_d2, s_d3, s_d4,
    s_e1, s_g1, s_e2, s_g2, s_ec, s_f,
):
    width_part = hid_ref.shape[2]
    width = width_part * nv
    half, q = width_part // 2, width_part // 4
    ng = 2 * nz
    rv = OWN * ng
    rh = rv // 2
    rows = rv * ny
    tb = rv // EXITS
    ff = dw_ref.shape[0]

    f = lax.axis_index("fsdp")
    v = lax.axis_index("vocab")
    y = f // ng
    g = f % ng
    z = g // 2
    c = g % 2
    o = 1 - c
    dev_y = lambda p: (p * ng + g, v)
    dev_g = lambda p: (y * ng + p, v)
    dev_z = lambda p: (y * ng + p * 2 + c, v)
    dev_v = lambda p: (f, p)
    dev_c = (y * ng + z * 2 + o, v)

    def to_core(src, dst, ss, rs):
        return pltpu.make_async_remote_copy(
            src_ref=src, dst_ref=dst, send_sem=ss, recv_sem=rs, device_id=dev_c, device_id_type=MESH
        )

    barrier = pltpu.get_barrier_semaphore()

    def greet(n, me, dev):
        def one(j, _):
            pl.semaphore_signal(barrier, inc=1, device_id=dev(lax.rem(me + j, n)), device_id_type=MESH)
            return 0

        lax.fori_loop(1, n, one, 0)

    greet(ny, y, dev_y)
    greet(ng, g, dev_g)
    greet(nv, v, dev_v)

    for e in range(EXITS):
        hown[2 * e : 2 * e + 2, :] = hid_ref[e].astype(F32)
    ga1[c, y, z] = stack(hown[:, :half]).astype(BF16)
    ga2[c, z, y] = stack(hown[:, half:]).astype(BF16)
    act[v, :, :ff] = act_ref[...]
    act[v, :, ff:] = jnp.zeros((act.shape[1], act.shape[2] - ff), BF16)

    pl.semaphore_wait(barrier, ny + ng + nv - 3)

    send_all(nz, z, dev_z, lambda p: ga1.at[c, y, z], ga1.at[c, y, z], s_a1)
    send_all(ny, y, dev_y, lambda p: ga2.at[c, z, y], ga2.at[c, z, y], s_a2)
    recv_all(nz, z, dev_z, lambda p: ga1.at[c, y, p], s_a1)
    send_all(ny, y, dev_y, lambda p: ga1.at[c, y], ga1.at[c, y], s_a3)
    to_core(ga1.at[c, y], ga1.at[c, y], s_c1.at[0, y], s_c1.at[1, y]).start()
    recv_all(ny, y, dev_y, lambda p: ga2.at[c, z, p], s_a2)
    send_all(nz, z, dev_z, lambda p: ga2.at[c, z], ga2.at[c, z], s_a4)
    to_core(ga2.at[c, z], ga2.at[c, z], s_c2.at[0, z], s_c2.at[1, z]).start()
    send_all(nv, v, dev_v, lambda p: act.at[v], act.at[v], s_act)

    cut = vc // 16 * 16
    headp[:cut, :] = head_ref[:cut, :]
    tail = head_ref[cut:vc, :].astype(F32)
    headp[cut:, :] = jnp.concatenate([tail, jnp.zeros((VP - vc, width_part), F32)], axis=0).astype(BF16)

    def forward1(p):
        to_core(ga1.at[c, p], ga1.at[c, p], s_c1.at[0, p], s_c1.at[1, p]).start()

    def forward2(p):
        to_core(ga2.at[c, p], ga2.at[c, p], s_c2.at[0, p], s_c2.at[1, p]).start()

    recv_all(ny, y, dev_y, lambda p: ga1.at[c, p], s_a3, forward1)
    recv_all(nz, z, dev_z, lambda p: ga2.at[c, p], s_a4, forward2)

    def core_in1(p, _):
        to_core(ga1.at[o, p], ga1.at[o, p], s_c1.at[0, p], s_c1.at[1, p]).wait_recv()
        return 0

    def core_in2(p, _):
        to_core(ga2.at[o, p], ga2.at[o, p], s_c2.at[0, p], s_c2.at[1, p]).wait_recv()
        return 0

    lax.fori_loop(0, ny, core_in1, 0)
    lax.fori_loop(0, nz, core_in2, 0)

    def arrange(k, _):
        for cc in range(2):
            for zz in range(0, nz, 2):
                at = pl.ds(pl.multiple_of(k * rv + cc * rh + zz * OWN, 16), 16)
                squares = None
                for h in range(2):
                    a = (ga1[cc, k, zz] if h == 0 else ga2[cc, zz, k]).astype(F32)
                    b = (ga1[cc, k, zz + 1] if h == 0 else ga2[cc, zz + 1, k]).astype(F32)
                    for s in range(2):
                        x = jnp.concatenate([a[s * 8 : s * 8 + 8], b[s * 8 : s * 8 + 8]], axis=0)
                        to = slice((2 * h + s) * q, (2 * h + s + 1) * q)
                        hr[at, to] = x.astype(BF16)
                        hg[at, to] = (x * gain_ref[:, to]).astype(BF16)
                        squares = x * x if squares is None else squares + x * x
                ssum[at, :] = jnp.broadcast_to(jnp.sum(squares, axis=1, keepdims=True), (16, 128))
        return 0

    lax.fori_loop(0, ny, arrange, 0)

    lanes = lax.broadcasted_iota(jnp.int32, (rv, VP), 1)
    mt = min(rows, 256)
    for m in range(0, rows, mt):
        part = lax.dot_general(
            hg[m : m + mt, :], headp[...], (((1,), (1,)), ((), ())), preferred_element_type=F32
        )
        for k in range(mt // rv):
            piece = part[k * rv : (k + 1) * rv]
            own = ssum[m + k * rv : m + (k + 1) * rv, 0:1]
            lg[m // rv + k] = jnp.where(lanes == vc, own, piece)

    send_all(nv, v, dev_v, lambda p: lg.at[p], rb.at[v], s_b)
    rb[v] = lg[v]
    r_id = lax.broadcasted_iota(jnp.int32, (rv, 1), 0)
    exit_id = (r_id & 7) >> 1
    tok_id = (((r_id & (rh - 1)) >> 3) << 2) + ((r_id // rh) << 1) + (r_id & 1)
    l16 = lax.broadcasted_iota(jnp.int32, (rv, tb), 1)
    here = l16 == tok_id
    tgt = jnp.sum(jnp.where(here, tgt_ref[...].astype(F32), 0.0), axis=1, keepdims=True)
    index = jnp.zeros((rv, 1), F32)
    for e in range(EXITS):
        index += jnp.sum(
            jnp.where(here & (exit_id == e), si_ref[e : e + 1, :].astype(F32), 0.0), axis=1, keepdims=True
        )
    weight = jnp.exp2(4.0 - index)
    column = (lanes + f * vc).astype(F32)
    valid = lanes < vc
    onehot = (column == tgt) & valid
    recv_all(nv, v, dev_v, lambda p: rb.at[p], s_b)
    logits = rb[0]
    for p in range(1, nv):
        logits = logits + rb[p]
    scale = lax.rsqrt(logits[:, vc : vc + 1] / width + EPS)
    logits = logits * scale
    peak = jnp.max(jnp.where(valid, logits, -3e38), axis=1, keepdims=True)
    grown = jnp.where(valid, jnp.exp(jnp.minimum(logits - peak, 0.0)), 0.0)
    total = jnp.sum(grown, axis=1, keepdims=True)
    moment = jnp.sum(grown * jnp.where(valid, logits, 0.0), axis=1, keepdims=True)
    picked = jnp.sum(jnp.where(onehot, logits, 0.0), axis=1, keepdims=True)

    eye = lax.broadcasted_iota(jnp.int32, (rv, 128), 0) == lax.broadcasted_iota(jnp.int32, (rv, 128), 1)
    to_row = lambda x: jnp.sum(jnp.where(eye, x, 0.0), axis=0, keepdims=True)
    to_col = lambda x: jnp.sum(jnp.where(eye, x, 0.0), axis=1, keepdims=True)

    def put(ref, at, values):
        for i, value in enumerate(values):
            ref[at, i : i + 1, :] = value
        ref[at, len(values) :, :] = jnp.zeros((8 - len(values), 128), F32)

    def merge(ref, n):
        top = ref[0, 0:1, :]
        for p in range(1, n):
            top = jnp.maximum(top, ref[p, 0:1, :])
        tot = mom = pick = jnp.zeros((1, 128), F32)
        for p in range(n):
            by = jnp.exp(ref[p, 0:1, :] - top)
            tot = tot + by * ref[p, 1:2, :]
            mom = mom + by * ref[p, 2:3, :]
            pick = pick + ref[p, 3:4, :]
        return top, tot, mom, pick

    put(st1, g, [to_row(peak), to_row(total), to_row(moment), to_row(picked)])
    send_all(ng, g, dev_g, lambda p: st1.at[g], st1.at[g], s_s1)
    recv_all(ng, g, dev_g, lambda p: st1.at[p], s_s1)
    put(st2, y, merge(st1, ng))
    send_all(ny, y, dev_y, lambda p: st2.at[y], st2.at[y], s_s2)
    recv_all(ny, y, dev_y, lambda p: st2.at[p], s_s2)
    top, tot, mom, pick = merge(st2, ny)
    lse = to_col(top + jnp.log(tot))
    picked = to_col(pick)
    inner = weight * (to_col(mom / tot) - picked)
    dlog = weight * (jnp.exp(jnp.minimum(logits - lse, 0.0)) - onehot.astype(F32))
    out = jnp.where(valid, dlog, 0.0)
    for i, value in enumerate(split3(scale) + split3(inner) + split3(weight * (lse - picked))):
        out = jnp.where(lanes == vc + i, value, out)
    mine = pl.ds(pl.multiple_of(v * rv, rv), rv)
    df[mine, :] = out.astype(BF16)

    at_v = lambda p: df.at[pl.ds(pl.multiple_of(p * rv, rv), rv)]
    send_all(nv, v, dev_v, lambda p: at_v(v), at_v(v), s_c)
    recv_all(nv, v, dev_v, at_v, s_c)

    def rows_of(core):
        lhs = jnp.concatenate(
            [df[pl.ds(pl.multiple_of(k * rv + core * rh, rh), rh), :] for k in range(ny)], axis=0
        )
        return lax.dot_general(lhs, headp[...], (((1,), (0,)), ((), ())), preferred_element_type=F32)

    po[...] = rows_of(o).reshape(ny, rh, width_part)
    core_d = to_core(po, rc, s_dc.at[0], s_dc.at[1])
    core_d.start()
    pm[...] = rows_of(c).reshape(ny, rh, width_part)
    extra = df[:, vc - vc % 128 :].astype(F32)
    i0 = vc % 128
    pull = lambda i: extra[:, i0 + i : i0 + i + 1] + extra[:, i0 + i + 1 : i0 + i + 2] + extra[:, i0 + i + 2 : i0 + i + 3]
    scale_all = pull(0)
    rowv[:, 0:1] = scale_all
    rowv[:, 1:2] = pull(3)
    loss_ref[...] = jnp.sum(pull(6), axis=0, keepdims=True) / rows
    core_d.wait_recv()

    def pack1(k, _):
        both = pm[k] + rc[k]
        pm[k] = both
        d1[k] = both[:, :half].astype(BF16)
        return 0

    lax.fori_loop(0, ny, pack1, 0)
    send_all(ny, y, dev_y, lambda p: d1.at[p], rd1.at[y], s_d1)
    rd1[y] = d1[y]

    def pack2(k, _):
        for zz in range(nz):
            pair = jnp.concatenate(
                [pm[2 * k, zz * 8 : zz * 8 + 8, half:], pm[2 * k + 1, zz * 8 : zz * 8 + 8, half:]], axis=0
            )
            d2[zz, pl.ds(pl.multiple_of(k * 16, 16), 16), :] = pair.astype(BF16)
        return 0

    lax.fori_loop(0, ny // 2, pack2, 0)
    send_all(nz, z, dev_z, lambda p: d2.at[p], rd2.at[z], s_d2)
    rd2[z] = d2[z]

    def norm(k, _):
        at = pl.ds(pl.multiple_of(k * rv, rv), rv)
        hg[at, :] = (hr[at, :].astype(F32) * rowv[at, 0:1] * gain_ref[...]).astype(BF16)
        return 0

    lax.fori_loop(0, ny, norm, 0)
    wt = min(width_part, 256)
    for m in range(0, width_part, wt):
        part = lax.dot_general(
            df[...], hg[:, m : m + wt], (((0,), (0,)), ((), ())), preferred_element_type=F32
        )
        ghead_ref[:, m : m + wt] = part[:vc].astype(BF16)

    recv_all(ny, y, dev_y, lambda p: rd1.at[p], s_d1)
    sum1 = rd1[0].astype(F32)
    for p in range(1, ny):
        sum1 = sum1 + rd1[p].astype(F32)
    for zz in range(nz):
        d1b[zz] = stack(sum1[zz * 8 : zz * 8 + 8]).astype(BF16)
    send_all(nz, z, dev_z, lambda p: d1b.at[p], rd1b.at[z], s_d3)
    rd1b[z] = d1b[z]
    recv_all(nz, z, dev_z, lambda p: rd2.at[p], s_d2)
    sum2 = rd2[0].astype(F32)
    for p in range(1, nz):
        sum2 = sum2 + rd2[p].astype(F32)
    for k in range(ny):
        d2b[k] = stack(sum2[k * 8 : k * 8 + 8]).astype(BF16)
    send_all(ny, y, dev_y, lambda p: d2b.at[p], rd2b.at[y], s_d4)
    rd2b[y] = d2b[y]
    recv_all(nz, z, dev_z, lambda p: rd1b.at[p], s_d3)
    g1 = rd1b[0].astype(F32)
    for p in range(1, nz):
        g1 = g1 + rd1b[p].astype(F32)
    recv_all(ny, y, dev_y, lambda p: rd2b.at[p], s_d4)
    g2 = rd2b[0].astype(F32)
    for p in range(1, ny):
        g2 = g2 + rd2b[p].astype(F32)
    grad_own = jnp.concatenate([g1[:8], g1[8:], g2[:8], g2[8:]], axis=1)

    own_at = pl.ds(pl.multiple_of(y * rv + c * rh + z * 8, 8), 8)
    scale_own = rowv[own_at, 0:1]
    inner_own = rowv[own_at, 1:2]
    h_own = hown[...]
    grad_hid = scale_own * (grad_own * gain_ref[...]) - h_own * (scale_own * scale_own * inner_own / width)
    ghs[...] = grad_hid
    wk = width_part // 8
    for k in range(8):
        erow[2 * k : 2 * k + 2, :] = ghs[6:8, k * wk : (k + 1) * wk]
    e1[g] = erow[...].astype(BF16)
    send_all(ng, g, dev_g, lambda p: e1.at[g], e1.at[g], s_e1)
    gain_part = jnp.sum(grad_own * h_own * scale_own, axis=0, keepdims=True)
    for k in range(8):
        gg1[g, k : k + 1, :] = gain_part[:, k * wk : (k + 1) * wk]
    send_all(ng, g, dev_g, lambda p: gg1.at[g], gg1.at[g], s_g1)
    for e in range(EXITS):
        gh_ref[e] = ghs[2 * e : 2 * e + 2, :].astype(BF16)

    recv_all(ng, g, dev_g, lambda p: e1.at[p], s_e1)
    for p in range(ng):
        block = e1[p].astype(F32)
        for k in range(8):
            lry[2 * p : 2 * p + 2, k * wk : (k + 1) * wk] = block[2 * k : 2 * k + 2]
    lr[y] = lry[...].astype(BF16)
    half_of = lambda p, core: lr.at[p, :, pl.ds(pl.multiple_of(core * half, half), half)]
    send_all(ny, y, dev_y, lambda p: half_of(y, c), half_of(y, c), s_e2)
    recv_all(ng, g, dev_g, lambda p: gg1.at[p], s_g1)
    gain_y = gg1[0]
    for p in range(1, ng):
        gain_y = gain_y + gg1[p]
    gg2[y] = gain_y
    send_all(ny, y, dev_y, lambda p: gg2.at[y], gg2.at[y], s_g2)

    def forward_e(p):
        to_core(half_of(p, c), half_of(p, c), s_ec.at[0, p], s_ec.at[1, p]).start()

    recv_all(ny, y, dev_y, lambda p: half_of(p, c), s_e2, forward_e)
    recv_all(nv, v, dev_v, lambda p: act.at[p], s_act)

    def core_in_e(j, _):
        p = lax.rem(y + j, ny)
        to_core(half_of(p, o), half_of(p, o), s_ec.at[0, p], s_ec.at[1, p]).wait_recv()
        return 0

    lax.fori_loop(1, ny, core_in_e, 0)
    tokens = ny * lr.shape[1]
    last = lr[...].reshape(tokens, width_part)
    part = lax.dot_general(last, dw_ref[...], (((1,), (1,)), ((), ())), preferred_element_type=F32)
    tv = tokens // nv
    for p in range(nv):
        fp[p] = part[p * tv : (p + 1) * tv]
    send_all(nv, v, dev_v, lambda p: fp.at[p], rf.at[v], s_f)
    rf[v] = fp[v]
    acts = act[...].reshape(tokens, act.shape[2])
    down = lax.dot_general(acts, last, (((0,), (0,)), ((), ())), preferred_element_type=F32)
    gdown_ref[...] = down[:ff].astype(BF16)
    recv_all(ny, y, dev_y, lambda p: gg2.at[p], s_g2)
    gain_all = gg2[0]
    for p in range(1, ny):
        gain_all = gain_all + gg2[p]
    for k in range(8):
        ggain_ref[:, k * wk : (k + 1) * wk] = gain_all[k : k + 1, :]
    recv_all(nv, v, dev_v, lambda p: rf.at[p], s_f)
    acc = rf[0]
    for p in range(1, nv):
        acc = acc + rf[p]
    gact_ref[...] = acc.astype(BF16)

    sent_all(nz, z, dev_z, lambda p: ga1.at[c, y, z], s_a1)
    sent_all(ny, y, dev_y, lambda p: ga2.at[c, z, y], s_a2)
    sent_all(ny, y, dev_y, lambda p: ga1.at[c, y], s_a3)
    sent_all(nz, z, dev_z, lambda p: ga2.at[c, z], s_a4)
    sent_all(nv, v, dev_v, lambda p: act.at[v], s_act)

    def core_out1(p, _):
        to_core(ga1.at[c, p], ga1.at[c, p], s_c1.at[0, p], s_c1.at[1, p]).wait_send()
        return 0

    def core_out2(p, _):
        to_core(ga2.at[c, p], ga2.at[c, p], s_c2.at[0, p], s_c2.at[1, p]).wait_send()
        return 0

    def core_out_e(j, _):
        p = lax.rem(y + j, ny)
        to_core(half_of(p, c), half_of(p, c), s_ec.at[0, p], s_ec.at[1, p]).wait_send()
        return 0

    lax.fori_loop(0, ny, core_out1, 0)
    lax.fori_loop(0, nz, core_out2, 0)
    lax.fori_loop(1, ny, core_out_e, 0)
    sent_all(nv, v, dev_v, lambda p: lg.at[p], s_b)
    sent_all(ng, g, dev_g, lambda p: st1.at[g], s_s1)
    sent_all(ny, y, dev_y, lambda p: st2.at[y], s_s2)
    sent_all(nv, v, dev_v, lambda p: at_v(v), s_c)
    core_d.wait_send()
    sent_all(ny, y, dev_y, lambda p: d1.at[p], s_d1)
    sent_all(nz, z, dev_z, lambda p: d2.at[p], s_d2)
    sent_all(nz, z, dev_z, lambda p: d1b.at[p], s_d3)
    sent_all(ny, y, dev_y, lambda p: d2b.at[p], s_d4)
    sent_all(ng, g, dev_g, lambda p: e1.at[g], s_e1)
    sent_all(ng, g, dev_g, lambda p: gg1.at[g], s_g1)
    sent_all(ny, y, dev_y, lambda p: half_of(y, c), s_e2)
    sent_all(ny, y, dev_y, lambda p: gg2.at[y], s_g2)
    sent_all(nv, v, dev_v, lambda p: fp.at[p], s_f)


def body(ny, nz, hidden, norm_gain, head, targets, scale_index, layer_act, down_weight):
    nv = lax.axis_size("vocab")
    exits, own_tokens, w = hidden.shape
    vc = head.shape[1]
    tok_v, ff = layer_act.shape
    fpad = -(-ff // 128) * 128
    ng = 2 * nz
    rv = OWN * ng
    rh = rv // 2
    rows = rv * ny
    half, q, wk = w // 2, w // 4, w // 8
    tok_y = own_tokens * ng
    vm = pltpu.VMEM
    dma = lambda n: pltpu.SemaphoreType.DMA((2, n))
    scratch = [
        vm((OWN, w), F32), vm((2, ny, nz, 16, q), BF16), vm((2, nz, ny, 16, q), BF16),
        vm((nv, tok_v, fpad), BF16), vm((VP, w), BF16), vm((rows, w), BF16), vm((rows, w), BF16),
        vm((rows, 128), F32), vm((nv, rv, VP), F32), vm((nv, rv, VP), F32),
        vm((ng, 8, 128), F32), vm((ny, 8, 128), F32), vm((rows, VP), BF16), vm((rows, 128), F32),
        vm((ny, rh, w), F32), vm((ny, rh, w), F32), vm((ny, rh, w), F32),
        vm((ny, rh, half), BF16), vm((nz, ny * 8, half), BF16),
        vm((ny, rh, half), BF16), vm((nz, ny * 8, half), BF16),
        vm((nz, 16, q), BF16), vm((ny, 16, q), BF16), vm((nz, 16, q), BF16), vm((ny, 16, q), BF16),
        vm((OWN, w), F32), vm((16, wk), F32), vm((ng, 16, wk), BF16),
        vm((ng, 8, wk), F32), vm((ny, 8, wk), F32),
        vm((tok_y, w), F32), vm((ny, tok_y, w), BF16),
        vm((nv, tok_v, ff), F32), vm((nv, tok_v, ff), F32),
        dma(nv), dma(nz), dma(ny), dma(ny), dma(nz), dma(ny), dma(nz), dma(nv), dma(ng), dma(ny), dma(nv),
        pltpu.SemaphoreType.DMA((2,)), dma(ny), dma(nz), dma(nz), dma(ny),
        dma(ng), dma(ng), dma(ny), dma(ny), dma(ny), dma(nv),
    ]
    spec = pl.BlockSpec(memory_space=vm)
    sds = jax.ShapeDtypeStruct
    loss, grad_hidden, grad_head, grad_gain, grad_act, grad_down = pl.pallas_call(
        functools.partial(kernel, ny, nz, nv, vc),
        out_shape=(
            sds((1, 1), F32), sds(hidden.shape, BF16), sds((vc, w), BF16), sds((1, w), F32),
            sds(layer_act.shape, BF16), sds(down_weight.shape, BF16),
        ),
        in_specs=[spec] * 7,
        out_specs=(spec,) * 6,
        scratch_shapes=scratch,
        compiler_params=pltpu.CompilerParams(
            collective_id=0, has_side_effects=True, vmem_limit_bytes=56 * 1024 * 1024
        ),
    )(
        hidden, norm_gain.reshape(1, w), head.T, targets.reshape(1, -1), scale_index, layer_act, down_weight
    )
    return loss[0, 0], grad_hidden, grad_head.T, grad_gain.reshape(w), grad_act, grad_down


def solution(mesh, ny=8, nz=4):
    return jax.shard_map(
        functools.partial(body, ny, nz),
        mesh=mesh,
        in_specs=(
            P(None, "fsdp", "vocab"),
            P("vocab"),
            P("vocab", "fsdp"),
            P("vocab"),
            P(None, "vocab"),
            P("vocab", "fsdp"),
            P("fsdp", "vocab"),
        ),
        out_specs=(
            P(),
            P(None, "fsdp", "vocab"),
            P("vocab", "fsdp"),
            P("vocab"),
            P("vocab", "fsdp"),
            P("fsdp", "vocab"),
        ),
        check_vma=False,
    )
```

```python
import functools

import jax
import jax.numpy as jnp
from jax import lax
from jax.experimental import pallas as pl
from jax.experimental.pallas import tpu as pltpu
from jax.sharding import PartitionSpec as P

MESH = pl.DeviceIdType.MESH
EPS = 1e-05
F32 = jnp.float32
BF16 = jnp.bfloat16
EXITS = 4
OWN = 8
VP = 512


class Exchange:
    def __init__(self, n, me, dev, src, slot, sems):
        self.n, self.me, self.dev, self.src, self.slot, self.sems = n, me, dev, src, slot, sems

    def copy(self, p, j, src, dst, recv):
        return pltpu.make_async_remote_copy(
            src_ref=src, dst_ref=dst, send_sem=self.sems.at[0, j], recv_sem=self.sems.at[1, recv],
            device_id=self.dev(p), device_id_type=MESH,
        )

    def each(self, do):
        def one(j, _):
            do(lax.rem(self.me + j, self.n), j)
            return 0

        lax.fori_loop(1, self.n, one, 0)

    def start(self):
        self.each(lambda p, j: self.copy(p, j, self.src(p), self.slot(self.me), self.me).start())
        return self

    def recv(self, then=None):
        def one(p, j):
            self.copy(p, j, self.slot(p), self.slot(p), p).wait_recv()
            if then is not None:
                then(p)

        self.each(one)

    def sent(self):
        self.each(lambda p, j: self.copy(p, j, self.src(p), self.slot(self.me), self.me).wait_send())


def split3(x):
    hi = x.astype(BF16).astype(F32)
    rest = x - hi
    mid = rest.astype(BF16).astype(F32)
    return hi, mid, rest - mid


def stack(x):
    q = x.shape[1] // 2
    return jnp.concatenate([x[:, :q], x[:, q:]], axis=0)


def kernel(
    ny, nz, nv, vc,
    hid_ref, gain_ref, head_ref, tgt_ref, si_ref, act_ref, dw_ref,
    loss_ref, gh_ref, ghead_ref, ggain_ref, gact_ref, gdown_ref,
    hown, ga, act, headv, headp, dwv, gheadv, gdownv, hr, hg, lg, rb, st1, st2, df, rowv,
    po, pm, rc, d1, d2, rd1, rd2, d1b, d2b, rd1b, rd2b, ghs, erow, e1, gg1, gg2, lry, lr, fp, rf,
    s_act, s_in, s_out, r_a, s_a0z, s_a0y, s_a1y, s_a1z, s_ac, s_b, s_s1, s_s2, s_c, s_dc, s_d1, s_d2, s_d3, s_d4,
    s_e1, s_g1, s_e2, s_g2, s_ec, s_f,
):
    width_part = hid_ref.shape[2]
    width = width_part * nv
    half, q = width_part // 2, width_part // 4
    ng = 2 * nz
    rv = OWN * ng
    rh = rv // 2
    rows = rv * ny
    tb = rv // EXITS
    ff = dw_ref.shape[0]

    f = lax.axis_index("fsdp")
    v = lax.axis_index("vocab")
    y = f // ng
    g = f % ng
    z = g // 2
    c = g % 2
    o = 1 - c
    dev_y = lambda p: (p * ng + g, v)
    dev_g = lambda p: (y * ng + p, v)
    dev_z = lambda p: (y * ng + p * 2 + c, v)
    dev_v = lambda p: (f, p)
    dev_c = (y * ng + z * 2 + o, v)

    def to_core(src, dst, ss, rs):
        return pltpu.make_async_remote_copy(
            src_ref=src, dst_ref=dst, send_sem=ss, recv_sem=rs, device_id=dev_c, device_id_type=MESH
        )

    barrier = pltpu.get_barrier_semaphore()

    def greet(n, me, dev):
        def one(j, _):
            pl.semaphore_signal(barrier, inc=1, device_id=dev(lax.rem(me + j, n)), device_id_type=MESH)
            return 0

        lax.fori_loop(1, n, one, 0)

    load_head = pltpu.make_async_copy(head_ref, headv, s_in.at[0])
    load_down = pltpu.make_async_copy(dw_ref, dwv, s_in.at[1])
    greet(ny, y, dev_y)
    greet(ng, g, dev_g)
    greet(nv, v, dev_v)
    load_head.start()
    load_down.start()

    for e in range(EXITS):
        hown[2 * e : 2 * e + 2, :] = hid_ref[e].astype(F32)
    ga[c, y, z, 0] = stack(hown[:, :half]).astype(BF16)
    ga[c, y, z, 1] = stack(hown[:, half:]).astype(BF16)
    act[v, :, :ff] = act_ref[...]
    act[v, :, ff:] = jnp.zeros((act.shape[1], act.shape[2] - ff), BF16)

    pl.semaphore_wait(barrier, ny + ng + nv - 3)

    half_of = lambda p, core: lr.at[p, :, pl.ds(pl.multiple_of(core * half, half), half)]
    at_v = lambda p: df.at[pl.ds(pl.multiple_of(p * rv, rv), rv)]
    in_y = functools.partial(Exchange, ny, y, dev_y)
    in_z = functools.partial(Exchange, nz, z, dev_z)
    in_g = functools.partial(Exchange, ng, g, dev_g)
    in_v = functools.partial(Exchange, nv, v, dev_v)
    x_act = in_v(lambda p: act.at[v], lambda p: act.at[p], s_act)
    x_b = in_v(lambda p: lg.at[p], lambda p: rb.at[p], s_b)
    x_s1 = in_g(lambda p: st1.at[g], lambda p: st1.at[p], s_s1)
    x_s2 = in_y(lambda p: st2.at[y], lambda p: st2.at[p], s_s2)
    x_c = in_v(lambda p: at_v(v), at_v, s_c)
    x_d1 = in_y(lambda p: d1.at[p], lambda p: rd1.at[p], s_d1)
    x_d2 = in_z(lambda p: d2.at[p], lambda p: rd2.at[p], s_d2)
    x_d3 = in_z(lambda p: d1b.at[p], lambda p: rd1b.at[p], s_d3)
    x_d4 = in_y(lambda p: d2b.at[p], lambda p: rd2b.at[p], s_d4)
    x_e1 = in_g(lambda p: e1.at[g], lambda p: e1.at[p], s_e1)
    x_g1 = in_g(lambda p: gg1.at[g], lambda p: gg1.at[p], s_g1)
    x_e2 = in_y(lambda p: half_of(y, c), lambda p: half_of(p, c), s_e2)
    x_g2 = in_y(lambda p: gg2.at[y], lambda p: gg2.at[p], s_g2)
    x_f = in_v(lambda p: fp.at[p], lambda p: rf.at[p], s_f)

    def block(dev, p, h, yy, zz, send):
        ref = ga.at[c, yy, zz, h]
        return pltpu.make_async_remote_copy(
            src_ref=ref, dst_ref=ref, send_sem=send, recv_sem=r_a.at[h, yy, zz],
            device_id=dev(p), device_id_type=MESH,
        )

    def each(n, me, do):
        def one(j, _):
            do(lax.rem(me + j, n), j)
            return 0

        lax.fori_loop(1, n, one, 0)

    own_z = lambda p, j: block(dev_z, p, 0, y, z, s_a0z.at[j])
    own_y = lambda p, j: block(dev_y, p, 1, y, z, s_a1y.at[j])
    on_y = lambda zz: lambda p, j: block(dev_y, p, 0, y, zz, s_a0y.at[zz, j])
    on_z = lambda yy: lambda p, j: block(dev_z, p, 1, yy, z, s_a1z.at[yy, j])
    begin = lambda make: lambda p, j: make(p, j).start()
    finish = lambda make: lambda p, j: make(p, j).wait_send()

    def arrived(h, yy, zz):
        block(dev_y, y, h, yy, zz, s_a0z.at[0]).wait_recv()

    each(nz, z, begin(own_z))
    each(ny, y, begin(own_y))
    each(ny, y, begin(on_y(z)))
    each(nz, z, begin(on_z(y)))
    x_act.start()

    load_head.wait()
    cut = vc // 16 * 16
    headp[:cut, :] = headv[:cut, :]
    tail = headv[cut:vc, :].astype(F32)
    headp[cut:, :] = jnp.concatenate([tail, jnp.zeros((VP - vc, width_part), F32)], axis=0).astype(BF16)

    for d in range(1, max(ny, nz) // 2 + 1):
        for shift in (d, -d):
            if d <= ny // 2 and (shift > 0 or 2 * d < ny):
                yy = lax.rem(y + shift + ny, ny)
                arrived(1, yy, z)
                each(nz, z, begin(on_z(yy)))
            if d <= nz // 2 and (shift > 0 or 2 * d < nz):
                zz = lax.rem(z + shift + nz, nz)
                arrived(0, y, zz)
                each(ny, y, begin(on_y(zz)))

    def across(yy):
        ref = ga.at[c, yy]
        return to_core(ref, ref, s_ac.at[0, yy], s_ac.at[1, yy])

    def nearest(j):
        return lax.rem(y + ny + jnp.where(j % 2 == 1, (j + 1) // 2, -(j // 2)), ny)

    def line_of(j, _):
        yy = nearest(j)

        @pl.when(j > 0)
        def _():
            lax.fori_loop(0, nz, lambda zz, _: (arrived(0, yy, zz), 0)[1], 0)

        each(nz, z, lambda p, _: arrived(1, yy, p))
        across(yy).start()
        return 0

    lanes = lax.broadcasted_iota(jnp.int32, (rv, VP), 1)

    def to_tokens(k):
        return pltpu.make_async_remote_copy(
            src_ref=lg.at[k], dst_ref=rb.at[v], send_sem=s_b.at[0, k], recv_sem=s_b.at[1, v],
            device_id=dev_v(k), device_id_type=MESH,
        )

    def rows_in(j):
        k = nearest(j)
        to_core(ga.at[o, k], ga.at[o, k], s_ac.at[0, k], s_ac.at[1, k]).wait_recv()
        at = pl.ds(pl.multiple_of(k * rv, rv), rv)
        sums = []
        for cc in range(2):
            for zz in range(0, nz, 2):
                to_at = pl.ds(pl.multiple_of(k * rv + cc * rh + zz * OWN, 16), 16)
                squares = None
                for h in range(2):
                    a = ga[cc, k, zz, h].astype(F32)
                    b = ga[cc, k, zz + 1, h].astype(F32)
                    for s in range(2):
                        x = jnp.concatenate([a[s * 8 : s * 8 + 8], b[s * 8 : s * 8 + 8]], axis=0)
                        to = slice((2 * h + s) * q, (2 * h + s + 1) * q)
                        hr[to_at, to] = x.astype(BF16)
                        hg[to_at, to] = (x * gain_ref[:, to]).astype(BF16)
                        squares = x * x if squares is None else squares + x * x
                sums.append(jnp.sum(squares, axis=1, keepdims=True))
        part = lax.dot_general(
            hg[at, :], headp[...], (((1,), (1,)), ((), ())), preferred_element_type=F32
        )
        lg[k] = jnp.where(lanes == vc, jnp.concatenate(sums, axis=0), part)

        @pl.when(k != v)
        def _():
            to_tokens(k).start()

        @pl.when(k == v)
        def _():
            rb[v] = lg[v]

    line_of(0, 0)

    def step(j, _):
        line_of(j, 0)
        rows_in(j - 1)
        return 0

    lax.fori_loop(1, ny, step, 0)
    rows_in(ny - 1)

    r_id = lax.broadcasted_iota(jnp.int32, (rv, 1), 0)
    exit_id = (r_id & 7) >> 1
    tok_id = (((r_id & (rh - 1)) >> 3) << 2) + ((r_id // rh) << 1) + (r_id & 1)
    l16 = lax.broadcasted_iota(jnp.int32, (rv, tb), 1)
    here = l16 == tok_id
    tgt = jnp.sum(jnp.where(here, tgt_ref[...].astype(F32), 0.0), axis=1, keepdims=True)
    index = jnp.zeros((rv, 1), F32)
    for e in range(EXITS):
        index += jnp.sum(
            jnp.where(here & (exit_id == e), si_ref[e : e + 1, :].astype(F32), 0.0), axis=1, keepdims=True
        )
    weight = jnp.exp2(4.0 - index)
    column = (lanes + f * vc).astype(F32)
    valid = lanes < vc
    onehot = (column == tgt) & valid
    x_b.recv()
    logits = rb[0]
    for p in range(1, nv):
        logits = logits + rb[p]
    scale = lax.rsqrt(logits[:, vc : vc + 1] / width + EPS)
    logits = logits * scale
    peak = jnp.max(jnp.where(valid, logits, -3e38), axis=1, keepdims=True)
    grown = jnp.where(valid, jnp.exp(jnp.minimum(logits - peak, 0.0)), 0.0)
    total = jnp.sum(grown, axis=1, keepdims=True)
    moment = jnp.sum(grown * jnp.where(valid, logits, 0.0), axis=1, keepdims=True)
    picked = jnp.sum(jnp.where(onehot, logits, 0.0), axis=1, keepdims=True)

    eye = lax.broadcasted_iota(jnp.int32, (rv, 128), 0) == lax.broadcasted_iota(jnp.int32, (rv, 128), 1)
    to_row = lambda x: jnp.sum(jnp.where(eye, x, 0.0), axis=0, keepdims=True)
    to_col = lambda x: jnp.sum(jnp.where(eye, x, 0.0), axis=1, keepdims=True)

    def put(ref, at, values):
        for i, value in enumerate(values):
            ref[at, i : i + 1, :] = value
        ref[at, len(values) :, :] = jnp.zeros((8 - len(values), 128), F32)

    def merge(ref, n):
        top = ref[0, 0:1, :]
        for p in range(1, n):
            top = jnp.maximum(top, ref[p, 0:1, :])
        tot = mom = pick = jnp.zeros((1, 128), F32)
        for p in range(n):
            by = jnp.exp(ref[p, 0:1, :] - top)
            tot = tot + by * ref[p, 1:2, :]
            mom = mom + by * ref[p, 2:3, :]
            pick = pick + ref[p, 3:4, :]
        return top, tot, mom, pick

    put(st1, g, [to_row(peak), to_row(total), to_row(moment), to_row(picked)])
    x_s1.start()
    x_s1.recv()
    put(st2, y, merge(st1, ng))
    x_s2.start()
    x_s2.recv()
    top, tot, mom, pick = merge(st2, ny)
    lse = to_col(top + jnp.log(tot))
    picked = to_col(pick)
    inner = weight * (to_col(mom / tot) - picked)
    dlog = weight * (jnp.exp(jnp.minimum(logits - lse, 0.0)) - onehot.astype(F32))
    out = jnp.where(valid, dlog, 0.0)
    for i, value in enumerate(split3(scale) + split3(inner) + split3(weight * (lse - picked))):
        out = jnp.where(lanes == vc + i, value, out)
    mine = pl.ds(pl.multiple_of(v * rv, rv), rv)
    df[mine, :] = out.astype(BF16)

    x_c.start()
    x_c.recv()

    def rows_of(core):
        lhs = jnp.concatenate(
            [df[pl.ds(pl.multiple_of(k * rv + core * rh, rh), rh), :] for k in range(ny)], axis=0
        )
        return lax.dot_general(lhs, headp[...], (((1,), (0,)), ((), ())), preferred_element_type=F32)

    po[...] = rows_of(o).reshape(ny, rh, width_part)
    core_d = to_core(po, rc, s_dc.at[0], s_dc.at[1])
    core_d.start()
    pm[...] = rows_of(c).reshape(ny, rh, width_part)
    extra = df[:, vc - vc % 128 :].astype(F32)
    i0 = vc % 128
    pull = lambda i: extra[:, i0 + i : i0 + i + 1] + extra[:, i0 + i + 1 : i0 + i + 2] + extra[:, i0 + i + 2 : i0 + i + 3]
    scale_all = pull(0)
    rowv[:, 0:1] = scale_all
    rowv[:, 1:2] = pull(3)
    loss_ref[...] = jnp.sum(pull(6), axis=0, keepdims=True) / rows
    core_d.wait_recv()

    def pack1(k, _):
        both = pm[k] + rc[k]
        pm[k] = both
        d1[k] = both[:, :half].astype(BF16)
        return 0

    lax.fori_loop(0, ny, pack1, 0)
    x_d1.start()
    rd1[y] = d1[y]

    def pack2(k, _):
        for zz in range(nz):
            pair = jnp.concatenate(
                [pm[2 * k, zz * 8 : zz * 8 + 8, half:], pm[2 * k + 1, zz * 8 : zz * 8 + 8, half:]], axis=0
            )
            d2[zz, pl.ds(pl.multiple_of(k * 16, 16), 16), :] = pair.astype(BF16)
        return 0

    lax.fori_loop(0, ny // 2, pack2, 0)
    x_d2.start()
    rd2[z] = d2[z]

    def norm(k, _):
        at = pl.ds(pl.multiple_of(k * rv, rv), rv)
        hg[at, :] = (hr[at, :].astype(F32) * rowv[at, 0:1] * gain_ref[...]).astype(BF16)
        return 0

    lax.fori_loop(0, ny, norm, 0)
    wt = min(width_part, 256)
    for m in range(0, width_part, wt):
        part = lax.dot_general(
            df[...], hg[:, m : m + wt], (((0,), (0,)), ((), ())), preferred_element_type=F32
        )
        gheadv[:, m : m + wt] = part[:vc].astype(BF16)
    store_head = pltpu.make_async_copy(gheadv, ghead_ref, s_out.at[0])
    store_head.start()

    x_d1.recv()
    sum1 = rd1[0].astype(F32)
    for p in range(1, ny):
        sum1 = sum1 + rd1[p].astype(F32)
    for zz in range(nz):
        d1b[zz] = stack(sum1[zz * 8 : zz * 8 + 8]).astype(BF16)
    x_d3.start()
    rd1b[z] = d1b[z]
    x_d2.recv()
    sum2 = rd2[0].astype(F32)
    for p in range(1, nz):
        sum2 = sum2 + rd2[p].astype(F32)
    for k in range(ny):
        d2b[k] = stack(sum2[k * 8 : k * 8 + 8]).astype(BF16)
    x_d4.start()
    rd2b[y] = d2b[y]
    x_d3.recv()
    g1 = rd1b[0].astype(F32)
    for p in range(1, nz):
        g1 = g1 + rd1b[p].astype(F32)
    x_d4.recv()
    g2 = rd2b[0].astype(F32)
    for p in range(1, ny):
        g2 = g2 + rd2b[p].astype(F32)
    grad_own = jnp.concatenate([g1[:8], g1[8:], g2[:8], g2[8:]], axis=1)

    own_at = pl.ds(pl.multiple_of(y * rv + c * rh + z * 8, 8), 8)
    scale_own = rowv[own_at, 0:1]
    inner_own = rowv[own_at, 1:2]
    h_own = hown[...]
    grad_hid = scale_own * (grad_own * gain_ref[...]) - h_own * (scale_own * scale_own * inner_own / width)
    ghs[...] = grad_hid
    wk = width_part // 8
    for k in range(8):
        erow[2 * k : 2 * k + 2, :] = ghs[6:8, k * wk : (k + 1) * wk]
    e1[g] = erow[...].astype(BF16)
    x_e1.start()
    gain_part = jnp.sum(grad_own * h_own * scale_own, axis=0, keepdims=True)
    for k in range(8):
        gg1[g, k : k + 1, :] = gain_part[:, k * wk : (k + 1) * wk]
    x_g1.start()
    for e in range(EXITS):
        gh_ref[e] = ghs[2 * e : 2 * e + 2, :].astype(BF16)

    x_e1.recv()
    for p in range(ng):
        tile = e1[p].astype(F32)
        for k in range(8):
            lry[2 * p : 2 * p + 2, k * wk : (k + 1) * wk] = tile[2 * k : 2 * k + 2]
    lr[y] = lry[...].astype(BF16)
    x_e2.start()
    x_g1.recv()
    gain_y = gg1[0]
    for p in range(1, ng):
        gain_y = gain_y + gg1[p]
    gg2[y] = gain_y
    x_g2.start()

    def forward_e(p):
        to_core(half_of(p, c), half_of(p, c), s_ec.at[0, p], s_ec.at[1, p]).start()

    x_e2.recv(forward_e)
    x_act.recv()

    def core_in_e(j, _):
        p = lax.rem(y + j, ny)
        to_core(half_of(p, o), half_of(p, o), s_ec.at[0, p], s_ec.at[1, p]).wait_recv()
        return 0

    lax.fori_loop(1, ny, core_in_e, 0)
    tokens = ny * lr.shape[1]
    last = lr[...].reshape(tokens, width_part)
    load_down.wait()
    part = lax.dot_general(last, dwv[...], (((1,), (1,)), ((), ())), preferred_element_type=F32)
    tv = tokens // nv
    for p in range(nv):
        fp[p] = part[p * tv : (p + 1) * tv]
    x_f.start()
    rf[v] = fp[v]
    acts = act[...].reshape(tokens, act.shape[2])
    down = lax.dot_general(acts, last, (((0,), (0,)), ((), ())), preferred_element_type=F32)
    gdownv[...] = down[:ff].astype(BF16)
    store_down = pltpu.make_async_copy(gdownv, gdown_ref, s_out.at[1])
    store_down.start()
    x_g2.recv()
    gain_all = gg2[0]
    for p in range(1, ny):
        gain_all = gain_all + gg2[p]
    for k in range(8):
        ggain_ref[:, k * wk : (k + 1) * wk] = gain_all[k : k + 1, :]
    x_f.recv()
    acc = rf[0]
    for p in range(1, nv):
        acc = acc + rf[p]
    gact_ref[...] = acc.astype(BF16)

    each(nz, z, finish(own_z))
    each(ny, y, finish(own_y))
    lax.fori_loop(0, nz, lambda zz, _: (each(ny, y, finish(on_y(zz))), 0)[1], 0)
    lax.fori_loop(0, ny, lambda yy, _: (each(nz, z, finish(on_z(yy))), 0)[1], 0)
    lax.fori_loop(0, ny, lambda yy, _: (across(yy).wait_send(), 0)[1], 0)
    x_act.sent()

    def core_out_e(j, _):
        p = lax.rem(y + j, ny)
        to_core(half_of(p, c), half_of(p, c), s_ec.at[0, p], s_ec.at[1, p]).wait_send()
        return 0

    lax.fori_loop(1, ny, core_out_e, 0)
    each(nv, v, lambda p, _: to_tokens(p).wait_send())
    x_s1.sent()
    x_s2.sent()
    x_c.sent()
    core_d.wait_send()
    x_d1.sent()
    x_d2.sent()
    x_d3.sent()
    x_d4.sent()
    x_e1.sent()
    x_g1.sent()
    x_e2.sent()
    x_g2.sent()
    x_f.sent()
    store_head.wait()
    store_down.wait()


def hand_on_kernel(n, *refs):
    sems = refs[2 * n]
    copies = [pltpu.make_async_copy(refs[i], refs[n + i], sems.at[i]) for i in range(n)]
    for copy in copies:
        copy.start()
    for copy in copies:
        copy.wait()


def hand_on(arrays):
    n = len(arrays)
    hbm = pl.BlockSpec(memory_space=pl.ANY)
    return pl.pallas_call(
        functools.partial(hand_on_kernel, n),
        out_shape=tuple(jax.ShapeDtypeStruct(a.shape, a.dtype) for a in arrays),
        in_specs=[hbm] * n,
        out_specs=(hbm,) * n,
        scratch_shapes=[pltpu.SemaphoreType.DMA((n,))],
        compiler_params=pltpu.CompilerParams(vmem_limit_bytes=56 * 1024 * 1024),
    )(*arrays)


def body(ny, nz, hidden, norm_gain, head, targets, scale_index, layer_act, down_weight):
    nv = lax.axis_size("vocab")
    exits, own_tokens, w = hidden.shape
    vc = head.shape[1]
    tok_v, ff = layer_act.shape
    fpad = -(-ff // 128) * 128
    ng = 2 * nz
    rv = OWN * ng
    rh = rv // 2
    rows = rv * ny
    half, q, wk = w // 2, w // 4, w // 8
    tok_y = own_tokens * ng
    vm = pltpu.VMEM
    sem = lambda *n: pltpu.SemaphoreType.DMA(n)
    dma = lambda n: sem(2, n)
    scratch = [
        vm((OWN, w), F32), vm((2, ny, nz, 2, 16, q), BF16),
        vm((nv, tok_v, fpad), BF16), vm((vc, w), BF16), vm((VP, w), BF16), vm((ff, w), BF16),
        vm((vc, w), BF16), vm((ff, w), BF16), vm((rows, w), BF16), vm((rows, w), BF16),
        vm((nv, rv, VP), F32), vm((nv, rv, VP), F32),
        vm((ng, 8, 128), F32), vm((ny, 8, 128), F32), vm((rows, VP), BF16), vm((rows, 128), F32),
        vm((ny, rh, w), F32), vm((ny, rh, w), F32), vm((ny, rh, w), F32),
        vm((ny, rh, half), BF16), vm((nz, ny * 8, half), BF16),
        vm((ny, rh, half), BF16), vm((nz, ny * 8, half), BF16),
        vm((nz, 16, q), BF16), vm((ny, 16, q), BF16), vm((nz, 16, q), BF16), vm((ny, 16, q), BF16),
        vm((OWN, w), F32), vm((16, wk), F32), vm((ng, 16, wk), BF16),
        vm((ng, 8, wk), F32), vm((ny, 8, wk), F32),
        vm((tok_y, w), F32), vm((ny, tok_y, w), BF16),
        vm((nv, tok_v, ff), F32), vm((nv, tok_v, ff), F32),
        dma(nv), sem(2), sem(2), sem(2, ny, nz), sem(nz), sem(nz, ny), sem(ny), sem(ny, nz), dma(ny),
        dma(nv), dma(ng), dma(ny), dma(nv),
        sem(2), dma(ny), dma(nz), dma(nz), dma(ny),
        dma(ng), dma(ng), dma(ny), dma(ny), dma(ny), dma(nv),
    ]
    spec = pl.BlockSpec(memory_space=vm)
    hbm = pl.BlockSpec(memory_space=pl.ANY)
    sds = jax.ShapeDtypeStruct
    results = pl.pallas_call(
        functools.partial(kernel, ny, nz, nv, vc),
        out_shape=(
            sds((1, 1), F32), sds(hidden.shape, BF16), sds((vc, w), BF16), sds((1, w), F32),
            sds(layer_act.shape, BF16), sds(down_weight.shape, BF16),
        ),
        in_specs=[spec, spec, hbm, spec, spec, spec, hbm],
        out_specs=(spec, spec, hbm, spec, spec, hbm),
        scratch_shapes=scratch,
        compiler_params=pltpu.CompilerParams(
            collective_id=0, has_side_effects=True, vmem_limit_bytes=56 * 1024 * 1024
        ),
    )(
        hidden, norm_gain.reshape(1, w), head.T, targets.reshape(1, -1), scale_index, layer_act, down_weight
    )
    loss, grad_hidden, grad_head, grad_gain, grad_act, grad_down = hand_on(results)
    return loss[0, 0], grad_hidden, grad_head.T, grad_gain.reshape(w), grad_act, grad_down


def solution(mesh, ny=8, nz=4):
    return jax.shard_map(
        functools.partial(body, ny, nz),
        mesh=mesh,
        in_specs=(
            P(None, "fsdp", "vocab"),
            P("vocab"),
            P("vocab", "fsdp"),
            P("vocab"),
            P(None, "vocab"),
            P("vocab", "fsdp"),
            P("fsdp", "vocab"),
        ),
        out_specs=(
            P(),
            P(None, "fsdp", "vocab"),
            P("vocab", "fsdp"),
            P("vocab"),
            P("vocab", "fsdp"),
            P("fsdp", "vocab"),
        ),
        check_vma=False,
    )
```

```python
import functools

import jax
import jax.numpy as jnp
from jax import lax
from jax.experimental import pallas as pl
from jax.experimental.pallas import tpu as pltpu
from jax.sharding import PartitionSpec as P

MESH = pl.DeviceIdType.MESH
EPS = 1e-05
F32 = jnp.float32
BF16 = jnp.bfloat16
EXITS = 4
OWN = 8
VP = 512


class Exchange:
    def __init__(self, n, me, dev, src, slot, sems):
        self.n, self.me, self.dev, self.src, self.slot, self.sems = n, me, dev, src, slot, sems

    def copy(self, p, j, src, dst, recv):
        return pltpu.make_async_remote_copy(
            src_ref=src, dst_ref=dst, send_sem=self.sems.at[0, j], recv_sem=self.sems.at[1, recv],
            device_id=self.dev(p), device_id_type=MESH,
        )

    def each(self, do):
        def one(j, _):
            do(lax.rem(self.me + j, self.n), j)
            return 0

        lax.fori_loop(1, self.n, one, 0)

    def start(self):
        self.each(lambda p, j: self.copy(p, j, self.src(p), self.slot(self.me), self.me).start())
        return self

    def recv(self, then=None):
        def one(p, j):
            self.copy(p, j, self.slot(p), self.slot(p), p).wait_recv()
            if then is not None:
                then(p)

        self.each(one)

    def sent(self):
        self.each(lambda p, j: self.copy(p, j, self.src(p), self.slot(self.me), self.me).wait_send())


def split3(x):
    hi = x.astype(BF16).astype(F32)
    rest = x - hi
    mid = rest.astype(BF16).astype(F32)
    return hi, mid, rest - mid


def stack(x):
    q = x.shape[1] // 2
    return jnp.concatenate([x[:, :q], x[:, q:]], axis=0)


def kernel(
    ny, nz, nv, vc,
    hid_ref, gain_ref, head_ref, tgt_ref, si_ref, act_ref, dw_ref,
    loss_ref, gh_ref, ghead_ref, ggain_ref, gact_ref, gdown_ref,
    hown, ga, act, headv, headp, dwv, gheadv, gdownv, hr, hg, lg, rb, st1, st2, df, rowv,
    po, pm, rc, d1, d2, rd1, rd2, d1b, d2b, rd1b, rd2b, ghs, q1, rq1, rq2, gg1, gg2, ls, lr, fp, rf, gactv,
    s_act, s_in, s_out, r_a, s_a0z, s_a0y, s_a1y, s_a1z, s_ac, s_b, s_s1, s_s2, s_c, s_dc, s_d1, s_d2, s_d3, s_d4,
    s_q1, s_q2, s_e, s_g1, s_g2, s_ec, s_f,
):
    width_part = hid_ref.shape[2]
    width = width_part * nv
    half, q = width_part // 2, width_part // 4
    ng = 2 * nz
    rv = OWN * ng
    rh = rv // 2
    rows = rv * ny
    tb = rv // EXITS
    ff = dw_ref.shape[0]

    f = lax.axis_index("fsdp")
    v = lax.axis_index("vocab")
    y = f // ng
    g = f % ng
    z = g // 2
    c = g % 2
    o = 1 - c
    dev_y = lambda p: (p * ng + g, v)
    dev_g = lambda p: (y * ng + p, v)
    dev_z = lambda p: (y * ng + p * 2 + c, v)
    dev_v = lambda p: (f, p)
    dev_c = (y * ng + z * 2 + o, v)

    def to_core(src, dst, ss, rs):
        return pltpu.make_async_remote_copy(
            src_ref=src, dst_ref=dst, send_sem=ss, recv_sem=rs, device_id=dev_c, device_id_type=MESH
        )

    barrier = pltpu.get_barrier_semaphore()

    def greet(n, me, dev):
        def one(j, _):
            pl.semaphore_signal(barrier, inc=1, device_id=dev(lax.rem(me + j, n)), device_id_type=MESH)
            return 0

        lax.fori_loop(1, n, one, 0)

    load_head = pltpu.make_async_copy(head_ref, headv, s_in.at[0])
    load_down = pltpu.make_async_copy(dw_ref, dwv, s_in.at[1])
    greet(ny, y, dev_y)
    greet(ng, g, dev_g)
    greet(nv, v, dev_v)
    load_head.start()
    load_down.start()

    for e in range(EXITS):
        hown[2 * e : 2 * e + 2, :] = hid_ref[e].astype(F32)
    ga[c, y, z, 0] = stack(hown[:, :half]).astype(BF16)
    ga[c, y, z, 1] = stack(hown[:, half:]).astype(BF16)
    act[v, :, :ff] = act_ref[...]
    act[v, :, ff:] = jnp.zeros((act.shape[1], act.shape[2] - ff), BF16)

    pl.semaphore_wait(barrier, ny + ng + nv - 3)

    at_v = lambda p: df.at[pl.ds(pl.multiple_of(p * rv, rv), rv)]
    in_y = functools.partial(Exchange, ny, y, dev_y)
    in_z = functools.partial(Exchange, nz, z, dev_z)
    in_g = functools.partial(Exchange, ng, g, dev_g)
    in_v = functools.partial(Exchange, nv, v, dev_v)
    x_act = in_v(lambda p: act.at[v], lambda p: act.at[p], s_act)
    x_b = in_v(lambda p: lg.at[p], lambda p: rb.at[p], s_b)
    x_s1 = in_g(lambda p: st1.at[g], lambda p: st1.at[p], s_s1)
    x_s2 = in_y(lambda p: st2.at[y], lambda p: st2.at[p], s_s2)
    x_c = in_v(lambda p: at_v(v), at_v, s_c)
    x_d1 = in_y(lambda p: d1.at[p], lambda p: rd1.at[p], s_d1)
    x_d2 = in_z(lambda p: d2.at[p], lambda p: rd2.at[p], s_d2)
    x_d3 = in_z(lambda p: d1b.at[p], lambda p: rd1b.at[p], s_d3)
    x_d4 = in_y(lambda p: d2b.at[p], lambda p: rd2b.at[p], s_d4)
    x_q1 = in_y(lambda p: q1.at[p], lambda p: rq1.at[p], s_q1)
    x_q2 = in_z(lambda p: rq2.at[z], lambda p: rq2.at[p], s_q2)
    x_e = in_y(lambda p: ls.at[c, y], lambda p: ls.at[c, p], s_e)
    x_g1 = in_y(lambda p: gg1.at[y], lambda p: gg1.at[p], s_g1)
    x_g2 = in_g(lambda p: gg2.at[g], lambda p: gg2.at[p], s_g2)
    x_f = in_v(lambda p: fp.at[p], lambda p: rf.at[p], s_f)

    def block(dev, p, h, yy, zz, send):
        ref = ga.at[c, yy, zz, h]
        return pltpu.make_async_remote_copy(
            src_ref=ref, dst_ref=ref, send_sem=send, recv_sem=r_a.at[h, yy, zz],
            device_id=dev(p), device_id_type=MESH,
        )

    def each(n, me, do):
        def one(j, _):
            do(lax.rem(me + j, n), j)
            return 0

        lax.fori_loop(1, n, one, 0)

    own_z = lambda p, j: block(dev_z, p, 0, y, z, s_a0z.at[j])
    own_y = lambda p, j: block(dev_y, p, 1, y, z, s_a1y.at[j])
    on_y = lambda zz: lambda p, j: block(dev_y, p, 0, y, zz, s_a0y.at[zz, j])
    on_z = lambda yy: lambda p, j: block(dev_z, p, 1, yy, z, s_a1z.at[yy, j])
    begin = lambda make: lambda p, j: make(p, j).start()
    finish = lambda make: lambda p, j: make(p, j).wait_send()

    def arrived(h, yy, zz):
        block(dev_y, y, h, yy, zz, s_a0z.at[0]).wait_recv()

    each(nz, z, begin(own_z))
    each(ny, y, begin(own_y))
    each(ny, y, begin(on_y(z)))
    each(nz, z, begin(on_z(y)))
    x_act.start()

    load_head.wait()
    cut = vc // 16 * 16
    headp[:cut, :] = headv[:cut, :]
    tail = headv[cut:vc, :].astype(F32)
    headp[cut:, :] = jnp.concatenate([tail, jnp.zeros((VP - vc, width_part), F32)], axis=0).astype(BF16)

    for d in range(1, max(ny, nz) // 2 + 1):
        for shift in (d, -d):
            if d <= ny // 2 and (shift > 0 or 2 * d < ny):
                yy = lax.rem(y + shift + ny, ny)
                arrived(1, yy, z)
                each(nz, z, begin(on_z(yy)))
            if d <= nz // 2 and (shift > 0 or 2 * d < nz):
                zz = lax.rem(z + shift + nz, nz)
                arrived(0, y, zz)
                each(ny, y, begin(on_y(zz)))

    def across(yy):
        ref = ga.at[c, yy]
        return to_core(ref, ref, s_ac.at[0, yy], s_ac.at[1, yy])

    def nearest(j):
        return lax.rem(y + ny + jnp.where(j % 2 == 1, (j + 1) // 2, -(j // 2)), ny)

    def line_of(j, _):
        yy = nearest(j)

        @pl.when(j > 0)
        def _():
            lax.fori_loop(0, nz, lambda zz, _: (arrived(0, yy, zz), 0)[1], 0)

        each(nz, z, lambda p, _: arrived(1, yy, p))
        across(yy).start()
        return 0

    lanes = lax.broadcasted_iota(jnp.int32, (rv, VP), 1)

    def to_tokens(k):
        return pltpu.make_async_remote_copy(
            src_ref=lg.at[k], dst_ref=rb.at[v], send_sem=s_b.at[0, k], recv_sem=s_b.at[1, v],
            device_id=dev_v(k), device_id_type=MESH,
        )

    def rows_in(j):
        k = nearest(j)
        to_core(ga.at[o, k], ga.at[o, k], s_ac.at[0, k], s_ac.at[1, k]).wait_recv()
        at = pl.ds(pl.multiple_of(k * rv, rv), rv)
        sums = []
        for cc in range(2):
            for zz in range(0, nz, 2):
                to_at = pl.ds(pl.multiple_of(k * rv + cc * rh + zz * OWN, 16), 16)
                squares = None
                for h in range(2):
                    a = ga[cc, k, zz, h].astype(F32)
                    b = ga[cc, k, zz + 1, h].astype(F32)
                    for s in range(2):
                        x = jnp.concatenate([a[s * 8 : s * 8 + 8], b[s * 8 : s * 8 + 8]], axis=0)
                        to = slice((2 * h + s) * q, (2 * h + s + 1) * q)
                        hr[to_at, to] = x.astype(BF16)
                        hg[to_at, to] = (x * gain_ref[:, to]).astype(BF16)
                        squares = x * x if squares is None else squares + x * x
                sums.append(jnp.sum(squares, axis=1, keepdims=True))
        part = lax.dot_general(
            hg[at, :], headp[...], (((1,), (1,)), ((), ())), preferred_element_type=F32
        )
        lg[k] = jnp.where(lanes == vc, jnp.concatenate(sums, axis=0), part)

        @pl.when(k != v)
        def _():
            to_tokens(k).start()

        @pl.when(k == v)
        def _():
            rb[v] = lg[v]

    line_of(0, 0)

    def step(j, _):
        line_of(j, 0)
        rows_in(j - 1)
        return 0

    lax.fori_loop(1, ny, step, 0)
    rows_in(ny - 1)

    r_id = lax.broadcasted_iota(jnp.int32, (rv, 1), 0)
    exit_id = (r_id & 7) >> 1
    tok_id = (((r_id & (rh - 1)) >> 3) << 2) + ((r_id // rh) << 1) + (r_id & 1)
    l16 = lax.broadcasted_iota(jnp.int32, (rv, tb), 1)
    here = l16 == tok_id
    tgt = jnp.sum(jnp.where(here, tgt_ref[...].astype(F32), 0.0), axis=1, keepdims=True)
    index = jnp.zeros((rv, 1), F32)
    for e in range(EXITS):
        index += jnp.sum(
            jnp.where(here & (exit_id == e), si_ref[e : e + 1, :].astype(F32), 0.0), axis=1, keepdims=True
        )
    weight = jnp.exp2(4.0 - index)
    column = (lanes + f * vc).astype(F32)
    valid = lanes < vc
    onehot = (column == tgt) & valid
    x_b.recv()
    logits = rb[0]
    for p in range(1, nv):
        logits = logits + rb[p]
    scale = lax.rsqrt(logits[:, vc : vc + 1] / width + EPS)
    logits = logits * scale
    peak = jnp.max(jnp.where(valid, logits, -3e38), axis=1, keepdims=True)
    grown = jnp.where(valid, jnp.exp(jnp.minimum(logits - peak, 0.0)), 0.0)
    total = jnp.sum(grown, axis=1, keepdims=True)
    moment = jnp.sum(grown * jnp.where(valid, logits, 0.0), axis=1, keepdims=True)
    picked = jnp.sum(jnp.where(onehot, logits, 0.0), axis=1, keepdims=True)

    eye = lax.broadcasted_iota(jnp.int32, (rv, 128), 0) == lax.broadcasted_iota(jnp.int32, (rv, 128), 1)
    to_row = lambda x: jnp.sum(jnp.where(eye, x, 0.0), axis=0, keepdims=True)
    to_col = lambda x: jnp.sum(jnp.where(eye, x, 0.0), axis=1, keepdims=True)

    def put(ref, at, values):
        for i, value in enumerate(values):
            ref[at, i : i + 1, :] = value
        ref[at, len(values) :, :] = jnp.zeros((8 - len(values), 128), F32)

    def merge(ref, n):
        top = ref[0, 0:1, :]
        for p in range(1, n):
            top = jnp.maximum(top, ref[p, 0:1, :])
        tot = mom = pick = jnp.zeros((1, 128), F32)
        for p in range(n):
            by = jnp.exp(ref[p, 0:1, :] - top)
            tot = tot + by * ref[p, 1:2, :]
            mom = mom + by * ref[p, 2:3, :]
            pick = pick + ref[p, 3:4, :]
        return top, tot, mom, pick

    put(st1, g, [to_row(peak), to_row(total), to_row(moment), to_row(picked)])
    x_s1.start()
    x_s1.recv()
    put(st2, y, merge(st1, ng))
    x_s2.start()
    x_s2.recv()
    top, tot, mom, pick = merge(st2, ny)
    lse = to_col(top + jnp.log(tot))
    picked = to_col(pick)
    inner = weight * (to_col(mom / tot) - picked)
    dlog = weight * (jnp.exp(jnp.minimum(logits - lse, 0.0)) - onehot.astype(F32))
    out = jnp.where(valid, dlog, 0.0)
    for i, value in enumerate(split3(scale) + split3(inner) + split3(weight * (lse - picked))):
        out = jnp.where(lanes == vc + i, value, out)
    mine = pl.ds(pl.multiple_of(v * rv, rv), rv)
    df[mine, :] = out.astype(BF16)

    x_c.start()
    x_c.recv()

    def rows_of(core):
        lhs = jnp.concatenate(
            [df[pl.ds(pl.multiple_of(k * rv + core * rh, rh), rh), :] for k in range(ny)], axis=0
        )
        return lax.dot_general(lhs, headp[...], (((1,), (0,)), ((), ())), preferred_element_type=F32)

    po[...] = rows_of(o).reshape(ny, rh, width_part)
    core_d = to_core(po, rc, s_dc.at[0], s_dc.at[1])
    core_d.start()
    pm[...] = rows_of(c).reshape(ny, rh, width_part)
    extra = df[:, vc - vc % 128 :].astype(F32)
    i0 = vc % 128
    pull = lambda i: extra[:, i0 + i : i0 + i + 1] + extra[:, i0 + i + 1 : i0 + i + 2] + extra[:, i0 + i + 2 : i0 + i + 3]
    scale_all = pull(0)
    rowv[:, 0:1] = scale_all
    rowv[:, 1:2] = pull(3)
    loss_ref[...] = jnp.sum(pull(6), axis=0, keepdims=True) / rows
    core_d.wait_recv()

    wk = width_part // 8

    def pack0(k, _):
        both = pm[k] + rc[k]
        pm[k] = both
        last = [both[zz * 8 + 6 : zz * 8 + 8] for zz in range(nz)]
        q1[k] = stack(jnp.concatenate(last, axis=0)).astype(BF16)
        return 0

    lax.fori_loop(0, ny, pack0, 0)
    x_q1.start()
    rq1[y] = q1[y]

    def pack1(k, _):
        d1[k] = pm[k, :, :half].astype(BF16)
        return 0

    lax.fori_loop(0, ny, pack1, 0)
    x_d1.start()
    rd1[y] = d1[y]

    def pack2(k, _):
        for zz in range(nz):
            pair = jnp.concatenate(
                [pm[2 * k, zz * 8 : zz * 8 + 8, half:], pm[2 * k + 1, zz * 8 : zz * 8 + 8, half:]], axis=0
            )
            d2[zz, pl.ds(pl.multiple_of(k * 16, 16), 16), :] = pair.astype(BF16)
        return 0

    lax.fori_loop(0, ny // 2, pack2, 0)
    x_d2.start()
    rd2[z] = d2[z]

    x_q1.recv()
    line = rq1[0].astype(F32)
    for p in range(1, ny):
        line = line + rq1[p].astype(F32)
    rq2[z] = line
    x_q2.start()

    def norm(k, total):
        at = pl.ds(pl.multiple_of(k * rv, rv), rv)
        hg[at, :] = (hr[at, :].astype(F32) * rowv[at, 0:1] * gain_ref[...]).astype(BF16)
        mine = pl.ds(pl.multiple_of(k * rv + c * rh, rh), rh)
        return total + jnp.sum(pm[k] * hr[mine, :].astype(F32) * rowv[mine, 0:1], axis=0, keepdims=True)

    gain_part = lax.fori_loop(0, ny, norm, jnp.zeros((1, width_part), F32))
    for k in range(8):
        gg1[y, k : k + 1, :] = gain_part[:, k * wk : (k + 1) * wk]
    x_g1.start()

    mine = pl.ds(pl.multiple_of(y * rv + c * rh, rh), rh)
    of_last = lambda x: jnp.concatenate([x[zz * 8 + 6 : zz * 8 + 8] for zz in range(nz)], axis=0)
    h_last = of_last(hr[mine, :].astype(F32))
    scale_last = of_last(rowv[mine, 0:1])
    inner_last = of_last(rowv[mine, 1:2])
    x_q2.recv()
    line = rq2[0]
    for p in range(1, nz):
        line = line + rq2[p]
    grad_last = jnp.concatenate([line[: 2 * nz], line[2 * nz :]], axis=1)
    rows_last = scale_last * (grad_last * gain_ref[...]) - h_last * (
        scale_last * scale_last * inner_last / width
    )
    ls[c, y] = stack(rows_last).astype(BF16)

    def pass_on(p):
        ref = ls.at[c, p]
        return to_core(ref, ref, s_ec.at[0, p], s_ec.at[1, p])

    x_e.start()
    pass_on(y).start()

    wt = min(width_part, 256)
    for m in range(0, width_part, wt):
        part = lax.dot_general(
            df[...], hg[:, m : m + wt], (((0,), (0,)), ((), ())), preferred_element_type=F32
        )
        gheadv[:, m : m + wt] = part[:vc].astype(BF16)
    store_head = pltpu.make_async_copy(gheadv, ghead_ref, s_out.at[0])
    store_head.start()
    x_act.recv()

    def acts_in(p, _):
        tile = act[p].astype(F32)
        parts = [tile[zz * 4 + cc * 2 : zz * 4 + cc * 2 + 2] for cc in range(2) for zz in range(nz)]
        act[p] = jnp.concatenate(parts, axis=0).astype(BF16)
        return 0

    x_act.sent()
    lax.fori_loop(0, nv, acts_in, 0)

    x_d1.recv()
    sum1 = rd1[0].astype(F32)
    for p in range(1, ny):
        sum1 = sum1 + rd1[p].astype(F32)
    for zz in range(nz):
        d1b[zz] = stack(sum1[zz * 8 : zz * 8 + 8]).astype(BF16)
    x_d3.start()
    rd1b[z] = d1b[z]
    x_d2.recv()
    sum2 = rd2[0].astype(F32)
    for p in range(1, nz):
        sum2 = sum2 + rd2[p].astype(F32)
    for k in range(ny):
        d2b[k] = stack(sum2[k * 8 : k * 8 + 8]).astype(BF16)
    x_d4.start()
    rd2b[y] = d2b[y]
    x_g1.recv()
    gain_y = gg1[0]
    for p in range(1, ny):
        gain_y = gain_y + gg1[p]
    gg2[g] = gain_y
    x_g2.start()

    x_e.recv(lambda p: pass_on(p).start())

    def rows_out(j, _):
        p = nearest(j)
        ref = ls.at[o, p]
        to_core(ref, ref, s_ec.at[0, p], s_ec.at[1, p]).wait_recv()
        a, b = ls[0, p].astype(F32), ls[1, p].astype(F32)
        lr[p, :, :half] = jnp.concatenate([a[: 2 * nz], b[: 2 * nz]], axis=0).astype(BF16)
        lr[p, :, half:] = jnp.concatenate([a[2 * nz :], b[2 * nz :]], axis=0).astype(BF16)
        return 0

    lax.fori_loop(0, ny, rows_out, 0)
    tokens = ny * lr.shape[1]
    last = lr[...].reshape(tokens, width_part)
    load_down.wait()
    part = lax.dot_general(last, dwv[...], (((1,), (1,)), ((), ())), preferred_element_type=F32)
    tv = tokens // nv
    for p in range(nv):
        fp[p] = part[p * tv : (p + 1) * tv]
    x_f.start()
    rf[v] = fp[v]
    acts = act[...].reshape(tokens, act.shape[2])
    down = lax.dot_general(acts, last, (((0,), (0,)), ((), ())), preferred_element_type=F32)
    gdownv[...] = down[:ff].astype(BF16)
    store_down = pltpu.make_async_copy(gdownv, gdown_ref, s_out.at[1])
    store_down.start()

    x_d3.recv()
    g1 = rd1b[0].astype(F32)
    for p in range(1, nz):
        g1 = g1 + rd1b[p].astype(F32)
    x_d4.recv()
    g2 = rd2b[0].astype(F32)
    for p in range(1, ny):
        g2 = g2 + rd2b[p].astype(F32)
    grad_own = jnp.concatenate([g1[:8], g1[8:], g2[:8], g2[8:]], axis=1)
    own_at = pl.ds(pl.multiple_of(y * rv + c * rh + z * 8, 8), 8)
    scale_own = rowv[own_at, 0:1]
    inner_own = rowv[own_at, 1:2]
    ghs[...] = scale_own * (grad_own * gain_ref[...]) - hown[...] * (
        scale_own * scale_own * inner_own / width
    )
    for e in range(EXITS):
        gh_ref[e] = ghs[2 * e : 2 * e + 2, :].astype(BF16)
    x_g2.recv()
    gain_all = gg2[0]
    for p in range(1, ng):
        gain_all = gain_all + gg2[p]
    for k in range(8):
        ggain_ref[:, k * wk : (k + 1) * wk] = gain_all[k : k + 1, :]

    x_f.recv()
    acc = rf[0]
    for p in range(1, nv):
        acc = acc + rf[p]
    for zz in range(nz):
        for cc in range(2):
            to = zz * 4 + cc * 2
            at = cc * 2 * nz + zz * 2
            gactv[to : to + 2, :] = acc[at : at + 2]
    gact_ref[...] = gactv[...].astype(BF16)

    each(nz, z, finish(own_z))
    each(ny, y, finish(own_y))
    lax.fori_loop(0, nz, lambda zz, _: (each(ny, y, finish(on_y(zz))), 0)[1], 0)
    lax.fori_loop(0, ny, lambda yy, _: (each(nz, z, finish(on_z(yy))), 0)[1], 0)
    lax.fori_loop(0, ny, lambda yy, _: (across(yy).wait_send(), 0)[1], 0)
    lax.fori_loop(0, ny, lambda p, _: (pass_on(p).wait_send(), 0)[1], 0)
    each(nv, v, lambda p, _: to_tokens(p).wait_send())
    x_s1.sent()
    x_s2.sent()
    x_c.sent()
    core_d.wait_send()
    x_d1.sent()
    x_d2.sent()
    x_d3.sent()
    x_d4.sent()
    x_q1.sent()
    x_q2.sent()
    x_g1.sent()
    x_e.sent()
    x_g2.sent()
    x_f.sent()
    store_head.wait()
    store_down.wait()


def hand_on_kernel(n, *refs):
    ins, outs, held, sems = refs[:n], refs[n : 2 * n], refs[2 * n : 3 * n], refs[3 * n]
    load = [pltpu.make_async_copy(ins[i], held[i], sems.at[0, i]) for i in range(n)]
    store = [pltpu.make_async_copy(held[i], outs[i], sems.at[1, i]) for i in range(n)]
    for copy in load:
        copy.start()
    for i in range(n):
        load[i].wait()
        store[i].start()
    for copy in store:
        copy.wait()


def hand_on(arrays):
    n = len(arrays)
    hbm = pl.BlockSpec(memory_space=pl.ANY)
    return pl.pallas_call(
        functools.partial(hand_on_kernel, n),
        out_shape=tuple(jax.ShapeDtypeStruct(a.shape, a.dtype) for a in arrays),
        in_specs=[hbm] * n,
        out_specs=(hbm,) * n,
        scratch_shapes=[pltpu.VMEM(a.shape, a.dtype) for a in arrays] + [pltpu.SemaphoreType.DMA((2, n))],
        compiler_params=pltpu.CompilerParams(vmem_limit_bytes=56 * 1024 * 1024),
    )(*arrays)


def body(ny, nz, hidden, norm_gain, head, targets, scale_index, layer_act, down_weight):
    nv = lax.axis_size("vocab")
    exits, own_tokens, w = hidden.shape
    vc = head.shape[1]
    tok_v, ff = layer_act.shape
    fpad = -(-ff // 128) * 128
    ng = 2 * nz
    rv = OWN * ng
    rh = rv // 2
    rows = rv * ny
    half, q, wk = w // 2, w // 4, w // 8
    tok_y = own_tokens * ng
    vm = pltpu.VMEM
    sem = lambda *n: pltpu.SemaphoreType.DMA(n)
    dma = lambda n: sem(2, n)
    scratch = [
        vm((OWN, w), F32), vm((2, ny, nz, 2, 16, q), BF16),
        vm((nv, tok_v, fpad), BF16), vm((vc, w), BF16), vm((VP, w), BF16), vm((ff, w), BF16),
        vm((vc, w), BF16), vm((ff, w), BF16), vm((rows, w), BF16), vm((rows, w), BF16),
        vm((nv, rv, VP), F32), vm((nv, rv, VP), F32),
        vm((ng, 8, 128), F32), vm((ny, 8, 128), F32), vm((rows, VP), BF16), vm((rows, 128), F32),
        vm((ny, rh, w), F32), vm((ny, rh, w), F32), vm((ny, rh, w), F32),
        vm((ny, rh, half), BF16), vm((nz, ny * 8, half), BF16),
        vm((ny, rh, half), BF16), vm((nz, ny * 8, half), BF16),
        vm((nz, 16, q), BF16), vm((ny, 16, q), BF16), vm((nz, 16, q), BF16), vm((ny, 16, q), BF16),
        vm((OWN, w), F32), vm((ny, 4 * nz, half), BF16), vm((ny, 4 * nz, half), BF16), vm((nz, 4 * nz, half), F32),
        vm((ny, 8, wk), F32), vm((ng, 8, wk), F32),
        vm((2, ny, 4 * nz, half), BF16), vm((ny, tok_y, w), BF16),
        vm((nv, tok_v, ff), F32), vm((nv, tok_v, ff), F32), vm((tok_v, ff), F32),
        dma(nv), sem(2), sem(2), sem(2, ny, nz), sem(nz), sem(nz, ny), sem(ny), sem(ny, nz), dma(ny),
        dma(nv), dma(ng), dma(ny), dma(nv),
        sem(2), dma(ny), dma(nz), dma(nz), dma(ny),
        dma(ny), dma(nz), dma(ny), dma(ny), dma(ng), dma(ny), dma(nv),
    ]
    spec = pl.BlockSpec(memory_space=vm)
    hbm = pl.BlockSpec(memory_space=pl.ANY)
    sds = jax.ShapeDtypeStruct
    results = pl.pallas_call(
        functools.partial(kernel, ny, nz, nv, vc),
        out_shape=(
            sds((1, 1), F32), sds(hidden.shape, BF16), sds((vc, w), BF16), sds((1, w), F32),
            sds(layer_act.shape, BF16), sds(down_weight.shape, BF16),
        ),
        in_specs=[spec, spec, hbm, spec, spec, spec, hbm],
        out_specs=(spec, spec, hbm, spec, spec, hbm),
        scratch_shapes=scratch,
        compiler_params=pltpu.CompilerParams(
            collective_id=0, has_side_effects=True, vmem_limit_bytes=56 * 1024 * 1024
        ),
    )(
        hidden, norm_gain.reshape(1, w), head.T, targets.reshape(1, -1), scale_index, layer_act, down_weight
    )
    loss, grad_hidden, grad_head, grad_gain, grad_act, grad_down = hand_on(results)
    return loss[0, 0], grad_hidden, grad_head.T, grad_gain.reshape(w), grad_act, grad_down


def solution(mesh, ny=8, nz=4):
    return jax.shard_map(
        functools.partial(body, ny, nz),
        mesh=mesh,
        in_specs=(
            P(None, "fsdp", "vocab"),
            P("vocab"),
            P("vocab", "fsdp"),
            P("vocab"),
            P(None, "vocab"),
            P("vocab", "fsdp"),
            P("fsdp", "vocab"),
        ),
        out_specs=(
            P(),
            P(None, "fsdp", "vocab"),
            P("vocab", "fsdp"),
            P("vocab"),
            P("vocab", "fsdp"),
            P("fsdp", "vocab"),
        ),
        check_vma=False,
    )
```

```python
import functools

import jax
import jax.numpy as jnp
from jax import lax
from jax.experimental import pallas as pl
from jax.experimental.pallas import tpu as pltpu
from jax.sharding import PartitionSpec as P

MESH = pl.DeviceIdType.MESH
EPS = 1e-05
F32 = jnp.float32
BF16 = jnp.bfloat16
EXITS = 4
OWN = 8
FULL = 32700.0
VP = 512


class Exchange:
    def __init__(self, n, me, dev, src, slot, sems):
        self.n, self.me, self.dev, self.src, self.slot, self.sems = n, me, dev, src, slot, sems

    def copy(self, p, j, src, dst, recv):
        return pltpu.make_async_remote_copy(
            src_ref=src, dst_ref=dst, send_sem=self.sems.at[0, j], recv_sem=self.sems.at[1, recv],
            device_id=self.dev(p), device_id_type=MESH,
        )

    def each(self, do):
        def one(j, _):
            do(lax.rem(self.me + j, self.n), j)
            return 0

        lax.fori_loop(1, self.n, one, 0)

    def start(self):
        self.each(lambda p, j: self.copy(p, j, self.src(p), self.slot(self.me), self.me).start())
        return self

    def recv(self, then=None):
        def one(p, j):
            self.copy(p, j, self.slot(p), self.slot(p), p).wait_recv()
            if then is not None:
                then(p)

        self.each(one)

    def sent(self):
        self.each(lambda p, j: self.copy(p, j, self.src(p), self.slot(self.me), self.me).wait_send())


def split3(x):
    hi = x.astype(BF16).astype(F32)
    rest = x - hi
    mid = rest.astype(BF16).astype(F32)
    return hi, mid, rest - mid


def to_fixed(x, extra, lanes, vc):
    top = jnp.maximum(jnp.max(jnp.abs(x), axis=1, keepdims=True), 1e-30)
    power = jnp.ceil(jnp.log2(top))
    out = jnp.floor(x * (jnp.exp2(-power) * FULL) + 0.5)
    first = jnp.floor(extra * 0.5)
    rest = (extra * 0.5 - first) * 32768.0
    second = jnp.floor(rest)
    third = jnp.floor((rest - second) * 32768.0)
    for i, value in enumerate((power, first, second, third)):
        out = jnp.where(lanes == vc + i, value, out)
    return out.astype(jnp.int32).astype(jnp.int16)


def from_fixed(q, vc):
    x = q.astype(jnp.int32).astype(F32)
    at = lambda i: x[:, vc + i : vc + i + 1]
    extra = 2.0 * (at(1) + (at(2) + at(3) * 2.0**-15) * 2.0**-15)
    return x * (jnp.exp2(at(0)) * (1.0 / FULL)), extra


def stack(x):
    q = x.shape[1] // 2
    return jnp.concatenate([x[:, :q], x[:, q:]], axis=0)


def kernel(
    ny, nz, nv, vc,
    hid_ref, gain_ref, head_ref, tgt_ref, si_ref, act_ref, dw_ref,
    loss_ref, gh_ref, ghead_ref, ggain_ref, gact_ref, gdown_ref,
    hown, ga, act, headv, headp, dwv, gheadv, gdownv, hr, hg, lg, rb, st1, st2, df, rowv,
    po, pm, rc, d1, d2, rd1, rd2, d1b, d2b, rd1b, rd2b, ghs, q1, rq1, rq2, gg1, gg2, ls, lr, fp, rf, gactv,
    s_act, s_in, s_out, r_a, s_a0z, s_a0y, s_a1y, s_a1z, s_ac, s_b, s_s1, s_s2, s_c, s_dc, s_d1, s_d2, s_d3, s_d4,
    s_q1, s_q2, s_e, s_g1, s_g2, s_ec, s_f,
):
    width_part = hid_ref.shape[2]
    width = width_part * nv
    half, q = width_part // 2, width_part // 4
    ng = 2 * nz
    rv = OWN * ng
    rh = rv // 2
    rows = rv * ny
    tb = rv // EXITS
    ff = dw_ref.shape[0]

    f = lax.axis_index("fsdp")
    v = lax.axis_index("vocab")
    y = f // ng
    g = f % ng
    z = g // 2
    c = g % 2
    o = 1 - c
    dev_y = lambda p: (p * ng + g, v)
    dev_g = lambda p: (y * ng + p, v)
    dev_z = lambda p: (y * ng + p * 2 + c, v)
    dev_v = lambda p: (f, p)
    dev_c = (y * ng + z * 2 + o, v)

    def to_core(src, dst, ss, rs):
        return pltpu.make_async_remote_copy(
            src_ref=src, dst_ref=dst, send_sem=ss, recv_sem=rs, device_id=dev_c, device_id_type=MESH
        )

    barrier = pltpu.get_barrier_semaphore()

    def greet(n, me, dev):
        def one(j, _):
            pl.semaphore_signal(barrier, inc=1, device_id=dev(lax.rem(me + j, n)), device_id_type=MESH)
            return 0

        lax.fori_loop(1, n, one, 0)

    load_head = pltpu.make_async_copy(head_ref, headv, s_in.at[0])
    load_down = pltpu.make_async_copy(dw_ref, dwv, s_in.at[1])
    greet(ny, y, dev_y)
    greet(ng, g, dev_g)
    greet(nv, v, dev_v)
    load_head.start()
    load_down.start()

    for e in range(EXITS):
        hown[2 * e : 2 * e + 2, :] = hid_ref[e].astype(F32)
    ga[c, y, z, 0] = stack(hown[:, :half]).astype(BF16)
    ga[c, y, z, 1] = stack(hown[:, half:]).astype(BF16)
    act[v, :, :ff] = act_ref[...]
    act[v, :, ff:] = jnp.zeros((act.shape[1], act.shape[2] - ff), BF16)

    pl.semaphore_wait(barrier, ny + ng + nv - 3)

    at_v = lambda p: df.at[pl.ds(pl.multiple_of(p * rv, rv), rv)]
    in_y = functools.partial(Exchange, ny, y, dev_y)
    in_z = functools.partial(Exchange, nz, z, dev_z)
    in_g = functools.partial(Exchange, ng, g, dev_g)
    in_v = functools.partial(Exchange, nv, v, dev_v)
    x_act = in_v(lambda p: act.at[v], lambda p: act.at[p], s_act)
    x_b = in_v(lambda p: lg.at[p], lambda p: rb.at[p], s_b)
    x_s1 = in_g(lambda p: st1.at[g], lambda p: st1.at[p], s_s1)
    x_s2 = in_y(lambda p: st2.at[y], lambda p: st2.at[p], s_s2)
    x_c = in_v(lambda p: at_v(v), at_v, s_c)
    x_d1 = in_y(lambda p: d1.at[p], lambda p: rd1.at[p], s_d1)
    x_d2 = in_z(lambda p: d2.at[p], lambda p: rd2.at[p], s_d2)
    x_d3 = in_z(lambda p: d1b.at[p], lambda p: rd1b.at[p], s_d3)
    x_d4 = in_y(lambda p: d2b.at[p], lambda p: rd2b.at[p], s_d4)
    x_q1 = in_y(lambda p: q1.at[p], lambda p: rq1.at[p], s_q1)
    x_q2 = in_z(lambda p: rq2.at[z], lambda p: rq2.at[p], s_q2)
    x_e = in_y(lambda p: ls.at[c, y], lambda p: ls.at[c, p], s_e)
    x_g1 = in_y(lambda p: gg1.at[y], lambda p: gg1.at[p], s_g1)
    x_g2 = in_g(lambda p: gg2.at[g], lambda p: gg2.at[p], s_g2)
    x_f = in_v(lambda p: fp.at[p], lambda p: rf.at[p], s_f)

    def block(dev, p, h, yy, zz, send):
        ref = ga.at[c, yy, zz, h]
        return pltpu.make_async_remote_copy(
            src_ref=ref, dst_ref=ref, send_sem=send, recv_sem=r_a.at[h, yy, zz],
            device_id=dev(p), device_id_type=MESH,
        )

    def each(n, me, do):
        def one(j, _):
            do(lax.rem(me + j, n), j)
            return 0

        lax.fori_loop(1, n, one, 0)

    own_z = lambda p, j: block(dev_z, p, 0, y, z, s_a0z.at[j])
    own_y = lambda p, j: block(dev_y, p, 1, y, z, s_a1y.at[j])
    on_y = lambda zz: lambda p, j: block(dev_y, p, 0, y, zz, s_a0y.at[zz, j])
    on_z = lambda yy: lambda p, j: block(dev_z, p, 1, yy, z, s_a1z.at[yy, j])
    begin = lambda make: lambda p, j: make(p, j).start()
    finish = lambda make: lambda p, j: make(p, j).wait_send()

    def arrived(h, yy, zz):
        block(dev_y, y, h, yy, zz, s_a0z.at[0]).wait_recv()

    each(nz, z, begin(own_z))
    each(ny, y, begin(own_y))
    each(ny, y, begin(on_y(z)))
    each(nz, z, begin(on_z(y)))
    x_act.start()

    load_head.wait()
    cut = vc // 16 * 16
    headp[:cut, :] = headv[:cut, :]
    tail = headv[cut:vc, :].astype(F32)
    headp[cut:, :] = jnp.concatenate([tail, jnp.zeros((VP - vc, width_part), F32)], axis=0).astype(BF16)

    for d in range(1, max(ny, nz) // 2 + 1):
        for shift in (d, -d):
            if d <= ny // 2 and (shift > 0 or 2 * d < ny):
                yy = lax.rem(y + shift + ny, ny)
                arrived(1, yy, z)
                each(nz, z, begin(on_z(yy)))
            if d <= nz // 2 and (shift > 0 or 2 * d < nz):
                zz = lax.rem(z + shift + nz, nz)
                arrived(0, y, zz)
                each(ny, y, begin(on_y(zz)))

    def across(yy):
        ref = ga.at[c, yy]
        return to_core(ref, ref, s_ac.at[0, yy], s_ac.at[1, yy])

    def nearest(j):
        return lax.rem(y + ny + jnp.where(j % 2 == 1, (j + 1) // 2, -(j // 2)), ny)

    def line_of(j, _):
        yy = nearest(j)

        @pl.when(j > 0)
        def _():
            lax.fori_loop(0, nz, lambda zz, _: (arrived(0, yy, zz), 0)[1], 0)

        each(nz, z, lambda p, _: arrived(1, yy, p))
        across(yy).start()
        return 0

    lanes = lax.broadcasted_iota(jnp.int32, (rv, VP), 1)

    def to_tokens(k):
        return pltpu.make_async_remote_copy(
            src_ref=lg.at[k], dst_ref=rb.at[v], send_sem=s_b.at[0, k], recv_sem=s_b.at[1, v],
            device_id=dev_v(k), device_id_type=MESH,
        )

    def rows_in(j):
        k = nearest(j)
        to_core(ga.at[o, k], ga.at[o, k], s_ac.at[0, k], s_ac.at[1, k]).wait_recv()
        at = pl.ds(pl.multiple_of(k * rv, rv), rv)
        sums = []
        for cc in range(2):
            for zz in range(0, nz, 2):
                to_at = pl.ds(pl.multiple_of(k * rv + cc * rh + zz * OWN, 16), 16)
                squares = None
                for h in range(2):
                    a = ga[cc, k, zz, h].astype(F32)
                    b = ga[cc, k, zz + 1, h].astype(F32)
                    for s in range(2):
                        x = jnp.concatenate([a[s * 8 : s * 8 + 8], b[s * 8 : s * 8 + 8]], axis=0)
                        to = slice((2 * h + s) * q, (2 * h + s + 1) * q)
                        hr[to_at, to] = x.astype(BF16)
                        hg[to_at, to] = (x * gain_ref[:, to]).astype(BF16)
                        squares = x * x if squares is None else squares + x * x
                sums.append(jnp.sum(squares, axis=1, keepdims=True))
        part = lax.dot_general(
            hg[at, :], headp[...], (((1,), (1,)), ((), ())), preferred_element_type=F32
        )
        lg[k] = to_fixed(part, jnp.concatenate(sums, axis=0), lanes, vc)

        @pl.when(k != v)
        def _():
            to_tokens(k).start()

        @pl.when(k == v)
        def _():
            rb[v] = lg[v]

    line_of(0, 0)

    def step(j, _):
        line_of(j, 0)
        rows_in(j - 1)
        return 0

    lax.fori_loop(1, ny, step, 0)
    rows_in(ny - 1)

    r_id = lax.broadcasted_iota(jnp.int32, (rv, 1), 0)
    exit_id = (r_id & 7) >> 1
    tok_id = (((r_id & (rh - 1)) >> 3) << 2) + ((r_id // rh) << 1) + (r_id & 1)
    l16 = lax.broadcasted_iota(jnp.int32, (rv, tb), 1)
    here = l16 == tok_id
    tgt = jnp.sum(jnp.where(here, tgt_ref[...].astype(F32), 0.0), axis=1, keepdims=True)
    index = jnp.zeros((rv, 1), F32)
    for e in range(EXITS):
        index += jnp.sum(
            jnp.where(here & (exit_id == e), si_ref[e : e + 1, :].astype(F32), 0.0), axis=1, keepdims=True
        )
    weight = jnp.exp2(4.0 - index)
    column = (lanes + f * vc).astype(F32)
    valid = lanes < vc
    onehot = (column == tgt) & valid
    x_b.recv()
    logits, squares = from_fixed(rb[0], vc)
    for p in range(1, nv):
        more = from_fixed(rb[p], vc)
        logits, squares = logits + more[0], squares + more[1]
    scale = lax.rsqrt(squares / width + EPS)
    logits = logits * scale
    peak = jnp.max(jnp.where(valid, logits, -3e38), axis=1, keepdims=True)
    grown = jnp.where(valid, jnp.exp(jnp.minimum(logits - peak, 0.0)), 0.0)
    total = jnp.sum(grown, axis=1, keepdims=True)
    moment = jnp.sum(grown * jnp.where(valid, logits, 0.0), axis=1, keepdims=True)
    picked = jnp.sum(jnp.where(onehot, logits, 0.0), axis=1, keepdims=True)

    eye = lax.broadcasted_iota(jnp.int32, (rv, 128), 0) == lax.broadcasted_iota(jnp.int32, (rv, 128), 1)
    to_row = lambda x: jnp.sum(jnp.where(eye, x, 0.0), axis=0, keepdims=True)
    to_col = lambda x: jnp.sum(jnp.where(eye, x, 0.0), axis=1, keepdims=True)

    def put(ref, at, values):
        for i, value in enumerate(values):
            ref[at, i : i + 1, :] = value
        ref[at, len(values) :, :] = jnp.zeros((8 - len(values), 128), F32)

    def merge(ref, n):
        top = ref[0, 0:1, :]
        for p in range(1, n):
            top = jnp.maximum(top, ref[p, 0:1, :])
        tot = mom = pick = jnp.zeros((1, 128), F32)
        for p in range(n):
            by = jnp.exp(ref[p, 0:1, :] - top)
            tot = tot + by * ref[p, 1:2, :]
            mom = mom + by * ref[p, 2:3, :]
            pick = pick + ref[p, 3:4, :]
        return top, tot, mom, pick

    put(st1, g, [to_row(peak), to_row(total), to_row(moment), to_row(picked)])
    x_s1.start()
    x_s1.recv()
    put(st2, y, merge(st1, ng))
    x_s2.start()
    x_s2.recv()
    top, tot, mom, pick = merge(st2, ny)
    lse = to_col(top + jnp.log(tot))
    picked = to_col(pick)
    inner = weight * (to_col(mom / tot) - picked)
    dlog = weight * (jnp.exp(jnp.minimum(logits - lse, 0.0)) - onehot.astype(F32))
    out = jnp.where(valid, dlog, 0.0)
    for i, value in enumerate(split3(scale) + split3(inner) + split3(weight * (lse - picked))):
        out = jnp.where(lanes == vc + i, value, out)
    mine = pl.ds(pl.multiple_of(v * rv, rv), rv)
    df[mine, :] = out.astype(BF16)

    x_c.start()
    x_c.recv()

    def rows_of(core):
        lhs = jnp.concatenate(
            [df[pl.ds(pl.multiple_of(k * rv + core * rh, rh), rh), :] for k in range(ny)], axis=0
        )
        return lax.dot_general(lhs, headp[...], (((1,), (0,)), ((), ())), preferred_element_type=F32)

    po[...] = rows_of(o).reshape(ny, rh, width_part)
    core_d = to_core(po, rc, s_dc.at[0], s_dc.at[1])
    core_d.start()
    pm[...] = rows_of(c).reshape(ny, rh, width_part)
    extra = df[:, vc - vc % 128 :].astype(F32)
    i0 = vc % 128
    pull = lambda i: extra[:, i0 + i : i0 + i + 1] + extra[:, i0 + i + 1 : i0 + i + 2] + extra[:, i0 + i + 2 : i0 + i + 3]
    scale_all = pull(0)
    rowv[:, 0:1] = scale_all
    rowv[:, 1:2] = pull(3)
    loss_ref[...] = jnp.sum(pull(6), axis=0, keepdims=True) / rows
    core_d.wait_recv()

    wk = width_part // 8

    def pack0(k, _):
        both = pm[k] + rc[k]
        pm[k] = both
        last = [both[zz * 8 + 6 : zz * 8 + 8] for zz in range(nz)]
        q1[k] = stack(jnp.concatenate(last, axis=0)).astype(BF16)
        return 0

    lax.fori_loop(0, ny, pack0, 0)
    x_q1.start()
    rq1[y] = q1[y]

    def pack1(k, _):
        d1[k] = pm[k, :, :half].astype(BF16)
        return 0

    lax.fori_loop(0, ny, pack1, 0)
    x_d1.start()
    rd1[y] = d1[y]

    def pack2(k, _):
        for zz in range(nz):
            pair = jnp.concatenate(
                [pm[2 * k, zz * 8 : zz * 8 + 8, half:], pm[2 * k + 1, zz * 8 : zz * 8 + 8, half:]], axis=0
            )
            d2[zz, pl.ds(pl.multiple_of(k * 16, 16), 16), :] = pair.astype(BF16)
        return 0

    lax.fori_loop(0, ny // 2, pack2, 0)
    x_d2.start()
    rd2[z] = d2[z]

    x_q1.recv()
    line = rq1[0].astype(F32)
    for p in range(1, ny):
        line = line + rq1[p].astype(F32)
    rq2[z] = line
    x_q2.start()

    def norm(k, total):
        at = pl.ds(pl.multiple_of(k * rv, rv), rv)
        hg[at, :] = (hr[at, :].astype(F32) * rowv[at, 0:1] * gain_ref[...]).astype(BF16)
        mine = pl.ds(pl.multiple_of(k * rv + c * rh, rh), rh)
        return total + jnp.sum(pm[k] * hr[mine, :].astype(F32) * rowv[mine, 0:1], axis=0, keepdims=True)

    gain_part = lax.fori_loop(0, ny, norm, jnp.zeros((1, width_part), F32))
    for k in range(8):
        gg1[y, k : k + 1, :] = gain_part[:, k * wk : (k + 1) * wk]
    x_g1.start()

    mine = pl.ds(pl.multiple_of(y * rv + c * rh, rh), rh)
    of_last = lambda x: jnp.concatenate([x[zz * 8 + 6 : zz * 8 + 8] for zz in range(nz)], axis=0)
    h_last = of_last(hr[mine, :].astype(F32))
    scale_last = of_last(rowv[mine, 0:1])
    inner_last = of_last(rowv[mine, 1:2])
    x_q2.recv()
    line = rq2[0]
    for p in range(1, nz):
        line = line + rq2[p]
    grad_last = jnp.concatenate([line[: 2 * nz], line[2 * nz :]], axis=1)
    rows_last = scale_last * (grad_last * gain_ref[...]) - h_last * (
        scale_last * scale_last * inner_last / width
    )
    ls[c, y] = stack(rows_last).astype(BF16)

    def pass_on(p):
        ref = ls.at[c, p]
        return to_core(ref, ref, s_ec.at[0, p], s_ec.at[1, p])

    x_e.start()
    pass_on(y).start()

    wt = min(width_part, 256)
    for m in range(0, width_part, wt):
        part = lax.dot_general(
            df[...], hg[:, m : m + wt], (((0,), (0,)), ((), ())), preferred_element_type=F32
        )
        gheadv[:, m : m + wt] = part[:vc].astype(BF16)
    store_head = pltpu.make_async_copy(gheadv, ghead_ref, s_out.at[0])
    store_head.start()
    x_act.recv()

    def acts_in(p, _):
        tile = act[p].astype(F32)
        parts = [tile[zz * 4 + cc * 2 : zz * 4 + cc * 2 + 2] for cc in range(2) for zz in range(nz)]
        act[p] = jnp.concatenate(parts, axis=0).astype(BF16)
        return 0

    x_act.sent()
    lax.fori_loop(0, nv, acts_in, 0)

    x_d1.recv()
    sum1 = rd1[0].astype(F32)
    for p in range(1, ny):
        sum1 = sum1 + rd1[p].astype(F32)
    for zz in range(nz):
        d1b[zz] = stack(sum1[zz * 8 : zz * 8 + 8]).astype(BF16)
    x_d3.start()
    rd1b[z] = d1b[z]
    x_d2.recv()
    sum2 = rd2[0].astype(F32)
    for p in range(1, nz):
        sum2 = sum2 + rd2[p].astype(F32)
    for k in range(ny):
        d2b[k] = stack(sum2[k * 8 : k * 8 + 8]).astype(BF16)
    x_d4.start()
    rd2b[y] = d2b[y]
    x_g1.recv()
    gain_y = gg1[0]
    for p in range(1, ny):
        gain_y = gain_y + gg1[p]
    gg2[g] = gain_y
    x_g2.start()

    x_e.recv(lambda p: pass_on(p).start())

    def rows_out(j, _):
        p = nearest(j)
        ref = ls.at[o, p]
        to_core(ref, ref, s_ec.at[0, p], s_ec.at[1, p]).wait_recv()
        a, b = ls[0, p].astype(F32), ls[1, p].astype(F32)
        lr[p, :, :half] = jnp.concatenate([a[: 2 * nz], b[: 2 * nz]], axis=0).astype(BF16)
        lr[p, :, half:] = jnp.concatenate([a[2 * nz :], b[2 * nz :]], axis=0).astype(BF16)
        return 0

    lax.fori_loop(0, ny, rows_out, 0)
    tokens = ny * lr.shape[1]
    last = lr[...].reshape(tokens, width_part)
    load_down.wait()
    part = lax.dot_general(last, dwv[...], (((1,), (1,)), ((), ())), preferred_element_type=F32)
    tv = tokens // nv
    for p in range(nv):
        fp[p] = part[p * tv : (p + 1) * tv]
    x_f.start()
    rf[v] = fp[v]
    acts = act[...].reshape(tokens, act.shape[2])
    down = lax.dot_general(acts, last, (((0,), (0,)), ((), ())), preferred_element_type=F32)
    gdownv[...] = down[:ff].astype(BF16)
    store_down = pltpu.make_async_copy(gdownv, gdown_ref, s_out.at[1])
    store_down.start()

    x_d3.recv()
    g1 = rd1b[0].astype(F32)
    for p in range(1, nz):
        g1 = g1 + rd1b[p].astype(F32)
    x_d4.recv()
    g2 = rd2b[0].astype(F32)
    for p in range(1, ny):
        g2 = g2 + rd2b[p].astype(F32)
    grad_own = jnp.concatenate([g1[:8], g1[8:], g2[:8], g2[8:]], axis=1)
    own_at = pl.ds(pl.multiple_of(y * rv + c * rh + z * 8, 8), 8)
    scale_own = rowv[own_at, 0:1]
    inner_own = rowv[own_at, 1:2]
    ghs[...] = scale_own * (grad_own * gain_ref[...]) - hown[...] * (
        scale_own * scale_own * inner_own / width
    )
    for e in range(EXITS):
        gh_ref[e] = ghs[2 * e : 2 * e + 2, :].astype(BF16)
    x_g2.recv()
    gain_all = gg2[0]
    for p in range(1, ng):
        gain_all = gain_all + gg2[p]
    for k in range(8):
        ggain_ref[:, k * wk : (k + 1) * wk] = gain_all[k : k + 1, :]

    x_f.recv()
    acc = rf[0]
    for p in range(1, nv):
        acc = acc + rf[p]
    for zz in range(nz):
        for cc in range(2):
            to = zz * 4 + cc * 2
            at = cc * 2 * nz + zz * 2
            gactv[to : to + 2, :] = acc[at : at + 2]
    gact_ref[...] = gactv[...].astype(BF16)

    each(nz, z, finish(own_z))
    each(ny, y, finish(own_y))
    lax.fori_loop(0, nz, lambda zz, _: (each(ny, y, finish(on_y(zz))), 0)[1], 0)
    lax.fori_loop(0, ny, lambda yy, _: (each(nz, z, finish(on_z(yy))), 0)[1], 0)
    lax.fori_loop(0, ny, lambda yy, _: (across(yy).wait_send(), 0)[1], 0)
    lax.fori_loop(0, ny, lambda p, _: (pass_on(p).wait_send(), 0)[1], 0)
    each(nv, v, lambda p, _: to_tokens(p).wait_send())
    x_s1.sent()
    x_s2.sent()
    x_c.sent()
    core_d.wait_send()
    x_d1.sent()
    x_d2.sent()
    x_d3.sent()
    x_d4.sent()
    x_q1.sent()
    x_q2.sent()
    x_g1.sent()
    x_e.sent()
    x_g2.sent()
    x_f.sent()
    store_head.wait()
    store_down.wait()


def hand_on_kernel(n, *refs):
    ins, outs, held, sems = refs[:n], refs[n : 2 * n], refs[2 * n : 3 * n], refs[3 * n]
    load = [pltpu.make_async_copy(ins[i], held[i], sems.at[0, i]) for i in range(n)]
    store = [pltpu.make_async_copy(held[i], outs[i], sems.at[1, i]) for i in range(n)]
    for copy in load:
        copy.start()
    for i in range(n):
        load[i].wait()
        store[i].start()
    for copy in store:
        copy.wait()


def hand_on(arrays):
    n = len(arrays)
    hbm = pl.BlockSpec(memory_space=pl.ANY)
    return pl.pallas_call(
        functools.partial(hand_on_kernel, n),
        out_shape=tuple(jax.ShapeDtypeStruct(a.shape, a.dtype) for a in arrays),
        in_specs=[hbm] * n,
        out_specs=(hbm,) * n,
        scratch_shapes=[pltpu.VMEM(a.shape, a.dtype) for a in arrays] + [pltpu.SemaphoreType.DMA((2, n))],
        compiler_params=pltpu.CompilerParams(vmem_limit_bytes=56 * 1024 * 1024),
    )(*arrays)


def body(ny, nz, hidden, norm_gain, head, targets, scale_index, layer_act, down_weight):
    nv = lax.axis_size("vocab")
    exits, own_tokens, w = hidden.shape
    vc = head.shape[1]
    tok_v, ff = layer_act.shape
    fpad = -(-ff // 128) * 128
    ng = 2 * nz
    rv = OWN * ng
    rh = rv // 2
    rows = rv * ny
    half, q, wk = w // 2, w // 4, w // 8
    tok_y = own_tokens * ng
    vm = pltpu.VMEM
    sem = lambda *n: pltpu.SemaphoreType.DMA(n)
    dma = lambda n: sem(2, n)
    scratch = [
        vm((OWN, w), F32), vm((2, ny, nz, 2, 16, q), BF16),
        vm((nv, tok_v, fpad), BF16), vm((vc, w), BF16), vm((VP, w), BF16), vm((ff, w), BF16),
        vm((vc, w), BF16), vm((ff, w), BF16), vm((rows, w), BF16), vm((rows, w), BF16),
        vm((nv, rv, VP), jnp.int16), vm((nv, rv, VP), jnp.int16),
        vm((ng, 8, 128), F32), vm((ny, 8, 128), F32), vm((rows, VP), BF16), vm((rows, 128), F32),
        vm((ny, rh, w), F32), vm((ny, rh, w), F32), vm((ny, rh, w), F32),
        vm((ny, rh, half), BF16), vm((nz, ny * 8, half), BF16),
        vm((ny, rh, half), BF16), vm((nz, ny * 8, half), BF16),
        vm((nz, 16, q), BF16), vm((ny, 16, q), BF16), vm((nz, 16, q), BF16), vm((ny, 16, q), BF16),
        vm((OWN, w), F32), vm((ny, 4 * nz, half), BF16), vm((ny, 4 * nz, half), BF16), vm((nz, 4 * nz, half), F32),
        vm((ny, 8, wk), F32), vm((ng, 8, wk), F32),
        vm((2, ny, 4 * nz, half), BF16), vm((ny, tok_y, w), BF16),
        vm((nv, tok_v, ff), F32), vm((nv, tok_v, ff), F32), vm((tok_v, ff), F32),
        dma(nv), sem(2), sem(2), sem(2, ny, nz), sem(nz), sem(nz, ny), sem(ny), sem(ny, nz), dma(ny),
        dma(nv), dma(ng), dma(ny), dma(nv),
        sem(2), dma(ny), dma(nz), dma(nz), dma(ny),
        dma(ny), dma(nz), dma(ny), dma(ny), dma(ng), dma(ny), dma(nv),
    ]
    spec = pl.BlockSpec(memory_space=vm)
    hbm = pl.BlockSpec(memory_space=pl.ANY)
    sds = jax.ShapeDtypeStruct
    results = pl.pallas_call(
        functools.partial(kernel, ny, nz, nv, vc),
        out_shape=(
            sds((1, 1), F32), sds(hidden.shape, BF16), sds((vc, w), BF16), sds((1, w), F32),
            sds(layer_act.shape, BF16), sds(down_weight.shape, BF16),
        ),
        in_specs=[spec, spec, hbm, spec, spec, spec, hbm],
        out_specs=(spec, spec, hbm, spec, spec, hbm),
        scratch_shapes=scratch,
        compiler_params=pltpu.CompilerParams(
            collective_id=0, has_side_effects=True, vmem_limit_bytes=56 * 1024 * 1024
        ),
    )(
        hidden, norm_gain.reshape(1, w), head.T, targets.reshape(1, -1), scale_index, layer_act, down_weight
    )
    loss, grad_hidden, grad_head, grad_gain, grad_act, grad_down = hand_on(results)
    return loss[0, 0], grad_hidden, grad_head.T, grad_gain.reshape(w), grad_act, grad_down


def solution(mesh, ny=8, nz=4):
    return jax.shard_map(
        functools.partial(body, ny, nz),
        mesh=mesh,
        in_specs=(
            P(None, "fsdp", "vocab"),
            P("vocab"),
            P("vocab", "fsdp"),
            P("vocab"),
            P(None, "vocab"),
            P("vocab", "fsdp"),
            P("fsdp", "vocab"),
        ),
        out_specs=(
            P(),
            P(None, "fsdp", "vocab"),
            P("vocab", "fsdp"),
            P("vocab"),
            P("vocab", "fsdp"),
            P("fsdp", "vocab"),
        ),
        check_vma=False,
    )
```

```python
import functools

import jax
import jax.numpy as jnp
from jax import lax
from jax.experimental import pallas as pl
from jax.experimental.pallas import tpu as pltpu
from jax.sharding import PartitionSpec as P

MESH = pl.DeviceIdType.MESH
EPS = 1e-05
F32 = jnp.float32
BF16 = jnp.bfloat16
EXITS = 4
OWN = 8
FULL = 32700.0
VP = 512


class Exchange:
    def __init__(self, n, me, dev, src, slot, sems):
        self.n, self.me, self.dev, self.src, self.slot, self.sems = n, me, dev, src, slot, sems

    def copy(self, p, j, src, dst, recv):
        return pltpu.make_async_remote_copy(
            src_ref=src, dst_ref=dst, send_sem=self.sems.at[0, j], recv_sem=self.sems.at[1, recv],
            device_id=self.dev(p), device_id_type=MESH,
        )

    def each(self, do):
        def one(j, _):
            do(lax.rem(self.me + j, self.n), j)
            return 0

        lax.fori_loop(1, self.n, one, 0)

    def start(self):
        self.each(lambda p, j: self.copy(p, j, self.src(p), self.slot(self.me), self.me).start())
        return self

    def recv(self, then=None):
        def one(p, j):
            self.copy(p, j, self.slot(p), self.slot(p), p).wait_recv()
            if then is not None:
                then(p)

        self.each(one)

    def sent(self):
        self.each(lambda p, j: self.copy(p, j, self.src(p), self.slot(self.me), self.me).wait_send())


def split3(x):
    hi = x.astype(BF16).astype(F32)
    rest = x - hi
    mid = rest.astype(BF16).astype(F32)
    return hi, mid, rest - mid


def to_fixed(x, extra, lanes, vc):
    top = jnp.maximum(jnp.max(jnp.abs(x), axis=1, keepdims=True), 1e-30)
    power = jnp.ceil(jnp.log2(top))
    out = jnp.floor(x * (jnp.exp2(-power) * FULL) + 0.5)
    first = jnp.floor(extra * 0.5)
    rest = (extra * 0.5 - first) * 32768.0
    second = jnp.floor(rest)
    third = jnp.floor((rest - second) * 32768.0)
    for i, value in enumerate((power, first, second, third)):
        out = jnp.where(lanes == vc + i, value, out)
    return out.astype(jnp.int32).astype(jnp.int16)


def from_fixed(q, vc):
    x = q.astype(jnp.int32).astype(F32)
    at = lambda i: x[:, vc + i : vc + i + 1]
    extra = 2.0 * (at(1) + (at(2) + at(3) * 2.0**-15) * 2.0**-15)
    return x * (jnp.exp2(at(0)) * (1.0 / FULL)), extra


def stack(x):
    q = x.shape[1] // 2
    return jnp.concatenate([x[:, :q], x[:, q:]], axis=0)


def kernel(
    ny, nz, nv, vc,
    hid_ref, gain_ref, head_ref, tgt_ref, si_ref, act_ref, dw_ref,
    loss_ref, gh_ref, ghead_ref, ggain_ref, gact_ref, gdown_ref,
    hown, ga, act, headv, headp, dwv, gheadv, gdownv, hr, hg, lg, rb, st1, st2, st3, ef, df, rowv,
    po, pm, rc, d1, d2, rd1, rd2, d1b, d2b, rd1b, rd2b, ghs, q1, rq1, rq2, gg1, gg2, ls, lr, fp, rf, gactv,
    s_act, s_in, s_out, r_a, s_a0z, s_a0y, s_a1y, s_a1z, s_ac, s_b, s_s1, s_s2, s_s3, s_c, s_dc, s_d1, s_d2, s_d3, s_d4,
    s_q1, s_q2, s_e, s_g1, s_g2, s_ec, s_f,
):
    width_part = hid_ref.shape[2]
    width = width_part * nv
    half, q = width_part // 2, width_part // 4
    ng = 2 * nz
    rv = OWN * ng
    rh = rv // 2
    rows = rv * ny
    tb = rv // EXITS
    ff = dw_ref.shape[0]

    f = lax.axis_index("fsdp")
    v = lax.axis_index("vocab")
    y = f // ng
    g = f % ng
    z = g // 2
    c = g % 2
    o = 1 - c
    dev_y = lambda p: (p * ng + g, v)
    dev_g = lambda p: (y * ng + p, v)
    dev_z = lambda p: (y * ng + p * 2 + c, v)
    dev_v = lambda p: (f, p)
    dev_c = (y * ng + z * 2 + o, v)

    def to_core(src, dst, ss, rs):
        return pltpu.make_async_remote_copy(
            src_ref=src, dst_ref=dst, send_sem=ss, recv_sem=rs, device_id=dev_c, device_id_type=MESH
        )

    barrier = pltpu.get_barrier_semaphore()

    def greet(n, me, dev):
        def one(j, _):
            pl.semaphore_signal(barrier, inc=1, device_id=dev(lax.rem(me + j, n)), device_id_type=MESH)
            return 0

        lax.fori_loop(1, n, one, 0)

    load_head = pltpu.make_async_copy(head_ref, headv, s_in.at[0])
    load_down = pltpu.make_async_copy(dw_ref, dwv.at[pl.ds(0, ff)], s_in.at[1])
    greet(ny, y, dev_y)
    greet(ng, g, dev_g)
    greet(nv, v, dev_v)
    load_head.start()
    load_down.start()

    for e in range(EXITS):
        hown[2 * e : 2 * e + 2, :] = hid_ref[e].astype(F32)
    ga[c, y, z, 0] = stack(hown[:, :half]).astype(BF16)
    ga[c, y, z, 1] = stack(hown[:, half:]).astype(BF16)
    act[v, :, :ff] = act_ref[...]
    dwv[ff:, :] = jnp.zeros((dwv.shape[0] - ff, width_part), BF16)
    act[v, :, ff:] = jnp.zeros((act.shape[1], act.shape[2] - ff), BF16)

    pl.semaphore_wait(barrier, ny + ng + nv - 3)

    at_v = lambda p: ef.at[pl.ds(pl.multiple_of(p * rv, rv), rv)]
    in_y = functools.partial(Exchange, ny, y, dev_y)
    in_z = functools.partial(Exchange, nz, z, dev_z)
    in_g = functools.partial(Exchange, ng, g, dev_g)
    in_v = functools.partial(Exchange, nv, v, dev_v)
    x_act = in_v(lambda p: act.at[v], lambda p: act.at[p], s_act)
    x_b = in_v(lambda p: lg.at[p], lambda p: rb.at[p], s_b)
    x_s1 = in_g(lambda p: st1.at[g], lambda p: st1.at[p], s_s1)
    x_s2 = in_y(lambda p: st2.at[y], lambda p: st2.at[p], s_s2)
    x_s3 = in_v(lambda p: st3.at[v], lambda p: st3.at[p], s_s3)
    x_c = in_v(lambda p: at_v(v), at_v, s_c)
    x_d1 = in_y(lambda p: d1.at[p], lambda p: rd1.at[p], s_d1)
    x_d2 = in_z(lambda p: d2.at[p], lambda p: rd2.at[p], s_d2)
    x_d3 = in_z(lambda p: d1b.at[p], lambda p: rd1b.at[p], s_d3)
    x_d4 = in_y(lambda p: d2b.at[p], lambda p: rd2b.at[p], s_d4)
    x_q1 = in_y(lambda p: q1.at[p], lambda p: rq1.at[p], s_q1)
    x_q2 = in_z(lambda p: rq2.at[z], lambda p: rq2.at[p], s_q2)
    x_e = in_y(lambda p: ls.at[c, y], lambda p: ls.at[c, p], s_e)
    x_g1 = in_y(lambda p: gg1.at[y], lambda p: gg1.at[p], s_g1)
    x_g2 = in_g(lambda p: gg2.at[g], lambda p: gg2.at[p], s_g2)
    x_f = in_v(lambda p: fp.at[p], lambda p: rf.at[p], s_f)

    def block(dev, p, h, yy, zz, send):
        ref = ga.at[c, yy, zz, h]
        return pltpu.make_async_remote_copy(
            src_ref=ref, dst_ref=ref, send_sem=send, recv_sem=r_a.at[h, yy, zz],
            device_id=dev(p), device_id_type=MESH,
        )

    def each(n, me, do):
        def one(j, _):
            do(lax.rem(me + j, n), j)
            return 0

        lax.fori_loop(1, n, one, 0)

    own_z = lambda p, j: block(dev_z, p, 0, y, z, s_a0z.at[j])
    own_y = lambda p, j: block(dev_y, p, 1, y, z, s_a1y.at[j])
    on_y = lambda zz: lambda p, j: block(dev_y, p, 0, y, zz, s_a0y.at[zz, j])
    on_z = lambda yy: lambda p, j: block(dev_z, p, 1, yy, z, s_a1z.at[yy, j])
    begin = lambda make: lambda p, j: make(p, j).start()
    finish = lambda make: lambda p, j: make(p, j).wait_send()

    def arrived(h, yy, zz):
        block(dev_y, y, h, yy, zz, s_a0z.at[0]).wait_recv()

    each(nz, z, begin(own_z))
    each(ny, y, begin(own_y))
    each(ny, y, begin(on_y(z)))
    each(nz, z, begin(on_z(y)))
    x_act.start()

    load_head.wait()
    cut = vc // 16 * 16
    headp[:cut, :] = headv[:cut, :]
    tail = headv[cut:vc, :].astype(F32)
    headp[cut:, :] = jnp.concatenate([tail, jnp.zeros((VP - vc, width_part), F32)], axis=0).astype(BF16)

    for d in range(1, max(ny, nz) // 2 + 1):
        for shift in (d, -d):
            if d <= ny // 2 and (shift > 0 or 2 * d < ny):
                yy = lax.rem(y + shift + ny, ny)
                arrived(1, yy, z)
                each(nz, z, begin(on_z(yy)))
            if d <= nz // 2 and (shift > 0 or 2 * d < nz):
                zz = lax.rem(z + shift + nz, nz)
                arrived(0, y, zz)
                each(ny, y, begin(on_y(zz)))

    def across(yy):
        ref = ga.at[c, yy]
        return to_core(ref, ref, s_ac.at[0, yy], s_ac.at[1, yy])

    def nearest(j):
        return lax.rem(y + ny + jnp.where(j % 2 == 1, (j + 1) // 2, -(j // 2)), ny)

    def line_of(j, _):
        yy = nearest(j)

        @pl.when(j > 0)
        def _():
            lax.fori_loop(0, nz, lambda zz, _: (arrived(0, yy, zz), 0)[1], 0)

        each(nz, z, lambda p, _: arrived(1, yy, p))
        across(yy).start()
        return 0

    lanes = lax.broadcasted_iota(jnp.int32, (rv, VP), 1)

    def to_tokens(k):
        return pltpu.make_async_remote_copy(
            src_ref=lg.at[k], dst_ref=rb.at[v], send_sem=s_b.at[0, k], recv_sem=s_b.at[1, v],
            device_id=dev_v(k), device_id_type=MESH,
        )

    def rows_in(j):
        k = nearest(j)
        to_core(ga.at[o, k], ga.at[o, k], s_ac.at[0, k], s_ac.at[1, k]).wait_recv()
        at = pl.ds(pl.multiple_of(k * rv, rv), rv)
        sums = []
        for cc in range(2):
            for zz in range(0, nz, 2):
                to_at = pl.ds(pl.multiple_of(k * rv + cc * rh + zz * OWN, 16), 16)
                squares = None
                for h in range(2):
                    a = ga[cc, k, zz, h].astype(F32)
                    b = ga[cc, k, zz + 1, h].astype(F32)
                    for s in range(2):
                        x = jnp.concatenate([a[s * 8 : s * 8 + 8], b[s * 8 : s * 8 + 8]], axis=0)
                        to = slice((2 * h + s) * q, (2 * h + s + 1) * q)
                        hr[to_at, to] = x.astype(BF16)
                        hg[to_at, to] = (x * gain_ref[:, to]).astype(BF16)
                        squares = x * x if squares is None else squares + x * x
                sums.append(jnp.sum(squares, axis=1, keepdims=True))
        part = lax.dot_general(
            hg[at, :], headp[...], (((1,), (1,)), ((), ())), preferred_element_type=F32
        )
        lg[k] = to_fixed(part, jnp.concatenate(sums, axis=0), lanes, vc)

        @pl.when(k != v)
        def _():
            to_tokens(k).start()

        @pl.when(k == v)
        def _():
            rb[v] = lg[v]

    line_of(0, 0)

    def step(j, _):
        line_of(j, 0)
        rows_in(j - 1)
        return 0

    lax.fori_loop(1, ny, step, 0)
    rows_in(ny - 1)

    r_id = lax.broadcasted_iota(jnp.int32, (rv, 1), 0)
    exit_id = (r_id & 7) >> 1
    tok_id = (((r_id & (rh - 1)) >> 3) << 2) + ((r_id // rh) << 1) + (r_id & 1)
    l16 = lax.broadcasted_iota(jnp.int32, (rv, tb), 1)
    here = l16 == tok_id
    tgt = jnp.sum(jnp.where(here, tgt_ref[...].astype(F32), 0.0), axis=1, keepdims=True)
    index = jnp.zeros((rv, 1), F32)
    for e in range(EXITS):
        index += jnp.sum(
            jnp.where(here & (exit_id == e), si_ref[e : e + 1, :].astype(F32), 0.0), axis=1, keepdims=True
        )
    weight = jnp.exp2(4.0 - index)
    column = (lanes + f * vc).astype(F32)
    valid = lanes < vc
    onehot = (column == tgt) & valid
    x_b.recv()
    logits, squares = from_fixed(rb[0], vc)
    for p in range(1, nv):
        more = from_fixed(rb[p], vc)
        logits, squares = logits + more[0], squares + more[1]
    scale = lax.rsqrt(squares / width + EPS)
    logits = logits * scale
    peak = jnp.max(jnp.where(valid, logits, -3e38), axis=1, keepdims=True)
    grown = jnp.where(valid, jnp.exp(jnp.minimum(logits - peak, 0.0)), 0.0)
    total = jnp.sum(grown, axis=1, keepdims=True)
    moment = jnp.sum(grown * jnp.where(valid, logits, 0.0), axis=1, keepdims=True)
    picked = jnp.sum(jnp.where(onehot, logits, 0.0), axis=1, keepdims=True)

    eye = lax.broadcasted_iota(jnp.int32, (rv, 128), 0) == lax.broadcasted_iota(jnp.int32, (rv, 128), 1)
    to_row = lambda x: jnp.sum(jnp.where(eye, x, 0.0), axis=0, keepdims=True)
    to_col = lambda x: jnp.sum(jnp.where(eye, x, 0.0), axis=1, keepdims=True)

    def put(ref, at, values):
        for i, value in enumerate(values):
            ref[at, i : i + 1, :] = value
        ref[at, len(values) :, :] = jnp.zeros((8 - len(values), 128), F32)

    def merge(ref, n):
        top = ref[0, 0:1, :]
        for p in range(1, n):
            top = jnp.maximum(top, ref[p, 0:1, :])
        tot = mom = pick = jnp.zeros((1, 128), F32)
        for p in range(n):
            by = jnp.exp(ref[p, 0:1, :] - top)
            tot = tot + by * ref[p, 1:2, :]
            mom = mom + by * ref[p, 2:3, :]
            pick = pick + ref[p, 3:4, :]
        return top, tot, mom, pick

    put(st1, g, [to_row(peak), to_row(total), to_row(moment), to_row(picked)])
    x_s1.start()
    out = jnp.where(onehot, 0.0, grown)
    for i, value in enumerate(split3(peak)):
        out = jnp.where(lanes == vc + i, value, out)
    ef[pl.ds(pl.multiple_of(v * rv, rv), rv), :] = out.astype(BF16)
    x_c.start()
    weight_row, scale_row, tgt_row = to_row(weight), to_row(scale), to_row(tgt)
    x_s1.recv()
    put(st2, y, merge(st1, ng))
    x_s2.start()
    x_s2.recv()
    top, tot, mom, pick = merge(st2, ny)
    lse = top + jnp.log(tot)
    inner = weight_row * (mom / tot - pick)
    missed = weight_row * (jnp.exp(jnp.minimum(pick - lse, 0.0)) - 1.0)
    put(st3, v, [scale_row, inner, lse, missed, weight_row * (lse - pick), weight_row, tgt_row])
    x_s3.start()
    x_s3.recv()
    x_c.recv()

    def logit_grads(k, loss):
        at = pl.ds(pl.multiple_of(k * rv, rv), rv)
        scale_k, inner_k, lse_k, missed_k, _, weight_k, tgt_k = (to_col(st3[k, i : i + 1, :]) for i in range(7))
        grown_k = ef[at, :].astype(F32)
        peak_k = grown_k[:, vc : vc + 1] + grown_k[:, vc + 1 : vc + 2] + grown_k[:, vc + 2 : vc + 3]
        prob = (weight_k * jnp.exp(jnp.minimum(peak_k - lse_k, 0.0))) * grown_k
        df[at, :] = jnp.where(valid, jnp.where(column == tgt_k, missed_k, prob), 0.0).astype(BF16)
        rowv[at, 0:1] = scale_k
        rowv[at, 1:2] = inner_k
        return loss + st3[k, 4:5, :]

    loss = lax.fori_loop(0, nv, logit_grads, jnp.zeros((1, 128), F32))
    in_use = lax.broadcasted_iota(jnp.int32, (1, 128), 1) < rv
    loss_ref[...] = jnp.sum(jnp.where(in_use, loss, 0.0), axis=1, keepdims=True) / rows

    hy = ny // 2

    def rows_of(core, i):
        lhs = jnp.concatenate(
            [
                df[pl.ds(pl.multiple_of(k * rv + core * rh, rh), rh), :]
                for k in range(i * hy, (i + 1) * hy)
            ],
            axis=0,
        )
        out = lax.dot_general(lhs, headp[...], (((1,), (0,)), ((), ())), preferred_element_type=F32)
        return out.reshape(hy, rh, width_part)

    def to_other(i):
        at = pl.ds(i * hy, hy)
        return to_core(po.at[at], rc.at[at], s_dc.at[0, i], s_dc.at[1, i])

    for i in range(2):
        po[i * hy : (i + 1) * hy] = rows_of(o, i)
        to_other(i).start()
    for i in range(2):
        pm[i * hy : (i + 1) * hy] = rows_of(c, i)
    for i in range(2):
        to_other(i).wait_recv()

    wk = width_part // 8

    def pack0(k, _):
        both = pm[k] + rc[k]
        pm[k] = both
        last = [both[zz * 8 + 6 : zz * 8 + 8] for zz in range(nz)]
        q1[k] = stack(jnp.concatenate(last, axis=0)).astype(BF16)
        return 0

    lax.fori_loop(0, ny, pack0, 0)
    x_q1.start()
    rq1[y] = q1[y]

    def pack1(k, _):
        d1[k] = pm[k, :, :half].astype(BF16)
        return 0

    lax.fori_loop(0, ny, pack1, 0)
    x_d1.start()
    rd1[y] = d1[y]

    def pack2(k, _):
        for zz in range(nz):
            pair = jnp.concatenate(
                [pm[2 * k, zz * 8 : zz * 8 + 8, half:], pm[2 * k + 1, zz * 8 : zz * 8 + 8, half:]], axis=0
            )
            d2[zz, pl.ds(pl.multiple_of(k * 16, 16), 16), :] = pair.astype(BF16)
        return 0

    lax.fori_loop(0, ny // 2, pack2, 0)
    x_d2.start()
    rd2[z] = d2[z]

    x_q1.recv()
    line = rq1[0].astype(F32)
    for p in range(1, ny):
        line = line + rq1[p].astype(F32)
    rq2[z] = line
    x_q2.start()

    def norm(k, total):
        at = pl.ds(pl.multiple_of(k * rv, rv), rv)
        hg[at, :] = (hr[at, :].astype(F32) * rowv[at, 0:1] * gain_ref[...]).astype(BF16)
        mine = pl.ds(pl.multiple_of(k * rv + c * rh, rh), rh)
        return total + jnp.sum(pm[k] * hr[mine, :].astype(F32) * rowv[mine, 0:1], axis=0, keepdims=True)

    gain_part = lax.fori_loop(0, ny, norm, jnp.zeros((1, width_part), F32))
    for k in range(8):
        gg1[y, k : k + 1, :] = gain_part[:, k * wk : (k + 1) * wk]
    x_g1.start()

    mine = pl.ds(pl.multiple_of(y * rv + c * rh, rh), rh)
    of_last = lambda x: jnp.concatenate([x[zz * 8 + 6 : zz * 8 + 8] for zz in range(nz)], axis=0)
    h_last = of_last(hr[mine, :].astype(F32))
    scale_last = of_last(rowv[mine, 0:1])
    inner_last = of_last(rowv[mine, 1:2])
    x_q2.recv()
    line = rq2[0]
    for p in range(1, nz):
        line = line + rq2[p]
    grad_last = jnp.concatenate([line[: 2 * nz], line[2 * nz :]], axis=1)
    rows_last = scale_last * (grad_last * gain_ref[...]) - h_last * (
        scale_last * scale_last * inner_last / width
    )
    ls[c, y] = stack(rows_last).astype(BF16)

    def pass_on(p):
        ref = ls.at[c, p]
        return to_core(ref, ref, s_ec.at[0, p], s_ec.at[1, p])

    x_e.start()
    pass_on(y).start()

    wt = min(width_part, 256)
    for m in range(0, width_part, wt):
        part = lax.dot_general(
            df[...], hg[:, m : m + wt], (((0,), (0,)), ((), ())), preferred_element_type=F32
        )
        gheadv[:, m : m + wt] = part[:vc].astype(BF16)
    store_head = pltpu.make_async_copy(gheadv, ghead_ref, s_out.at[0])
    store_head.start()
    x_act.recv()

    def acts_in(p, _):
        tile = act[p].astype(F32)
        parts = [tile[zz * 4 + cc * 2 : zz * 4 + cc * 2 + 2] for cc in range(2) for zz in range(nz)]
        act[p] = jnp.concatenate(parts, axis=0).astype(BF16)
        return 0

    x_act.sent()
    lax.fori_loop(0, nv, acts_in, 0)

    x_d1.recv()
    sum1 = rd1[0].astype(F32)
    for p in range(1, ny):
        sum1 = sum1 + rd1[p].astype(F32)
    for zz in range(nz):
        d1b[zz] = stack(sum1[zz * 8 : zz * 8 + 8]).astype(BF16)
    x_d3.start()
    rd1b[z] = d1b[z]
    x_d2.recv()
    sum2 = rd2[0].astype(F32)
    for p in range(1, nz):
        sum2 = sum2 + rd2[p].astype(F32)
    for k in range(ny):
        d2b[k] = stack(sum2[k * 8 : k * 8 + 8]).astype(BF16)
    x_d4.start()
    rd2b[y] = d2b[y]
    x_g1.recv()
    gain_y = gg1[0]
    for p in range(1, ny):
        gain_y = gain_y + gg1[p]
    gg2[g] = gain_y
    x_g2.start()

    x_e.recv(lambda p: pass_on(p).start())

    def rows_out(j, _):
        p = nearest(j)
        ref = ls.at[o, p]
        to_core(ref, ref, s_ec.at[0, p], s_ec.at[1, p]).wait_recv()
        a, b = ls[0, p].astype(F32), ls[1, p].astype(F32)
        lr[p, :, :half] = jnp.concatenate([a[: 2 * nz], b[: 2 * nz]], axis=0).astype(BF16)
        lr[p, :, half:] = jnp.concatenate([a[2 * nz :], b[2 * nz :]], axis=0).astype(BF16)
        return 0

    lax.fori_loop(0, ny, rows_out, 0)
    tokens = ny * lr.shape[1]
    last = lr[...].reshape(tokens, width_part)
    load_down.wait()
    part = lax.dot_general(last, dwv[...], (((1,), (1,)), ((), ())), preferred_element_type=F32)
    tv = tokens // nv
    lanes_f = lax.broadcasted_iota(jnp.int32, (tv, fp.shape[2]), 1)
    for p in range(nv):
        fp[p] = to_fixed(part[p * tv : (p + 1) * tv], jnp.zeros((tv, 1), F32), lanes_f, ff)
    x_f.start()
    rf[v] = fp[v]
    acts = act[...].reshape(tokens, act.shape[2])
    down = lax.dot_general(acts, last, (((0,), (0,)), ((), ())), preferred_element_type=F32)
    gdownv[...] = down[:ff].astype(BF16)
    store_down = pltpu.make_async_copy(gdownv, gdown_ref, s_out.at[1])
    store_down.start()

    x_d3.recv()
    g1 = rd1b[0].astype(F32)
    for p in range(1, nz):
        g1 = g1 + rd1b[p].astype(F32)
    x_d4.recv()
    g2 = rd2b[0].astype(F32)
    for p in range(1, ny):
        g2 = g2 + rd2b[p].astype(F32)
    grad_own = jnp.concatenate([g1[:8], g1[8:], g2[:8], g2[8:]], axis=1)
    own_at = pl.ds(pl.multiple_of(y * rv + c * rh + z * 8, 8), 8)
    scale_own = rowv[own_at, 0:1]
    inner_own = rowv[own_at, 1:2]
    ghs[...] = scale_own * (grad_own * gain_ref[...]) - hown[...] * (
        scale_own * scale_own * inner_own / width
    )
    for e in range(EXITS):
        gh_ref[e] = ghs[2 * e : 2 * e + 2, :].astype(BF16)
    x_g2.recv()
    gain_all = gg2[0]
    for p in range(1, ng):
        gain_all = gain_all + gg2[p]
    for k in range(8):
        ggain_ref[:, k * wk : (k + 1) * wk] = gain_all[k : k + 1, :]

    x_f.recv()
    acc = from_fixed(rf[0], ff)[0]
    for p in range(1, nv):
        acc = acc + from_fixed(rf[p], ff)[0]
    for zz in range(nz):
        for cc in range(2):
            to = zz * 4 + cc * 2
            at = cc * 2 * nz + zz * 2
            gactv[to : to + 2, :] = acc[at : at + 2, :ff]
    gact_ref[...] = gactv[...].astype(BF16)

    each(nz, z, finish(own_z))
    each(ny, y, finish(own_y))
    lax.fori_loop(0, nz, lambda zz, _: (each(ny, y, finish(on_y(zz))), 0)[1], 0)
    lax.fori_loop(0, ny, lambda yy, _: (each(nz, z, finish(on_z(yy))), 0)[1], 0)
    lax.fori_loop(0, ny, lambda yy, _: (across(yy).wait_send(), 0)[1], 0)
    lax.fori_loop(0, ny, lambda p, _: (pass_on(p).wait_send(), 0)[1], 0)
    each(nv, v, lambda p, _: to_tokens(p).wait_send())
    x_s1.sent()
    x_s2.sent()
    x_s3.sent()
    x_c.sent()
    for i in range(2):
        to_other(i).wait_send()
    x_d1.sent()
    x_d2.sent()
    x_d3.sent()
    x_d4.sent()
    x_q1.sent()
    x_q2.sent()
    x_g1.sent()
    x_e.sent()
    x_g2.sent()
    x_f.sent()
    store_head.wait()
    store_down.wait()


def hand_on_kernel(n, *refs):
    ins, outs, held, sems = refs[:n], refs[n : 2 * n], refs[2 * n : 3 * n], refs[3 * n]
    load = [pltpu.make_async_copy(ins[i], held[i], sems.at[0, i]) for i in range(n)]
    store = [pltpu.make_async_copy(held[i], outs[i], sems.at[1, i]) for i in range(n)]
    for copy in load:
        copy.start()
    for i in range(n):
        load[i].wait()
        store[i].start()
    for copy in store:
        copy.wait()


def hand_on(arrays):
    n = len(arrays)
    hbm = pl.BlockSpec(memory_space=pl.ANY)
    return pl.pallas_call(
        functools.partial(hand_on_kernel, n),
        out_shape=tuple(jax.ShapeDtypeStruct(a.shape, a.dtype) for a in arrays),
        in_specs=[hbm] * n,
        out_specs=(hbm,) * n,
        scratch_shapes=[pltpu.VMEM(a.shape, a.dtype) for a in arrays] + [pltpu.SemaphoreType.DMA((2, n))],
        compiler_params=pltpu.CompilerParams(vmem_limit_bytes=56 * 1024 * 1024),
    )(*arrays)


def body(ny, nz, hidden, norm_gain, head, targets, scale_index, layer_act, down_weight):
    nv = lax.axis_size("vocab")
    exits, own_tokens, w = hidden.shape
    vc = head.shape[1]
    tok_v, ff = layer_act.shape
    fpad = -(-ff // 128) * 128
    ng = 2 * nz
    rv = OWN * ng
    rh = rv // 2
    rows = rv * ny
    half, q, wk = w // 2, w // 4, w // 8
    tok_y = own_tokens * ng
    vm = pltpu.VMEM
    sem = lambda *n: pltpu.SemaphoreType.DMA(n)
    dma = lambda n: sem(2, n)
    scratch = [
        vm((OWN, w), F32), vm((2, ny, nz, 2, 16, q), BF16),
        vm((nv, tok_v, fpad), BF16), vm((vc, w), BF16), vm((VP, w), BF16), vm((fpad, w), BF16),
        vm((vc, w), BF16), vm((ff, w), BF16), vm((rows, w), BF16), vm((rows, w), BF16),
        vm((nv, rv, VP), jnp.int16), vm((nv, rv, VP), jnp.int16),
        vm((ng, 8, 128), F32), vm((ny, 8, 128), F32), vm((nv, 8, 128), F32),
        vm((rows, VP), BF16), vm((rows, VP), BF16), vm((rows, 128), F32),
        vm((ny, rh, w), F32), vm((ny, rh, w), F32), vm((ny, rh, w), F32),
        vm((ny, rh, half), BF16), vm((nz, ny * 8, half), BF16),
        vm((ny, rh, half), BF16), vm((nz, ny * 8, half), BF16),
        vm((nz, 16, q), BF16), vm((ny, 16, q), BF16), vm((nz, 16, q), BF16), vm((ny, 16, q), BF16),
        vm((OWN, w), F32), vm((ny, 4 * nz, half), BF16), vm((ny, 4 * nz, half), BF16), vm((nz, 4 * nz, half), F32),
        vm((ny, 8, wk), F32), vm((ng, 8, wk), F32),
        vm((2, ny, 4 * nz, half), BF16), vm((ny, tok_y, w), BF16),
        vm((nv, tok_v, fpad), jnp.int16), vm((nv, tok_v, fpad), jnp.int16), vm((tok_v, ff), F32),
        dma(nv), sem(2), sem(2), sem(2, ny, nz), sem(nz), sem(nz, ny), sem(ny), sem(ny, nz), dma(ny),
        dma(nv), dma(ng), dma(ny), dma(nv), dma(nv),
        dma(2), dma(ny), dma(nz), dma(nz), dma(ny),
        dma(ny), dma(nz), dma(ny), dma(ny), dma(ng), dma(ny), dma(nv),
    ]
    spec = pl.BlockSpec(memory_space=vm)
    hbm = pl.BlockSpec(memory_space=pl.ANY)
    sds = jax.ShapeDtypeStruct
    results = pl.pallas_call(
        functools.partial(kernel, ny, nz, nv, vc),
        out_shape=(
            sds((1, 1), F32), sds(hidden.shape, BF16), sds((vc, w), BF16), sds((1, w), F32),
            sds(layer_act.shape, BF16), sds(down_weight.shape, BF16),
        ),
        in_specs=[spec, spec, hbm, spec, spec, spec, hbm],
        out_specs=(spec, spec, hbm, spec, spec, hbm),
        scratch_shapes=scratch,
        compiler_params=pltpu.CompilerParams(
            collective_id=0, has_side_effects=True, vmem_limit_bytes=56 * 1024 * 1024
        ),
    )(
        hidden, norm_gain.reshape(1, w), head.T, targets.reshape(1, -1), scale_index, layer_act, down_weight
    )
    loss, grad_hidden, grad_head, grad_gain, grad_act, grad_down = hand_on(results)
    return loss[0, 0], grad_hidden, grad_head.T, grad_gain.reshape(w), grad_act, grad_down


def solution(mesh, ny=8, nz=4):
    return jax.shard_map(
        functools.partial(body, ny, nz),
        mesh=mesh,
        in_specs=(
            P(None, "fsdp", "vocab"),
            P("vocab"),
            P("vocab", "fsdp"),
            P("vocab"),
            P(None, "vocab"),
            P("vocab", "fsdp"),
            P("fsdp", "vocab"),
        ),
        out_specs=(
            P(),
            P(None, "fsdp", "vocab"),
            P("vocab", "fsdp"),
            P("vocab"),
            P("vocab", "fsdp"),
            P("fsdp", "vocab"),
        ),
        check_vma=False,
    )
```

```python
import functools

import jax
import jax.numpy as jnp
from jax import lax
from jax.experimental import pallas as pl
from jax.experimental.pallas import tpu as pltpu
from jax.sharding import PartitionSpec as P

MESH = pl.DeviceIdType.MESH
EPS = 1e-05
F32 = jnp.float32
BF16 = jnp.bfloat16
EXITS = 4
OWN = 8
FULL = 32700.0
VP = 512


class Exchange:
    def __init__(self, n, me, dev, src, slot, sems):
        self.n, self.me, self.dev, self.src, self.slot, self.sems = n, me, dev, src, slot, sems

    def copy(self, p, j, src, dst, recv):
        return pltpu.make_async_remote_copy(
            src_ref=src, dst_ref=dst, send_sem=self.sems.at[0, j], recv_sem=self.sems.at[1, recv],
            device_id=self.dev(p), device_id_type=MESH,
        )

    def each(self, do):
        def one(j, _):
            do(lax.rem(self.me + j, self.n), j)
            return 0

        lax.fori_loop(1, self.n, one, 0)

    def start(self):
        self.each(lambda p, j: self.copy(p, j, self.src(p), self.slot(self.me), self.me).start())
        return self

    def recv(self, then=None):
        def one(p, j):
            self.copy(p, j, self.slot(p), self.slot(p), p).wait_recv()
            if then is not None:
                then(p)

        self.each(one)

    def sent(self):
        self.each(lambda p, j: self.copy(p, j, self.src(p), self.slot(self.me), self.me).wait_send())


def split3(x):
    hi = x.astype(BF16).astype(F32)
    rest = x - hi
    mid = rest.astype(BF16).astype(F32)
    return hi, mid, rest - mid


def to_fixed(x, extra, lanes, vc):
    top = jnp.maximum(jnp.max(jnp.abs(x), axis=1, keepdims=True), 1e-30)
    power = jnp.ceil(jnp.log2(top))
    out = jnp.floor(x * (jnp.exp2(-power) * FULL) + 0.5)
    first = jnp.floor(extra * 0.5)
    rest = (extra * 0.5 - first) * 32768.0
    second = jnp.floor(rest)
    third = jnp.floor((rest - second) * 32768.0)
    for i, value in enumerate((power, first, second, third)):
        out = jnp.where(lanes == vc + i, value, out)
    return out.astype(jnp.int32).astype(jnp.int16)


def from_fixed(q, vc):
    x = q.astype(jnp.int32).astype(F32)
    at = lambda i: x[:, vc + i : vc + i + 1]
    extra = 2.0 * (at(1) + (at(2) + at(3) * 2.0**-15) * 2.0**-15)
    return x * (jnp.exp2(at(0)) * (1.0 / FULL)), extra


def stack(x):
    q = x.shape[1] // 2
    return jnp.concatenate([x[:, :q], x[:, q:]], axis=0)


def kernel(
    ny, nz, nv, vc,
    hid_ref, gain_ref, head_ref, tgt_ref, si_ref, act_ref, dw_ref,
    loss_ref, gh_ref, ghead_ref, ggain_ref, gact_ref, gdown_ref,
    hown, ga1, ga2, act, headv, headp, dwv, gheadv, gdownv, hr, hg, lg, rb, st1, st2, st3, ef, df, rowv,
    po, pm, rc, d1, d2, rd1, rd2, d1b, d2b, rd1b, rd2b, ghs, q1, rq1, rq2, gg1, gg2, ls, lr, fp, rf, gactv,
    s_act, s_in, s_out, s_a1, s_a2, s_a3, s_a4, s_c1, s_c2, s_b, s_s1, s_s2, s_s3, s_c, s_dc, s_d1, s_d2, s_d3, s_d4,
    s_q1, s_q2, s_e, s_g1, s_g2, s_ec, s_f,
):
    width_part = hid_ref.shape[2]
    width = width_part * nv
    half, q = width_part // 2, width_part // 4
    ng = 2 * nz
    rv = OWN * ng
    rh = rv // 2
    rows = rv * ny
    tb = rv // EXITS
    ff = dw_ref.shape[0]

    f = lax.axis_index("fsdp")
    v = lax.axis_index("vocab")
    y = f // ng
    g = f % ng
    z = g // 2
    c = g % 2
    o = 1 - c
    dev_y = lambda p: (p * ng + g, v)
    dev_g = lambda p: (y * ng + p, v)
    dev_z = lambda p: (y * ng + p * 2 + c, v)
    dev_v = lambda p: (f, p)
    dev_c = (y * ng + z * 2 + o, v)

    def to_core(src, dst, ss, rs):
        return pltpu.make_async_remote_copy(
            src_ref=src, dst_ref=dst, send_sem=ss, recv_sem=rs, device_id=dev_c, device_id_type=MESH
        )

    barrier = pltpu.get_barrier_semaphore()

    def greet(n, me, dev):
        def one(j, _):
            pl.semaphore_signal(barrier, inc=1, device_id=dev(lax.rem(me + j, n)), device_id_type=MESH)
            return 0

        lax.fori_loop(1, n, one, 0)

    load_head = pltpu.make_async_copy(head_ref, headv, s_in.at[0])
    load_down = pltpu.make_async_copy(dw_ref, dwv.at[pl.ds(0, ff)], s_in.at[1])
    greet(ny, y, dev_y)
    greet(ng, g, dev_g)
    greet(nv, v, dev_v)
    load_head.start()
    load_down.start()

    for e in range(EXITS):
        hown[2 * e : 2 * e + 2, :] = hid_ref[e].astype(F32)
    ga1[c, y, z] = stack(hown[:, :half]).astype(BF16)
    ga2[c, z, y] = stack(hown[:, half:]).astype(BF16)
    act[v, :, :ff] = act_ref[...]
    dwv[ff:, :] = jnp.zeros((dwv.shape[0] - ff, width_part), BF16)
    act[v, :, ff:] = jnp.zeros((act.shape[1], act.shape[2] - ff), BF16)

    pl.semaphore_wait(barrier, ny + ng + nv - 3)

    at_v = lambda p: ef.at[pl.ds(pl.multiple_of(p * rv, rv), rv)]
    in_y = functools.partial(Exchange, ny, y, dev_y)
    in_z = functools.partial(Exchange, nz, z, dev_z)
    in_g = functools.partial(Exchange, ng, g, dev_g)
    in_v = functools.partial(Exchange, nv, v, dev_v)
    x_a1 = in_z(lambda p: ga1.at[c, y, z], lambda p: ga1.at[c, y, p], s_a1)
    x_a2 = in_y(lambda p: ga2.at[c, z, y], lambda p: ga2.at[c, z, p], s_a2)
    x_a3 = in_y(lambda p: ga1.at[c, y], lambda p: ga1.at[c, p], s_a3)
    x_a4 = in_z(lambda p: ga2.at[c, z], lambda p: ga2.at[c, p], s_a4)
    x_act = in_v(lambda p: act.at[v], lambda p: act.at[p], s_act)
    x_b = in_v(lambda p: lg.at[p], lambda p: rb.at[p], s_b)
    x_s1 = in_y(lambda p: st1.at[y], lambda p: st1.at[p], s_s1)
    x_s2 = in_g(lambda p: st2.at[g], lambda p: st2.at[p], s_s2)
    x_s3 = in_v(lambda p: st3.at[v], lambda p: st3.at[p], s_s3)
    x_c = in_v(lambda p: at_v(v), at_v, s_c)
    x_d1 = in_y(lambda p: d1.at[p], lambda p: rd1.at[p], s_d1)
    x_d2 = in_z(lambda p: d2.at[p], lambda p: rd2.at[p], s_d2)
    x_d3 = in_z(lambda p: d1b.at[p], lambda p: rd1b.at[p], s_d3)
    x_d4 = in_y(lambda p: d2b.at[p], lambda p: rd2b.at[p], s_d4)
    x_q1 = in_y(lambda p: q1.at[p], lambda p: rq1.at[p], s_q1)
    x_q2 = in_z(lambda p: rq2.at[z], lambda p: rq2.at[p], s_q2)
    x_e = in_y(lambda p: ls.at[c, y], lambda p: ls.at[c, p], s_e)
    x_g1 = in_y(lambda p: gg1.at[y], lambda p: gg1.at[p], s_g1)
    x_g2 = in_g(lambda p: gg2.at[g], lambda p: gg2.at[p], s_g2)
    x_f = in_v(lambda p: fp.at[p], lambda p: rf.at[p], s_f)

    def each(n, me, do):
        def one(j, _):
            do(lax.rem(me + j, n), j)
            return 0

        lax.fori_loop(1, n, one, 0)

    def across1(p, core):
        return to_core(ga1.at[core, p], ga1.at[core, p], s_c1.at[0, p], s_c1.at[1, p])

    def across2(p, core):
        return to_core(ga2.at[core, p], ga2.at[core, p], s_c2.at[0, p], s_c2.at[1, p])

    x_a1.start()
    x_a2.start()
    x_a1.recv()
    x_a3.start()
    x_a2.recv()
    x_a4.start()
    across1(y, c).start()
    across2(z, c).start()
    x_act.start()

    load_head.wait()
    cut = vc // 16 * 16
    headp[:cut, :] = headv[:cut, :]
    tail = headv[cut:vc, :].astype(F32)
    headp[cut:, :] = jnp.concatenate([tail, jnp.zeros((VP - vc, width_part), F32)], axis=0).astype(BF16)

    x_a4.recv(lambda p: across2(p, c).start())
    lax.fori_loop(0, nz, lambda p, _: (across2(p, o).wait_recv(), 0)[1], 0)

    def nearest(j):
        return lax.rem(y + ny + jnp.where(j % 2 == 1, (j + 1) // 2, -(j // 2)), ny)

    def line_of(j):
        p = nearest(j)
        x_a3.copy(p, 0, x_a3.slot(p), x_a3.slot(p), p).wait_recv()
        across1(p, c).start()

    lanes = lax.broadcasted_iota(jnp.int32, (rv, VP), 1)

    def to_tokens(k):
        return pltpu.make_async_remote_copy(
            src_ref=lg.at[k], dst_ref=rb.at[v], send_sem=s_b.at[0, k], recv_sem=s_b.at[1, v],
            device_id=dev_v(k), device_id_type=MESH,
        )

    def rows_in(j):
        k = nearest(j)
        across1(k, o).wait_recv()
        at = pl.ds(pl.multiple_of(k * rv, rv), rv)
        sums = []
        for cc in range(2):
            for zz in range(0, nz, 2):
                to_at = pl.ds(pl.multiple_of(k * rv + cc * rh + zz * OWN, 16), 16)
                squares = None
                for h in range(2):
                    a = (ga1[cc, k, zz] if h == 0 else ga2[cc, zz, k]).astype(F32)
                    b = (ga1[cc, k, zz + 1] if h == 0 else ga2[cc, zz + 1, k]).astype(F32)
                    for s in range(2):
                        x = jnp.concatenate([a[s * 8 : s * 8 + 8], b[s * 8 : s * 8 + 8]], axis=0)
                        to = slice((2 * h + s) * q, (2 * h + s + 1) * q)
                        hr[to_at, to] = x.astype(BF16)
                        hg[to_at, to] = (x * gain_ref[:, to]).astype(BF16)
                        squares = x * x if squares is None else squares + x * x
                sums.append(jnp.sum(squares, axis=1, keepdims=True))
        part = lax.dot_general(
            hg[at, :], headp[...], (((1,), (1,)), ((), ())), preferred_element_type=F32
        )
        lg[k] = to_fixed(part, jnp.concatenate(sums, axis=0), lanes, vc)

        @pl.when(k != v)
        def _():
            to_tokens(k).start()

        @pl.when(k == v)
        def _():
            rb[v] = lg[v]

    def step(j, _):
        line_of(j)
        rows_in(j - 1)
        return 0

    lax.fori_loop(1, ny, step, 0)
    rows_in(ny - 1)

    r_id = lax.broadcasted_iota(jnp.int32, (rv, 1), 0)
    exit_id = (r_id & 7) >> 1
    tok_id = (((r_id & (rh - 1)) >> 3) << 2) + ((r_id // rh) << 1) + (r_id & 1)
    l16 = lax.broadcasted_iota(jnp.int32, (rv, tb), 1)
    here = l16 == tok_id
    tgt = jnp.sum(jnp.where(here, tgt_ref[...].astype(F32), 0.0), axis=1, keepdims=True)
    index = jnp.zeros((rv, 1), F32)
    for e in range(EXITS):
        index += jnp.sum(
            jnp.where(here & (exit_id == e), si_ref[e : e + 1, :].astype(F32), 0.0), axis=1, keepdims=True
        )
    weight = jnp.exp2(4.0 - index)
    column = (lanes + f * vc).astype(F32)
    valid = lanes < vc
    onehot = (column == tgt) & valid
    x_b.recv()
    logits, squares = from_fixed(rb[0], vc)
    for p in range(1, nv):
        more = from_fixed(rb[p], vc)
        logits, squares = logits + more[0], squares + more[1]
    scale = lax.rsqrt(squares / width + EPS)
    logits = logits * scale
    peak = jnp.max(jnp.where(valid, logits, -3e38), axis=1, keepdims=True)
    grown = jnp.where(valid, jnp.exp(jnp.minimum(logits - peak, 0.0)), 0.0)
    total = jnp.sum(grown, axis=1, keepdims=True)
    moment = jnp.sum(grown * jnp.where(valid, logits, 0.0), axis=1, keepdims=True)
    picked = jnp.sum(jnp.where(onehot, logits, 0.0), axis=1, keepdims=True)

    eye = lax.broadcasted_iota(jnp.int32, (rv, 128), 0) == lax.broadcasted_iota(jnp.int32, (rv, 128), 1)
    to_row = lambda x: jnp.sum(jnp.where(eye, x, 0.0), axis=0, keepdims=True)
    to_col = lambda x: jnp.sum(jnp.where(eye, x, 0.0), axis=1, keepdims=True)

    def put(ref, at, values):
        for i, value in enumerate(values):
            ref[at, i : i + 1, :] = value
        ref[at, len(values) :, :] = jnp.zeros((8 - len(values), 128), F32)

    def merge(ref, n):
        top = ref[0, 0:1, :]
        for p in range(1, n):
            top = jnp.maximum(top, ref[p, 0:1, :])
        tot = mom = pick = jnp.zeros((1, 128), F32)
        for p in range(n):
            by = jnp.exp(ref[p, 0:1, :] - top)
            tot = tot + by * ref[p, 1:2, :]
            mom = mom + by * ref[p, 2:3, :]
            pick = pick + ref[p, 3:4, :]
        return top, tot, mom, pick

    put(st1, y, [to_row(peak), to_row(total), to_row(moment), to_row(picked)])
    x_s1.start()
    out = jnp.where(onehot, 0.0, grown)
    for i, value in enumerate(split3(peak)):
        out = jnp.where(lanes == vc + i, value, out)
    ef[pl.ds(pl.multiple_of(v * rv, rv), rv), :] = out.astype(BF16)
    x_c.start()
    weight_row, scale_row, tgt_row = to_row(weight), to_row(scale), to_row(tgt)
    x_s1.recv()
    put(st2, g, merge(st1, ny))
    x_s2.start()
    x_s2.recv()
    top, tot, mom, pick = merge(st2, ng)
    lse = top + jnp.log(tot)
    inner = weight_row * (mom / tot - pick)
    missed = weight_row * (jnp.exp(jnp.minimum(pick - lse, 0.0)) - 1.0)
    put(st3, v, [scale_row, inner, lse, missed, weight_row * (lse - pick), weight_row, tgt_row])
    x_s3.start()
    x_s3.recv()
    x_c.recv()

    def logit_grads(k, loss):
        at = pl.ds(pl.multiple_of(k * rv, rv), rv)
        scale_k, inner_k, lse_k, missed_k, _, weight_k, tgt_k = (to_col(st3[k, i : i + 1, :]) for i in range(7))
        grown_k = ef[at, :].astype(F32)
        peak_k = grown_k[:, vc : vc + 1] + grown_k[:, vc + 1 : vc + 2] + grown_k[:, vc + 2 : vc + 3]
        prob = (weight_k * jnp.exp(jnp.minimum(peak_k - lse_k, 0.0))) * grown_k
        df[at, :] = jnp.where(valid, jnp.where(column == tgt_k, missed_k, prob), 0.0).astype(BF16)
        rowv[at, 0:1] = scale_k
        rowv[at, 1:2] = inner_k
        return loss + st3[k, 4:5, :]

    loss = lax.fori_loop(0, nv, logit_grads, jnp.zeros((1, 128), F32))
    in_use = lax.broadcasted_iota(jnp.int32, (1, 128), 1) < rv
    loss_ref[...] = jnp.sum(jnp.where(in_use, loss, 0.0), axis=1, keepdims=True) / rows

    hy = ny // 2

    def rows_of(core, i):
        lhs = jnp.concatenate(
            [
                df[pl.ds(pl.multiple_of(k * rv + core * rh, rh), rh), :]
                for k in range(i * hy, (i + 1) * hy)
            ],
            axis=0,
        )
        out = lax.dot_general(lhs, headp[...], (((1,), (0,)), ((), ())), preferred_element_type=F32)
        return out.reshape(hy, rh, width_part)

    def to_other(i):
        at = pl.ds(i * hy, hy)
        return to_core(po.at[at], rc.at[at], s_dc.at[0, i], s_dc.at[1, i])

    for i in range(2):
        po[i * hy : (i + 1) * hy] = rows_of(o, i)
        to_other(i).start()
    for i in range(2):
        pm[i * hy : (i + 1) * hy] = rows_of(c, i)
    for i in range(2):
        to_other(i).wait_recv()

    wk = width_part // 8

    def pack0(k, _):
        both = pm[k] + rc[k]
        pm[k] = both
        last = [both[zz * 8 + 6 : zz * 8 + 8] for zz in range(nz)]
        q1[k] = stack(jnp.concatenate(last, axis=0)).astype(BF16)
        return 0

    lax.fori_loop(0, ny, pack0, 0)
    x_q1.start()
    rq1[y] = q1[y]

    def pack1(k, _):
        d1[k] = pm[k, :, :half].astype(BF16)
        return 0

    lax.fori_loop(0, ny, pack1, 0)
    x_d1.start()
    rd1[y] = d1[y]

    x_q1.recv()
    line = rq1[0].astype(F32)
    for p in range(1, ny):
        line = line + rq1[p].astype(F32)
    rq2[z] = line
    x_q2.start()

    def pack2(k, _):
        for zz in range(nz):
            pair = jnp.concatenate(
                [pm[2 * k, zz * 8 : zz * 8 + 8, half:], pm[2 * k + 1, zz * 8 : zz * 8 + 8, half:]], axis=0
            )
            d2[zz, pl.ds(pl.multiple_of(k * 16, 16), 16), :] = pair.astype(BF16)
        return 0

    lax.fori_loop(0, ny // 2, pack2, 0)
    x_d2.start()
    rd2[z] = d2[z]

    def norm(k, total):
        at = pl.ds(pl.multiple_of(k * rv, rv), rv)
        hg[at, :] = (hr[at, :].astype(F32) * rowv[at, 0:1] * gain_ref[...]).astype(BF16)
        mine = pl.ds(pl.multiple_of(k * rv + c * rh, rh), rh)
        return total + jnp.sum(pm[k] * hr[mine, :].astype(F32) * rowv[mine, 0:1], axis=0, keepdims=True)

    gain_part = lax.fori_loop(0, ny, norm, jnp.zeros((1, width_part), F32))
    for k in range(8):
        gg1[y, k : k + 1, :] = gain_part[:, k * wk : (k + 1) * wk]
    x_g1.start()

    mine = pl.ds(pl.multiple_of(y * rv + c * rh, rh), rh)
    of_last = lambda x: jnp.concatenate([x[zz * 8 + 6 : zz * 8 + 8] for zz in range(nz)], axis=0)
    h_last = of_last(hr[mine, :].astype(F32))
    scale_last = of_last(rowv[mine, 0:1])
    inner_last = of_last(rowv[mine, 1:2])
    x_q2.recv()
    line = rq2[0]
    for p in range(1, nz):
        line = line + rq2[p]
    grad_last = jnp.concatenate([line[: 2 * nz], line[2 * nz :]], axis=1)
    rows_last = scale_last * (grad_last * gain_ref[...]) - h_last * (
        scale_last * scale_last * inner_last / width
    )
    ls[c, y] = stack(rows_last).astype(BF16)

    def pass_on(p):
        ref = ls.at[c, p]
        return to_core(ref, ref, s_ec.at[0, p], s_ec.at[1, p])

    x_e.start()
    pass_on(y).start()

    wt = min(width_part, 256)
    for m in range(0, width_part, wt):
        part = lax.dot_general(
            df[...], hg[:, m : m + wt], (((0,), (0,)), ((), ())), preferred_element_type=F32
        )
        gheadv[:, m : m + wt] = part[:vc].astype(BF16)
    store_head = pltpu.make_async_copy(gheadv, ghead_ref, s_out.at[0])
    store_head.start()
    x_act.recv()

    def acts_in(p, _):
        tile = act[p].astype(F32)
        parts = [tile[zz * 4 + cc * 2 : zz * 4 + cc * 2 + 2] for cc in range(2) for zz in range(nz)]
        act[p] = jnp.concatenate(parts, axis=0).astype(BF16)
        return 0

    x_act.sent()
    lax.fori_loop(0, nv, acts_in, 0)

    x_d1.recv()
    sum1 = rd1[0].astype(F32)
    for p in range(1, ny):
        sum1 = sum1 + rd1[p].astype(F32)
    for zz in range(nz):
        d1b[zz] = stack(sum1[zz * 8 : zz * 8 + 8]).astype(BF16)
    x_d3.start()
    rd1b[z] = d1b[z]
    x_d2.recv()
    sum2 = rd2[0].astype(F32)
    for p in range(1, nz):
        sum2 = sum2 + rd2[p].astype(F32)
    for k in range(ny):
        d2b[k] = stack(sum2[k * 8 : k * 8 + 8]).astype(BF16)
    x_d4.start()
    rd2b[y] = d2b[y]
    x_g1.recv()
    gain_y = gg1[0]
    for p in range(1, ny):
        gain_y = gain_y + gg1[p]
    gg2[g] = gain_y
    x_g2.start()

    x_e.recv(lambda p: pass_on(p).start())

    def rows_out(j, _):
        p = nearest(j)
        ref = ls.at[o, p]
        to_core(ref, ref, s_ec.at[0, p], s_ec.at[1, p]).wait_recv()
        a, b = ls[0, p].astype(F32), ls[1, p].astype(F32)
        lr[p, :, :half] = jnp.concatenate([a[: 2 * nz], b[: 2 * nz]], axis=0).astype(BF16)
        lr[p, :, half:] = jnp.concatenate([a[2 * nz :], b[2 * nz :]], axis=0).astype(BF16)
        return 0

    lax.fori_loop(0, ny, rows_out, 0)
    tokens = ny * lr.shape[1]
    last = lr[...].reshape(tokens, width_part)
    load_down.wait()
    part = lax.dot_general(last, dwv[...], (((1,), (1,)), ((), ())), preferred_element_type=F32)
    tv = tokens // nv
    lanes_f = lax.broadcasted_iota(jnp.int32, (tv, fp.shape[2]), 1)
    for p in range(nv):
        fp[p] = to_fixed(part[p * tv : (p + 1) * tv], jnp.zeros((tv, 1), F32), lanes_f, ff)
    x_f.start()
    rf[v] = fp[v]
    acts = act[...].reshape(tokens, act.shape[2])
    down = lax.dot_general(acts, last, (((0,), (0,)), ((), ())), preferred_element_type=F32)
    gdownv[...] = down[:ff].astype(BF16)
    store_down = pltpu.make_async_copy(gdownv, gdown_ref, s_out.at[1])
    store_down.start()

    x_d3.recv()
    g1 = rd1b[0].astype(F32)
    for p in range(1, nz):
        g1 = g1 + rd1b[p].astype(F32)
    x_d4.recv()
    g2 = rd2b[0].astype(F32)
    for p in range(1, ny):
        g2 = g2 + rd2b[p].astype(F32)
    grad_own = jnp.concatenate([g1[:8], g1[8:], g2[:8], g2[8:]], axis=1)
    own_at = pl.ds(pl.multiple_of(y * rv + c * rh + z * 8, 8), 8)
    scale_own = rowv[own_at, 0:1]
    inner_own = rowv[own_at, 1:2]
    ghs[...] = scale_own * (grad_own * gain_ref[...]) - hown[...] * (
        scale_own * scale_own * inner_own / width
    )
    for e in range(EXITS):
        gh_ref[e] = ghs[2 * e : 2 * e + 2, :].astype(BF16)
    x_g2.recv()
    gain_all = gg2[0]
    for p in range(1, ng):
        gain_all = gain_all + gg2[p]
    for k in range(8):
        ggain_ref[:, k * wk : (k + 1) * wk] = gain_all[k : k + 1, :]

    x_f.recv()
    acc = from_fixed(rf[0], ff)[0]
    for p in range(1, nv):
        acc = acc + from_fixed(rf[p], ff)[0]
    for zz in range(nz):
        for cc in range(2):
            to = zz * 4 + cc * 2
            at = cc * 2 * nz + zz * 2
            gactv[to : to + 2, :] = acc[at : at + 2, :ff]
    gact_ref[...] = gactv[...].astype(BF16)

    x_a1.sent()
    x_a2.sent()
    x_a3.sent()
    x_a4.sent()
    lax.fori_loop(0, ny, lambda p, _: (across1(p, c).wait_send(), 0)[1], 0)
    lax.fori_loop(0, nz, lambda p, _: (across2(p, c).wait_send(), 0)[1], 0)

    lax.fori_loop(0, ny, lambda p, _: (pass_on(p).wait_send(), 0)[1], 0)
    each(nv, v, lambda p, _: to_tokens(p).wait_send())
    x_s1.sent()
    x_s2.sent()
    x_s3.sent()
    x_c.sent()
    for i in range(2):
        to_other(i).wait_send()
    x_d1.sent()
    x_d2.sent()
    x_d3.sent()
    x_d4.sent()
    x_q1.sent()
    x_q2.sent()
    x_g1.sent()
    x_e.sent()
    x_g2.sent()
    x_f.sent()
    store_head.wait()
    store_down.wait()


def hand_on_kernel(n, *refs):
    ins, outs, held, sems = refs[:n], refs[n : 2 * n], refs[2 * n : 3 * n], refs[3 * n]
    load = [pltpu.make_async_copy(ins[i], held[i], sems.at[0, i]) for i in range(n)]
    store = [pltpu.make_async_copy(held[i], outs[i], sems.at[1, i]) for i in range(n)]
    for copy in load:
        copy.start()
    for i in range(n):
        load[i].wait()
        store[i].start()
    for copy in store:
        copy.wait()


def hand_on(arrays):
    n = len(arrays)
    hbm = pl.BlockSpec(memory_space=pl.ANY)
    return pl.pallas_call(
        functools.partial(hand_on_kernel, n),
        out_shape=tuple(jax.ShapeDtypeStruct(a.shape, a.dtype) for a in arrays),
        in_specs=[hbm] * n,
        out_specs=(hbm,) * n,
        scratch_shapes=[pltpu.VMEM(a.shape, a.dtype) for a in arrays] + [pltpu.SemaphoreType.DMA((2, n))],
        compiler_params=pltpu.CompilerParams(vmem_limit_bytes=56 * 1024 * 1024),
    )(*arrays)


def body(ny, nz, hidden, norm_gain, head, targets, scale_index, layer_act, down_weight):
    nv = lax.axis_size("vocab")
    exits, own_tokens, w = hidden.shape
    vc = head.shape[1]
    tok_v, ff = layer_act.shape
    fpad = -(-ff // 128) * 128
    ng = 2 * nz
    rv = OWN * ng
    rh = rv // 2
    rows = rv * ny
    half, q, wk = w // 2, w // 4, w // 8
    tok_y = own_tokens * ng
    vm = pltpu.VMEM
    sem = lambda *n: pltpu.SemaphoreType.DMA(n)
    dma = lambda n: sem(2, n)
    scratch = [
        vm((OWN, w), F32), vm((2, ny, nz, 16, q), BF16), vm((2, nz, ny, 16, q), BF16),
        vm((nv, tok_v, fpad), BF16), vm((vc, w), BF16), vm((VP, w), BF16), vm((fpad, w), BF16),
        vm((vc, w), BF16), vm((ff, w), BF16), vm((rows, w), BF16), vm((rows, w), BF16),
        vm((nv, rv, VP), jnp.int16), vm((nv, rv, VP), jnp.int16),
        vm((ny, 8, 128), F32), vm((ng, 8, 128), F32), vm((nv, 8, 128), F32),
        vm((rows, VP), BF16), vm((rows, VP), BF16), vm((rows, 128), F32),
        vm((ny, rh, w), F32), vm((ny, rh, w), F32), vm((ny, rh, w), F32),
        vm((ny, rh, half), BF16), vm((nz, ny * 8, half), BF16),
        vm((ny, rh, half), BF16), vm((nz, ny * 8, half), BF16),
        vm((nz, 16, q), BF16), vm((ny, 16, q), BF16), vm((nz, 16, q), BF16), vm((ny, 16, q), BF16),
        vm((OWN, w), F32), vm((ny, 4 * nz, half), BF16), vm((ny, 4 * nz, half), BF16), vm((nz, 4 * nz, half), F32),
        vm((ny, 8, wk), F32), vm((ng, 8, wk), F32),
        vm((2, ny, 4 * nz, half), BF16), vm((ny, tok_y, w), BF16),
        vm((nv, tok_v, fpad), jnp.int16), vm((nv, tok_v, fpad), jnp.int16), vm((tok_v, ff), F32),
        dma(nv), sem(2), sem(2), dma(nz), dma(ny), dma(ny), dma(nz), dma(ny), dma(nz),
        dma(nv), dma(ny), dma(ng), dma(nv), dma(nv),
        dma(2), dma(ny), dma(nz), dma(nz), dma(ny),
        dma(ny), dma(nz), dma(ny), dma(ny), dma(ng), dma(ny), dma(nv),
    ]
    spec = pl.BlockSpec(memory_space=vm)
    hbm = pl.BlockSpec(memory_space=pl.ANY)
    sds = jax.ShapeDtypeStruct
    results = pl.pallas_call(
        functools.partial(kernel, ny, nz, nv, vc),
        out_shape=(
            sds((1, 1), F32), sds(hidden.shape, BF16), sds((vc, w), BF16), sds((1, w), F32),
            sds(layer_act.shape, BF16), sds(down_weight.shape, BF16),
        ),
        in_specs=[spec, spec, hbm, spec, spec, spec, hbm],
        out_specs=(spec, spec, hbm, spec, spec, hbm),
        scratch_shapes=scratch,
        compiler_params=pltpu.CompilerParams(
            collective_id=0, has_side_effects=True, vmem_limit_bytes=56 * 1024 * 1024
        ),
    )(
        hidden, norm_gain.reshape(1, w), head.T, targets.reshape(1, -1), scale_index, layer_act, down_weight
    )
    loss, grad_hidden, grad_head, grad_gain, grad_act, grad_down = hand_on(results)
    return loss[0, 0], grad_hidden, grad_head.T, grad_gain.reshape(w), grad_act, grad_down


def solution(mesh, ny=8, nz=4):
    return jax.shard_map(
        functools.partial(body, ny, nz),
        mesh=mesh,
        in_specs=(
            P(None, "fsdp", "vocab"),
            P("vocab"),
            P("vocab", "fsdp"),
            P("vocab"),
            P(None, "vocab"),
            P("vocab", "fsdp"),
            P("fsdp", "vocab"),
        ),
        out_specs=(
            P(),
            P(None, "fsdp", "vocab"),
            P("vocab", "fsdp"),
            P("vocab"),
            P("vocab", "fsdp"),
            P("fsdp", "vocab"),
        ),
        check_vma=False,
    )
```

```python
import functools

import jax
import jax.numpy as jnp
from jax import lax
from jax.experimental import pallas as pl
from jax.experimental.pallas import tpu as pltpu
from jax.sharding import PartitionSpec as P

MESH = pl.DeviceIdType.MESH
EPS = 1e-05
F32 = jnp.float32
BF16 = jnp.bfloat16
EXITS = 4
OWN = 8
FULL = 32700.0
VP = 512


class Exchange:
    def __init__(self, n, me, dev, src, slot, sems):
        self.n, self.me, self.dev, self.src, self.slot, self.sems = n, me, dev, src, slot, sems

    def copy(self, p, j, src, dst, recv):
        return pltpu.make_async_remote_copy(
            src_ref=src, dst_ref=dst, send_sem=self.sems.at[0, j], recv_sem=self.sems.at[1, recv],
            device_id=self.dev(p), device_id_type=MESH,
        )

    def each(self, do):
        def one(j, _):
            do(lax.rem(self.me + j, self.n), j)
            return 0

        lax.fori_loop(1, self.n, one, 0)

    def start(self):
        self.each(lambda p, j: self.copy(p, j, self.src(p), self.slot(self.me), self.me).start())
        return self

    def recv(self, then=None):
        def one(p, j):
            self.copy(p, j, self.slot(p), self.slot(p), p).wait_recv()
            if then is not None:
                then(p)

        self.each(one)

    def sent(self):
        self.each(lambda p, j: self.copy(p, j, self.src(p), self.slot(self.me), self.me).wait_send())


def split3(x):
    hi = x.astype(BF16).astype(F32)
    rest = x - hi
    mid = rest.astype(BF16).astype(F32)
    return hi, mid, rest - mid


def to_fixed(x, extra, lanes, vc):
    top = jnp.maximum(jnp.max(jnp.abs(x), axis=1, keepdims=True), 1e-30)
    power = jnp.ceil(jnp.log2(top))
    out = jnp.floor(x * (jnp.exp2(-power) * FULL) + 0.5)
    first = jnp.floor(extra * 0.5)
    rest = (extra * 0.5 - first) * 32768.0
    second = jnp.floor(rest)
    third = jnp.floor((rest - second) * 32768.0)
    for i, value in enumerate((power, first, second, third)):
        out = jnp.where(lanes == vc + i, value, out)
    return out.astype(jnp.int32).astype(jnp.int16)


def from_fixed(q, vc):
    x = q.astype(jnp.int32).astype(F32)
    at = lambda i: x[:, vc + i : vc + i + 1]
    extra = 2.0 * (at(1) + (at(2) + at(3) * 2.0**-15) * 2.0**-15)
    return x * (jnp.exp2(at(0)) * (1.0 / FULL)), extra


def stack(x):
    q = x.shape[1] // 2
    return jnp.concatenate([x[:, :q], x[:, q:]], axis=0)


def kernel(
    ny, nz, nv, vc,
    hid_ref, gain_ref, head_ref, tgt_ref, si_ref, act_ref, dw_ref,
    loss_ref, gh_ref, ghead_ref, ggain_ref, gact_ref, gdown_ref,
    hown, ga, act, headv, headp, dwv, gheadv, gdownv, hr, hg, lg, rb, st1, st2, st3, ef, df, rowv,
    po, pm, rc, d1, d2, rd1, rd2, d1b, d2b, rd1b, rd2b, ghs, q1, rq1, rq2, gg1, gg2, ls, lr, fp, rf, gactv,
    s_act, s_in, s_out, r_a, s_a0z, s_a0y, s_a1y, s_a1z, s_ac, s_b, s_s1, s_s2, s_s3, s_c, s_dc, s_d1, s_d2, s_d3, s_d4,
    s_q1, s_q2, s_e, s_g1, s_g2, s_ec, s_f,
):
    width_part = hid_ref.shape[2]
    width = width_part * nv
    half, q = width_part // 2, width_part // 4
    ng = 2 * nz
    rv = OWN * ng
    rh = rv // 2
    rows = rv * ny
    tb = rv // EXITS
    ff = dw_ref.shape[0]

    f = lax.axis_index("fsdp")
    v = lax.axis_index("vocab")
    y = f // ng
    g = f % ng
    z = g // 2
    c = g % 2
    o = 1 - c
    dev_y = lambda p: (p * ng + g, v)
    dev_g = lambda p: (y * ng + p, v)
    dev_z = lambda p: (y * ng + p * 2 + c, v)
    dev_v = lambda p: (f, p)
    dev_c = (y * ng + z * 2 + o, v)

    def to_core(src, dst, ss, rs):
        return pltpu.make_async_remote_copy(
            src_ref=src, dst_ref=dst, send_sem=ss, recv_sem=rs, device_id=dev_c, device_id_type=MESH
        )

    barrier = pltpu.get_barrier_semaphore()

    def greet(n, me, dev):
        def one(j, _):
            pl.semaphore_signal(barrier, inc=1, device_id=dev(lax.rem(me + j, n)), device_id_type=MESH)
            return 0

        lax.fori_loop(1, n, one, 0)

    load_head = pltpu.make_async_copy(head_ref, headv, s_in.at[0])
    load_down = pltpu.make_async_copy(dw_ref, dwv.at[pl.ds(0, ff)], s_in.at[1])
    greet(ny, y, dev_y)
    greet(ng, g, dev_g)
    greet(nv, v, dev_v)
    load_head.start()
    load_down.start()

    for e in range(EXITS):
        hown[2 * e : 2 * e + 2, :] = hid_ref[e].astype(F32)
    ga[c, y, z, 0] = stack(hown[:, :half]).astype(BF16)
    ga[c, y, z, 1] = stack(hown[:, half:]).astype(BF16)
    act[v, :, :ff] = act_ref[...]
    dwv[ff:, :] = jnp.zeros((dwv.shape[0] - ff, width_part), BF16)
    act[v, :, ff:] = jnp.zeros((act.shape[1], act.shape[2] - ff), BF16)

    pl.semaphore_wait(barrier, ny + ng + nv - 3)

    at_v = lambda p: ef.at[pl.ds(pl.multiple_of(p * rv, rv), rv)]
    in_y = functools.partial(Exchange, ny, y, dev_y)
    in_z = functools.partial(Exchange, nz, z, dev_z)
    in_g = functools.partial(Exchange, ng, g, dev_g)
    in_v = functools.partial(Exchange, nv, v, dev_v)
    x_act = in_v(lambda p: act.at[v], lambda p: act.at[p], s_act)
    x_b = in_v(lambda p: lg.at[p], lambda p: rb.at[p], s_b)
    x_s1 = in_g(lambda p: st1.at[g], lambda p: st1.at[p], s_s1)
    x_s2 = in_y(lambda p: st2.at[y], lambda p: st2.at[p], s_s2)
    x_s3 = in_v(lambda p: st3.at[v], lambda p: st3.at[p], s_s3)
    x_c = in_v(lambda p: at_v(v), at_v, s_c)
    x_d1 = in_y(lambda p: d1.at[p], lambda p: rd1.at[p], s_d1)
    x_d2 = in_z(lambda p: d2.at[p], lambda p: rd2.at[p], s_d2)
    x_d3 = in_z(lambda p: d1b.at[p], lambda p: rd1b.at[p], s_d3)
    x_d4 = in_y(lambda p: d2b.at[p], lambda p: rd2b.at[p], s_d4)
    x_q1 = in_y(lambda p: q1.at[p], lambda p: rq1.at[p], s_q1)
    x_q2 = in_z(lambda p: rq2.at[z], lambda p: rq2.at[p], s_q2)
    x_e = in_y(lambda p: ls.at[c, y], lambda p: ls.at[c, p], s_e)
    x_g1 = in_y(lambda p: gg1.at[y], lambda p: gg1.at[p], s_g1)
    x_g2 = in_g(lambda p: gg2.at[g], lambda p: gg2.at[p], s_g2)
    x_f = in_v(lambda p: fp.at[p], lambda p: rf.at[p], s_f)

    def block(dev, p, h, yy, zz, send):
        ref = ga.at[c, yy, zz, h]
        return pltpu.make_async_remote_copy(
            src_ref=ref, dst_ref=ref, send_sem=send, recv_sem=r_a.at[h, yy, zz],
            device_id=dev(p), device_id_type=MESH,
        )

    def each(n, me, do):
        def one(j, _):
            do(lax.rem(me + j, n), j)
            return 0

        lax.fori_loop(1, n, one, 0)

    own_z = lambda p, j: block(dev_z, p, 0, y, z, s_a0z.at[j])
    own_y = lambda p, j: block(dev_y, p, 1, y, z, s_a1y.at[j])
    on_y = lambda zz: lambda p, j: block(dev_y, p, 0, y, zz, s_a0y.at[zz, j])
    on_z = lambda yy: lambda p, j: block(dev_z, p, 1, yy, z, s_a1z.at[yy, j])
    begin = lambda make: lambda p, j: make(p, j).start()
    finish = lambda make: lambda p, j: make(p, j).wait_send()

    def arrived(h, yy, zz):
        block(dev_y, y, h, yy, zz, s_a0z.at[0]).wait_recv()

    each(nz, z, begin(own_z))
    each(ny, y, begin(own_y))
    each(ny, y, begin(on_y(z)))
    each(nz, z, begin(on_z(y)))

    load_head.wait()
    cut = vc // 16 * 16
    headp[:cut, :] = headv[:cut, :]
    tail = headv[cut:vc, :].astype(F32)
    headp[cut:, :] = jnp.concatenate([tail, jnp.zeros((VP - vc, width_part), F32)], axis=0).astype(BF16)

    for d in range(1, max(ny, nz) // 2 + 1):
        for shift in (d, -d):
            if d <= ny // 2 and (shift > 0 or 2 * d < ny):
                yy = lax.rem(y + shift + ny, ny)
                arrived(1, yy, z)
                each(nz, z, begin(on_z(yy)))
            if d <= nz // 2 and (shift > 0 or 2 * d < nz):
                zz = lax.rem(z + shift + nz, nz)
                arrived(0, y, zz)
                each(ny, y, begin(on_y(zz)))

    def across(yy):
        ref = ga.at[c, yy]
        return to_core(ref, ref, s_ac.at[0, yy], s_ac.at[1, yy])

    def nearest(j):
        return lax.rem(y + ny + jnp.where(j % 2 == 1, (j + 1) // 2, -(j // 2)), ny)

    def line_of(j, _):
        yy = nearest(j)

        @pl.when(j > 0)
        def _():
            lax.fori_loop(0, nz, lambda zz, _: (arrived(0, yy, zz), 0)[1], 0)

        each(nz, z, lambda p, _: arrived(1, yy, p))
        across(yy).start()
        return 0

    lanes = lax.broadcasted_iota(jnp.int32, (rv, VP), 1)

    def to_tokens(k):
        return pltpu.make_async_remote_copy(
            src_ref=lg.at[k], dst_ref=rb.at[v], send_sem=s_b.at[0, k], recv_sem=s_b.at[1, v],
            device_id=dev_v(k), device_id_type=MESH,
        )

    def rows_in(j):
        k = nearest(j)
        to_core(ga.at[o, k], ga.at[o, k], s_ac.at[0, k], s_ac.at[1, k]).wait_recv()
        at = pl.ds(pl.multiple_of(k * rv, rv), rv)
        sums = []
        for cc in range(2):
            for zz in range(0, nz, 2):
                to_at = pl.ds(pl.multiple_of(k * rv + cc * rh + zz * OWN, 16), 16)
                squares = None
                for h in range(2):
                    a = ga[cc, k, zz, h].astype(F32)
                    b = ga[cc, k, zz + 1, h].astype(F32)
                    for s in range(2):
                        x = jnp.concatenate([a[s * 8 : s * 8 + 8], b[s * 8 : s * 8 + 8]], axis=0)
                        to = slice((2 * h + s) * q, (2 * h + s + 1) * q)
                        hr[to_at, to] = x.astype(BF16)
                        hg[to_at, to] = (x * gain_ref[:, to]).astype(BF16)
                        squares = x * x if squares is None else squares + x * x
                sums.append(jnp.sum(squares, axis=1, keepdims=True))
        part = lax.dot_general(
            hg[at, :], headp[...], (((1,), (1,)), ((), ())), preferred_element_type=F32
        )
        lg[k] = to_fixed(part, jnp.concatenate(sums, axis=0), lanes, vc)

        @pl.when(k != v)
        def _():
            to_tokens(k).start()

        @pl.when(k == v)
        def _():
            rb[v] = lg[v]

    line_of(0, 0)

    def step(j, _):
        line_of(j, 0)
        rows_in(j - 1)
        return 0

    lax.fori_loop(1, ny, step, 0)
    rows_in(ny - 1)

    r_id = lax.broadcasted_iota(jnp.int32, (rv, 1), 0)
    exit_id = (r_id & 7) >> 1
    tok_id = (((r_id & (rh - 1)) >> 3) << 2) + ((r_id // rh) << 1) + (r_id & 1)
    l16 = lax.broadcasted_iota(jnp.int32, (rv, tb), 1)
    here = l16 == tok_id
    tgt = jnp.sum(jnp.where(here, tgt_ref[...].astype(F32), 0.0), axis=1, keepdims=True)
    index = jnp.zeros((rv, 1), F32)
    for e in range(EXITS):
        index += jnp.sum(
            jnp.where(here & (exit_id == e), si_ref[e : e + 1, :].astype(F32), 0.0), axis=1, keepdims=True
        )
    weight = jnp.exp2(4.0 - index)
    column = (lanes + f * vc).astype(F32)
    valid = lanes < vc
    onehot = (column == tgt) & valid
    x_b.recv()
    logits, squares = from_fixed(rb[0], vc)
    for p in range(1, nv):
        more = from_fixed(rb[p], vc)
        logits, squares = logits + more[0], squares + more[1]
    scale = lax.rsqrt(squares / width + EPS)
    logits = logits * scale
    peak = jnp.max(jnp.where(valid, logits, -3e38), axis=1, keepdims=True)
    grown = jnp.where(valid, jnp.exp(jnp.minimum(logits - peak, 0.0)), 0.0)
    total = jnp.sum(grown, axis=1, keepdims=True)
    moment = jnp.sum(grown * jnp.where(valid, logits, 0.0), axis=1, keepdims=True)
    picked = jnp.sum(jnp.where(onehot, logits, 0.0), axis=1, keepdims=True)

    eye = lax.broadcasted_iota(jnp.int32, (rv, 128), 0) == lax.broadcasted_iota(jnp.int32, (rv, 128), 1)
    to_row = lambda x: jnp.sum(jnp.where(eye, x, 0.0), axis=0, keepdims=True)
    to_col = lambda x: jnp.sum(jnp.where(eye, x, 0.0), axis=1, keepdims=True)

    def put(ref, at, values):
        for i, value in enumerate(values):
            ref[at, i : i + 1, :] = value
        ref[at, len(values) :, :] = jnp.zeros((8 - len(values), 128), F32)

    def merge(ref, n):
        top = ref[0, 0:1, :]
        for p in range(1, n):
            top = jnp.maximum(top, ref[p, 0:1, :])
        tot = mom = pick = jnp.zeros((1, 128), F32)
        for p in range(n):
            by = jnp.exp(ref[p, 0:1, :] - top)
            tot = tot + by * ref[p, 1:2, :]
            mom = mom + by * ref[p, 2:3, :]
            pick = pick + ref[p, 3:4, :]
        return top, tot, mom, pick

    put(st1, g, [to_row(peak), to_row(total), to_row(moment), to_row(picked)])
    x_s1.start()
    out = jnp.where(onehot, 0.0, grown)
    for i, value in enumerate(split3(peak)):
        out = jnp.where(lanes == vc + i, value, out)
    ef[pl.ds(pl.multiple_of(v * rv, rv), rv), :] = out.astype(BF16)
    weight_row, scale_row, tgt_row = to_row(weight), to_row(scale), to_row(tgt)
    x_s1.recv()
    put(st2, y, merge(st1, ng))
    x_s2.start()
    x_c.start()
    x_s2.recv()
    top, tot, mom, pick = merge(st2, ny)
    lse = top + jnp.log(tot)
    inner = weight_row * (mom / tot - pick)
    missed = weight_row * (jnp.exp(jnp.minimum(pick - lse, 0.0)) - 1.0)
    put(st3, v, [scale_row, inner, lse, missed, weight_row * (lse - pick), weight_row, tgt_row])
    x_s3.start()
    x_act.start()
    x_s3.recv()
    x_c.recv()

    def logit_grads(k, loss):
        at = pl.ds(pl.multiple_of(k * rv, rv), rv)
        scale_k, inner_k, lse_k, missed_k, _, weight_k, tgt_k = (to_col(st3[k, i : i + 1, :]) for i in range(7))
        grown_k = ef[at, :].astype(F32)
        peak_k = grown_k[:, vc : vc + 1] + grown_k[:, vc + 1 : vc + 2] + grown_k[:, vc + 2 : vc + 3]
        prob = (weight_k * jnp.exp(jnp.minimum(peak_k - lse_k, 0.0))) * grown_k
        df[at, :] = jnp.where(valid, jnp.where(column == tgt_k, missed_k, prob), 0.0).astype(BF16)
        rowv[at, 0:1] = scale_k
        rowv[at, 1:2] = inner_k
        return loss + st3[k, 4:5, :]

    loss = lax.fori_loop(0, nv, logit_grads, jnp.zeros((1, 128), F32))
    in_use = lax.broadcasted_iota(jnp.int32, (1, 128), 1) < rv
    loss_ref[...] = jnp.sum(jnp.where(in_use, loss, 0.0), axis=1, keepdims=True) / rows

    hy = ny // 2

    def rows_of(core, i):
        lhs = jnp.concatenate(
            [
                df[pl.ds(pl.multiple_of(k * rv + core * rh, rh), rh), :]
                for k in range(i * hy, (i + 1) * hy)
            ],
            axis=0,
        )
        out = lax.dot_general(lhs, headp[...], (((1,), (0,)), ((), ())), preferred_element_type=F32)
        return out.reshape(hy, rh, width_part)

    def to_other(i):
        at = pl.ds(i * hy, hy)
        return to_core(po.at[at], rc.at[at], s_dc.at[0, i], s_dc.at[1, i])

    for i in range(2):
        po[i * hy : (i + 1) * hy] = rows_of(o, i).astype(BF16)
        to_other(i).start()
    for i in range(2):
        pm[i * hy : (i + 1) * hy] = rows_of(c, i)
    for i in range(2):
        to_other(i).wait_recv()

    wk = width_part // 8

    def pack0(k, _):
        both = pm[k] + rc[k].astype(F32)
        pm[k] = both
        last = [both[zz * 8 + 6 : zz * 8 + 8] for zz in range(nz)]
        q1[k] = stack(jnp.concatenate(last, axis=0)).astype(BF16)
        return 0

    lax.fori_loop(0, ny, pack0, 0)
    x_q1.start()
    rq1[y] = q1[y]

    def pack1(k, _):
        d1[k] = pm[k, :, :half].astype(BF16)
        return 0

    lax.fori_loop(0, ny, pack1, 0)
    x_d1.start()
    rd1[y] = d1[y]

    def pack2(k, _):
        for zz in range(nz):
            pair = jnp.concatenate(
                [pm[2 * k, zz * 8 : zz * 8 + 8, half:], pm[2 * k + 1, zz * 8 : zz * 8 + 8, half:]], axis=0
            )
            d2[zz, pl.ds(pl.multiple_of(k * 16, 16), 16), :] = pair.astype(BF16)
        return 0

    lax.fori_loop(0, ny // 2, pack2, 0)
    x_d2.start()
    rd2[z] = d2[z]

    x_q1.recv()
    line = rq1[0].astype(F32)
    for p in range(1, ny):
        line = line + rq1[p].astype(F32)
    rq2[z] = line
    x_q2.start()

    def norm(k, total):
        at = pl.ds(pl.multiple_of(k * rv, rv), rv)
        hg[at, :] = (hr[at, :].astype(F32) * rowv[at, 0:1] * gain_ref[...]).astype(BF16)
        mine = pl.ds(pl.multiple_of(k * rv + c * rh, rh), rh)
        return total + jnp.sum(pm[k] * hr[mine, :].astype(F32) * rowv[mine, 0:1], axis=0, keepdims=True)

    gain_part = lax.fori_loop(0, ny, norm, jnp.zeros((1, width_part), F32))
    for k in range(8):
        gg1[y, k : k + 1, :] = gain_part[:, k * wk : (k + 1) * wk]
    x_g1.start()

    mine = pl.ds(pl.multiple_of(y * rv + c * rh, rh), rh)
    of_last = lambda x: jnp.concatenate([x[zz * 8 + 6 : zz * 8 + 8] for zz in range(nz)], axis=0)
    h_last = of_last(hr[mine, :].astype(F32))
    scale_last = of_last(rowv[mine, 0:1])
    inner_last = of_last(rowv[mine, 1:2])
    x_q2.recv()
    line = rq2[0]
    for p in range(1, nz):
        line = line + rq2[p]
    grad_last = jnp.concatenate([line[: 2 * nz], line[2 * nz :]], axis=1)
    rows_last = scale_last * (grad_last * gain_ref[...]) - h_last * (
        scale_last * scale_last * inner_last / width
    )
    ls[c, y] = stack(rows_last).astype(BF16)

    def pass_on(p):
        ref = ls.at[c, p]
        return to_core(ref, ref, s_ec.at[0, p], s_ec.at[1, p])

    x_e.start()
    pass_on(y).start()

    wt = min(width_part, 256)
    for m in range(0, width_part, wt):
        part = lax.dot_general(
            df[...], hg[:, m : m + wt], (((0,), (0,)), ((), ())), preferred_element_type=F32
        )
        gheadv[:, m : m + wt] = part[:vc].astype(BF16)
    store_head = pltpu.make_async_copy(gheadv, ghead_ref, s_out.at[0])
    store_head.start()
    x_act.recv()

    def acts_in(p, _):
        tile = act[p].astype(F32)
        parts = [tile[zz * 4 + cc * 2 : zz * 4 + cc * 2 + 2] for cc in range(2) for zz in range(nz)]
        act[p] = jnp.concatenate(parts, axis=0).astype(BF16)
        return 0

    x_act.sent()
    lax.fori_loop(0, nv, acts_in, 0)

    x_d1.recv()
    sum1 = rd1[0].astype(F32)
    for p in range(1, ny):
        sum1 = sum1 + rd1[p].astype(F32)
    for zz in range(nz):
        d1b[zz] = stack(sum1[zz * 8 : zz * 8 + 8]).astype(BF16)
    x_d3.start()
    rd1b[z] = d1b[z]
    x_d2.recv()
    sum2 = rd2[0].astype(F32)
    for p in range(1, nz):
        sum2 = sum2 + rd2[p].astype(F32)
    for k in range(ny):
        d2b[k] = stack(sum2[k * 8 : k * 8 + 8]).astype(BF16)
    x_d4.start()
    rd2b[y] = d2b[y]
    x_g1.recv()
    gain_y = gg1[0]
    for p in range(1, ny):
        gain_y = gain_y + gg1[p]
    gg2[g] = gain_y
    x_g2.start()

    x_e.recv(lambda p: pass_on(p).start())

    def rows_out(j, _):
        p = nearest(j)
        ref = ls.at[o, p]
        to_core(ref, ref, s_ec.at[0, p], s_ec.at[1, p]).wait_recv()
        a, b = ls[0, p].astype(F32), ls[1, p].astype(F32)
        lr[p, :, :half] = jnp.concatenate([a[: 2 * nz], b[: 2 * nz]], axis=0).astype(BF16)
        lr[p, :, half:] = jnp.concatenate([a[2 * nz :], b[2 * nz :]], axis=0).astype(BF16)
        return 0

    lax.fori_loop(0, ny, rows_out, 0)
    tokens = ny * lr.shape[1]
    last = lr[...].reshape(tokens, width_part)
    load_down.wait()
    part = lax.dot_general(last, dwv[...], (((1,), (1,)), ((), ())), preferred_element_type=F32)
    tv = tokens // nv
    lanes_f = lax.broadcasted_iota(jnp.int32, (tv, fp.shape[2]), 1)
    for p in range(nv):
        fp[p] = to_fixed(part[p * tv : (p + 1) * tv], jnp.zeros((tv, 1), F32), lanes_f, ff)
    x_f.start()
    rf[v] = fp[v]
    acts = act[...].reshape(tokens, act.shape[2])
    down = lax.dot_general(acts, last, (((0,), (0,)), ((), ())), preferred_element_type=F32)
    gdownv[...] = down[:ff].astype(BF16)
    store_down = pltpu.make_async_copy(gdownv, gdown_ref, s_out.at[1])
    store_down.start()

    x_d3.recv()
    g1 = rd1b[0].astype(F32)
    for p in range(1, nz):
        g1 = g1 + rd1b[p].astype(F32)
    x_d4.recv()
    g2 = rd2b[0].astype(F32)
    for p in range(1, ny):
        g2 = g2 + rd2b[p].astype(F32)
    grad_own = jnp.concatenate([g1[:8], g1[8:], g2[:8], g2[8:]], axis=1)
    own_at = pl.ds(pl.multiple_of(y * rv + c * rh + z * 8, 8), 8)
    scale_own = rowv[own_at, 0:1]
    inner_own = rowv[own_at, 1:2]
    ghs[...] = scale_own * (grad_own * gain_ref[...]) - hown[...] * (
        scale_own * scale_own * inner_own / width
    )
    for e in range(EXITS):
        gh_ref[e] = ghs[2 * e : 2 * e + 2, :].astype(BF16)
    x_g2.recv()
    gain_all = gg2[0]
    for p in range(1, ng):
        gain_all = gain_all + gg2[p]
    for k in range(8):
        ggain_ref[:, k * wk : (k + 1) * wk] = gain_all[k : k + 1, :]

    x_f.recv()
    acc = from_fixed(rf[0], ff)[0]
    for p in range(1, nv):
        acc = acc + from_fixed(rf[p], ff)[0]
    for zz in range(nz):
        for cc in range(2):
            to = zz * 4 + cc * 2
            at = cc * 2 * nz + zz * 2
            gactv[to : to + 2, :] = acc[at : at + 2, :ff]
    gact_ref[...] = gactv[...].astype(BF16)

    each(nz, z, finish(own_z))
    each(ny, y, finish(own_y))
    lax.fori_loop(0, nz, lambda zz, _: (each(ny, y, finish(on_y(zz))), 0)[1], 0)
    lax.fori_loop(0, ny, lambda yy, _: (each(nz, z, finish(on_z(yy))), 0)[1], 0)
    lax.fori_loop(0, ny, lambda yy, _: (across(yy).wait_send(), 0)[1], 0)
    lax.fori_loop(0, ny, lambda p, _: (pass_on(p).wait_send(), 0)[1], 0)
    each(nv, v, lambda p, _: to_tokens(p).wait_send())
    x_s1.sent()
    x_s2.sent()
    x_s3.sent()
    x_c.sent()
    for i in range(2):
        to_other(i).wait_send()
    x_d1.sent()
    x_d2.sent()
    x_d3.sent()
    x_d4.sent()
    x_q1.sent()
    x_q2.sent()
    x_g1.sent()
    x_e.sent()
    x_g2.sent()
    x_f.sent()
    store_head.wait()
    store_down.wait()


def hand_on_kernel(n, *refs):
    ins, outs, held, sems = refs[:n], refs[n : 2 * n], refs[2 * n : 3 * n], refs[3 * n]
    load = [pltpu.make_async_copy(ins[i], held[i], sems.at[0, i]) for i in range(n)]
    store = [pltpu.make_async_copy(held[i], outs[i], sems.at[1, i]) for i in range(n)]
    for copy in load:
        copy.start()
    for i in range(n):
        load[i].wait()
        store[i].start()
    for copy in store:
        copy.wait()


def hand_on(arrays):
    n = len(arrays)
    hbm = pl.BlockSpec(memory_space=pl.ANY)
    return pl.pallas_call(
        functools.partial(hand_on_kernel, n),
        out_shape=tuple(jax.ShapeDtypeStruct(a.shape, a.dtype) for a in arrays),
        in_specs=[hbm] * n,
        out_specs=(hbm,) * n,
        scratch_shapes=[pltpu.VMEM(a.shape, a.dtype) for a in arrays] + [pltpu.SemaphoreType.DMA((2, n))],
        compiler_params=pltpu.CompilerParams(vmem_limit_bytes=56 * 1024 * 1024),
    )(*arrays)


def body(ny, nz, hidden, norm_gain, head, targets, scale_index, layer_act, down_weight):
    nv = lax.axis_size("vocab")
    exits, own_tokens, w = hidden.shape
    vc = head.shape[1]
    tok_v, ff = layer_act.shape
    fpad = -(-ff // 128) * 128
    ng = 2 * nz
    rv = OWN * ng
    rh = rv // 2
    rows = rv * ny
    half, q, wk = w // 2, w // 4, w // 8
    tok_y = own_tokens * ng
    vm = pltpu.VMEM
    sem = lambda *n: pltpu.SemaphoreType.DMA(n)
    dma = lambda n: sem(2, n)
    scratch = [
        vm((OWN, w), F32), vm((2, ny, nz, 2, 16, q), BF16),
        vm((nv, tok_v, fpad), BF16), vm((vc, w), BF16), vm((VP, w), BF16), vm((fpad, w), BF16),
        vm((vc, w), BF16), vm((ff, w), BF16), vm((rows, w), BF16), vm((rows, w), BF16),
        vm((nv, rv, VP), jnp.int16), vm((nv, rv, VP), jnp.int16),
        vm((ng, 8, 128), F32), vm((ny, 8, 128), F32), vm((nv, 8, 128), F32),
        vm((rows, VP), BF16), vm((rows, VP), BF16), vm((rows, 128), F32),
        vm((ny, rh, w), BF16), vm((ny, rh, w), F32), vm((ny, rh, w), BF16),
        vm((ny, rh, half), BF16), vm((nz, ny * 8, half), BF16),
        vm((ny, rh, half), BF16), vm((nz, ny * 8, half), BF16),
        vm((nz, 16, q), BF16), vm((ny, 16, q), BF16), vm((nz, 16, q), BF16), vm((ny, 16, q), BF16),
        vm((OWN, w), F32), vm((ny, 4 * nz, half), BF16), vm((ny, 4 * nz, half), BF16), vm((nz, 4 * nz, half), F32),
        vm((ny, 8, wk), F32), vm((ng, 8, wk), F32),
        vm((2, ny, 4 * nz, half), BF16), vm((ny, tok_y, w), BF16),
        vm((nv, tok_v, fpad), jnp.int16), vm((nv, tok_v, fpad), jnp.int16), vm((tok_v, ff), F32),
        dma(nv), sem(2), sem(2), sem(2, ny, nz), sem(nz), sem(nz, ny), sem(ny), sem(ny, nz), dma(ny),
        dma(nv), dma(ng), dma(ny), dma(nv), dma(nv),
        dma(2), dma(ny), dma(nz), dma(nz), dma(ny),
        dma(ny), dma(nz), dma(ny), dma(ny), dma(ng), dma(ny), dma(nv),
    ]
    spec = pl.BlockSpec(memory_space=vm)
    hbm = pl.BlockSpec(memory_space=pl.ANY)
    sds = jax.ShapeDtypeStruct
    results = pl.pallas_call(
        functools.partial(kernel, ny, nz, nv, vc),
        out_shape=(
            sds((1, 1), F32), sds(hidden.shape, BF16), sds((vc, w), BF16), sds((1, w), F32),
            sds(layer_act.shape, BF16), sds(down_weight.shape, BF16),
        ),
        in_specs=[spec, spec, hbm, spec, spec, spec, hbm],
        out_specs=(spec, spec, hbm, spec, spec, hbm),
        scratch_shapes=scratch,
        compiler_params=pltpu.CompilerParams(
            collective_id=0, has_side_effects=True, vmem_limit_bytes=56 * 1024 * 1024
        ),
    )(
        hidden, norm_gain.reshape(1, w), head.T, targets.reshape(1, -1), scale_index, layer_act, down_weight
    )
    loss, grad_hidden, grad_head, grad_gain, grad_act, grad_down = hand_on(results)
    return loss[0, 0], grad_hidden, grad_head.T, grad_gain.reshape(w), grad_act, grad_down


def solution(mesh, ny=8, nz=4):
    return jax.shard_map(
        functools.partial(body, ny, nz),
        mesh=mesh,
        in_specs=(
            P(None, "fsdp", "vocab"),
            P("vocab"),
            P("vocab", "fsdp"),
            P("vocab"),
            P(None, "vocab"),
            P("vocab", "fsdp"),
            P("fsdp", "vocab"),
        ),
        out_specs=(
            P(),
            P(None, "fsdp", "vocab"),
            P("vocab", "fsdp"),
            P("vocab"),
            P("vocab", "fsdp"),
            P("fsdp", "vocab"),
        ),
        check_vma=False,
    )
```

```python
import functools

import jax
import jax.numpy as jnp
from jax import lax
from jax.experimental import pallas as pl
from jax.experimental.pallas import tpu as pltpu
from jax.sharding import PartitionSpec as P

MESH = pl.DeviceIdType.MESH
EPS = 1e-05
F32 = jnp.float32
BF16 = jnp.bfloat16
EXITS = 4
OWN = 8
FULL = 32700.0
VP = 512


class Exchange:
    def __init__(self, n, me, dev, src, slot, sems):
        self.n, self.me, self.dev, self.src, self.slot, self.sems = n, me, dev, src, slot, sems

    def copy(self, p, j, src, dst, recv):
        return pltpu.make_async_remote_copy(
            src_ref=src, dst_ref=dst, send_sem=self.sems.at[0, j], recv_sem=self.sems.at[1, recv],
            device_id=self.dev(p), device_id_type=MESH,
        )

    def each(self, do, lo=1, hi=None):
        def one(j, _):
            do(lax.rem(self.me + j, self.n), j)
            return 0

        lax.fori_loop(lo, self.n if hi is None else hi, one, 0)

    def start(self, lo=1, hi=None):
        self.each(lambda p, j: self.copy(p, j, self.src(p), self.slot(self.me), self.me).start(), lo, hi)

    def recv(self, then=None):
        def one(p, j):
            self.copy(p, j, self.slot(p), self.slot(p), p).wait_recv()
            if then is not None:
                then(p)

        self.each(one)

    def sent(self):
        self.each(lambda p, j: self.copy(p, j, self.src(p), self.slot(self.me), self.me).wait_send())


def split3(x):
    hi = x.astype(BF16).astype(F32)
    rest = x - hi
    mid = rest.astype(BF16).astype(F32)
    return hi, mid, rest - mid


def to_fixed(x, extra, lanes, vc):
    top = jnp.maximum(jnp.max(jnp.abs(x), axis=1, keepdims=True), 1e-30)
    power = jnp.ceil(jnp.log2(top))
    out = jnp.floor(x * (jnp.exp2(-power) * FULL) + 0.5)
    first = jnp.floor(extra * 0.5)
    rest = (extra * 0.5 - first) * 32768.0
    second = jnp.floor(rest)
    third = jnp.floor((rest - second) * 32768.0)
    for i, value in enumerate((power, first, second, third)):
        out = jnp.where(lanes == vc + i, value, out)
    return out.astype(jnp.int32).astype(jnp.int16)


def from_fixed(q, vc):
    x = q.astype(jnp.int32).astype(F32)
    at = lambda i: x[:, vc + i : vc + i + 1]
    extra = 2.0 * (at(1) + (at(2) + at(3) * 2.0**-15) * 2.0**-15)
    return x * (jnp.exp2(at(0)) * (1.0 / FULL)), extra


def stack(x):
    q = x.shape[1] // 2
    return jnp.concatenate([x[:, :q], x[:, q:]], axis=0)


def kernel(
    ny, nz, nv, vc,
    hid_ref, gain_ref, head_ref, tgt_ref, si_ref, act_ref, dw_ref,
    loss_ref, gh_ref, ghead_ref, ggain_ref, gact_ref, gdown_ref,
    hown, ga, act, headv, headp, dwv, gheadv, gdownv, hr, hg, lg, rb, st1, st2, st3, ef, df, rowv,
    po, pm, rc, d1, d2, rd1, rd2, d1b, d2b, rd1b, rd2b, ghs, q1, rq1, rq2, gg1, gg2, ls, lr, fp, rf, gactv,
    s_act, s_in, s_out, r_a, s_a0z, s_a0y, s_a1y, s_a1z, s_ac, s_b, s_s1, s_s2, s_s3, s_c, s_dc, s_d1, s_d2, s_d3, s_d4,
    s_q1, s_q2, s_e, s_g1, s_g2, s_ec, s_f,
):
    width_part = hid_ref.shape[2]
    width = width_part * nv
    half, q = width_part // 2, width_part // 4
    ng = 2 * nz
    rv = OWN * ng
    rh = rv // 2
    rows = rv * ny
    tb = rv // EXITS
    ff = dw_ref.shape[0]

    f = lax.axis_index("fsdp")
    v = lax.axis_index("vocab")
    y = f // ng
    g = f % ng
    z = g // 2
    c = g % 2
    o = 1 - c
    dev_y = lambda p: (p * ng + g, v)
    dev_g = lambda p: (y * ng + p, v)
    dev_z = lambda p: (y * ng + p * 2 + c, v)
    dev_v = lambda p: (f, p)
    dev_c = (y * ng + z * 2 + o, v)

    def to_core(src, dst, ss, rs):
        return pltpu.make_async_remote_copy(
            src_ref=src, dst_ref=dst, send_sem=ss, recv_sem=rs, device_id=dev_c, device_id_type=MESH
        )

    barrier = pltpu.get_barrier_semaphore()

    def greet(n, me, dev):
        def one(j, _):
            pl.semaphore_signal(barrier, inc=1, device_id=dev(lax.rem(me + j, n)), device_id_type=MESH)
            return 0

        lax.fori_loop(1, n, one, 0)

    load_head = pltpu.make_async_copy(head_ref, headv, s_in.at[0])
    load_down = pltpu.make_async_copy(dw_ref, dwv.at[pl.ds(0, ff)], s_in.at[1])
    greet(ny, y, dev_y)
    greet(ng, g, dev_g)
    greet(nv, v, dev_v)
    load_head.start()
    load_down.start()

    for e in range(EXITS):
        hown[2 * e : 2 * e + 2, :] = hid_ref[e].astype(F32)
    ga[c, y, z, 0] = stack(hown[:, :half]).astype(BF16)
    ga[c, y, z, 1] = stack(hown[:, half:]).astype(BF16)
    act[v, :, :ff] = act_ref[...]
    dwv[ff:, :] = jnp.zeros((dwv.shape[0] - ff, width_part), BF16)
    act[v, :, ff:] = jnp.zeros((act.shape[1], act.shape[2] - ff), BF16)

    pl.semaphore_wait(barrier, ny + ng + nv - 3)

    at_v = lambda p: ef.at[pl.ds(pl.multiple_of(p * rv, rv), rv)]
    in_y = functools.partial(Exchange, ny, y, dev_y)
    in_z = functools.partial(Exchange, nz, z, dev_z)
    in_g = functools.partial(Exchange, ng, g, dev_g)
    in_v = functools.partial(Exchange, nv, v, dev_v)
    x_act = in_v(lambda p: act.at[v], lambda p: act.at[p], s_act)
    x_b = in_v(lambda p: lg.at[p], lambda p: rb.at[p], s_b)
    x_s1 = in_g(lambda p: st1.at[g], lambda p: st1.at[p], s_s1)
    x_s2 = in_y(lambda p: st2.at[y], lambda p: st2.at[p], s_s2)
    x_s3 = in_v(lambda p: st3.at[v], lambda p: st3.at[p], s_s3)
    x_c = in_v(lambda p: at_v(v), at_v, s_c)
    x_d1 = in_y(lambda p: d1.at[p], lambda p: rd1.at[p], s_d1)
    x_d2 = in_z(lambda p: d2.at[p], lambda p: rd2.at[p], s_d2)
    x_d3 = in_z(lambda p: d1b.at[p], lambda p: rd1b.at[p], s_d3)
    x_d4 = in_y(lambda p: d2b.at[p], lambda p: rd2b.at[p], s_d4)
    x_q1 = in_y(lambda p: q1.at[p], lambda p: rq1.at[p], s_q1)
    x_q2 = in_z(lambda p: rq2.at[z], lambda p: rq2.at[p], s_q2)
    x_e = in_y(lambda p: ls.at[c, y], lambda p: ls.at[c, p], s_e)
    x_g1 = in_y(lambda p: gg1.at[y], lambda p: gg1.at[p], s_g1)
    x_g2 = in_g(lambda p: gg2.at[g], lambda p: gg2.at[p], s_g2)
    x_f = in_v(lambda p: fp.at[p], lambda p: rf.at[p], s_f)

    def block(dev, p, h, yy, zz, send):
        ref = ga.at[c, yy, zz, h]
        return pltpu.make_async_remote_copy(
            src_ref=ref, dst_ref=ref, send_sem=send, recv_sem=r_a.at[h, yy, zz],
            device_id=dev(p), device_id_type=MESH,
        )

    def each(n, me, do):
        def one(j, _):
            do(lax.rem(me + j, n), j)
            return 0

        lax.fori_loop(1, n, one, 0)

    own_z = lambda p, j: block(dev_z, p, 0, y, z, s_a0z.at[j])
    own_y = lambda p, j: block(dev_y, p, 1, y, z, s_a1y.at[j])
    on_y = lambda zz: lambda p, j: block(dev_y, p, 0, y, zz, s_a0y.at[zz, j])
    on_z = lambda yy: lambda p, j: block(dev_z, p, 1, yy, z, s_a1z.at[yy, j])
    begin = lambda make: lambda p, j: make(p, j).start()
    finish = lambda make: lambda p, j: make(p, j).wait_send()

    def arrived(h, yy, zz):
        block(dev_y, y, h, yy, zz, s_a0z.at[0]).wait_recv()

    each(nz, z, begin(own_z))
    each(ny, y, begin(own_y))
    each(ny, y, begin(on_y(z)))
    each(nz, z, begin(on_z(y)))

    load_head.wait()
    cut = vc // 16 * 16
    headp[:cut, :] = headv[:cut, :]
    tail = headv[cut:vc, :].astype(F32)
    headp[cut:, :] = jnp.concatenate([tail, jnp.zeros((VP - vc, width_part), F32)], axis=0).astype(BF16)

    for d in range(1, max(ny, nz) // 2 + 1):
        for shift in (d, -d):
            if d <= ny // 2 and (shift > 0 or 2 * d < ny):
                yy = lax.rem(y + shift + ny, ny)
                arrived(1, yy, z)
                each(nz, z, begin(on_z(yy)))
            if d <= nz // 2 and (shift > 0 or 2 * d < nz):
                zz = lax.rem(z + shift + nz, nz)
                arrived(0, y, zz)
                each(ny, y, begin(on_y(zz)))

    def across(yy):
        ref = ga.at[c, yy]
        return to_core(ref, ref, s_ac.at[0, yy], s_ac.at[1, yy])

    def nearest(j):
        return lax.rem(y + ny + jnp.where(j % 2 == 1, (j + 1) // 2, -(j // 2)), ny)

    def line_of(j, _):
        yy = nearest(j)

        @pl.when(j > 0)
        def _():
            lax.fori_loop(0, nz, lambda zz, _: (arrived(0, yy, zz), 0)[1], 0)

        each(nz, z, lambda p, _: arrived(1, yy, p))
        across(yy).start()
        return 0

    lanes = lax.broadcasted_iota(jnp.int32, (rv, VP), 1)

    def to_tokens(k):
        return pltpu.make_async_remote_copy(
            src_ref=lg.at[k], dst_ref=rb.at[v], send_sem=s_b.at[0, k], recv_sem=s_b.at[1, v],
            device_id=dev_v(k), device_id_type=MESH,
        )

    def rows_in(j):
        k = nearest(j)
        to_core(ga.at[o, k], ga.at[o, k], s_ac.at[0, k], s_ac.at[1, k]).wait_recv()
        at = pl.ds(pl.multiple_of(k * rv, rv), rv)
        sums = []
        for cc in range(2):
            for zz in range(0, nz, 2):
                to_at = pl.ds(pl.multiple_of(k * rv + cc * rh + zz * OWN, 16), 16)
                squares = None
                for h in range(2):
                    a = ga[cc, k, zz, h].astype(F32)
                    b = ga[cc, k, zz + 1, h].astype(F32)
                    for s in range(2):
                        x = jnp.concatenate([a[s * 8 : s * 8 + 8], b[s * 8 : s * 8 + 8]], axis=0)
                        to = slice((2 * h + s) * q, (2 * h + s + 1) * q)
                        hr[to_at, to] = x.astype(BF16)
                        hg[to_at, to] = (x * gain_ref[:, to]).astype(BF16)
                        squares = x * x if squares is None else squares + x * x
                sums.append(jnp.sum(squares, axis=1, keepdims=True))
        part = lax.dot_general(
            hg[at, :], headp[...], (((1,), (1,)), ((), ())), preferred_element_type=F32
        )
        lg[k] = to_fixed(part, jnp.concatenate(sums, axis=0), lanes, vc)

        @pl.when(k != v)
        def _():
            to_tokens(k).start()

        @pl.when(k == v)
        def _():
            rb[v] = lg[v]

    line_of(0, 0)

    def step(j, _):
        line_of(j, 0)
        rows_in(j - 1)
        return 0

    lax.fori_loop(1, ny, step, 0)
    rows_in(ny - 1)

    r_id = lax.broadcasted_iota(jnp.int32, (rv, 1), 0)
    exit_id = (r_id & 7) >> 1
    tok_id = (((r_id & (rh - 1)) >> 3) << 2) + ((r_id // rh) << 1) + (r_id & 1)
    l16 = lax.broadcasted_iota(jnp.int32, (rv, tb), 1)
    here = l16 == tok_id
    tgt = jnp.sum(jnp.where(here, tgt_ref[...].astype(F32), 0.0), axis=1, keepdims=True)
    index = jnp.zeros((rv, 1), F32)
    for e in range(EXITS):
        index += jnp.sum(
            jnp.where(here & (exit_id == e), si_ref[e : e + 1, :].astype(F32), 0.0), axis=1, keepdims=True
        )
    weight = jnp.exp2(4.0 - index)
    column = (lanes + f * vc).astype(F32)
    valid = lanes < vc
    onehot = (column == tgt) & valid
    x_b.recv()
    logits, squares = from_fixed(rb[0], vc)
    for p in range(1, nv):
        more = from_fixed(rb[p], vc)
        logits, squares = logits + more[0], squares + more[1]
    scale = lax.rsqrt(squares / width + EPS)
    logits = logits * scale
    peak = jnp.max(jnp.where(valid, logits, -3e38), axis=1, keepdims=True)
    grown = jnp.where(valid, jnp.exp(jnp.minimum(logits - peak, 0.0)), 0.0)
    total = jnp.sum(grown, axis=1, keepdims=True)
    moment = jnp.sum(grown * jnp.where(valid, logits, 0.0), axis=1, keepdims=True)
    picked = jnp.sum(jnp.where(onehot, logits, 0.0), axis=1, keepdims=True)

    eye = lax.broadcasted_iota(jnp.int32, (rv, 128), 0) == lax.broadcasted_iota(jnp.int32, (rv, 128), 1)
    to_row = lambda x: jnp.sum(jnp.where(eye, x, 0.0), axis=0, keepdims=True)
    to_col = lambda x: jnp.sum(jnp.where(eye, x, 0.0), axis=1, keepdims=True)

    def put(ref, at, values):
        for i, value in enumerate(values):
            ref[at, i : i + 1, :] = value
        ref[at, len(values) :, :] = jnp.zeros((8 - len(values), 128), F32)

    def merge(ref, n):
        top = ref[0, 0:1, :]
        for p in range(1, n):
            top = jnp.maximum(top, ref[p, 0:1, :])
        tot = mom = pick = jnp.zeros((1, 128), F32)
        for p in range(n):
            by = jnp.exp(ref[p, 0:1, :] - top)
            tot = tot + by * ref[p, 1:2, :]
            mom = mom + by * ref[p, 2:3, :]
            pick = pick + ref[p, 3:4, :]
        return top, tot, mom, pick

    put(st1, g, [to_row(peak), to_row(total), to_row(moment), to_row(picked)])
    x_s1.start()
    out = jnp.where(onehot, 0.0, grown)
    for i, value in enumerate(split3(peak)):
        out = jnp.where(lanes == vc + i, value, out)
    ef[pl.ds(pl.multiple_of(v * rv, rv), rv), :] = out.astype(BF16)
    x_c.start(1, nv // 2)
    weight_row, scale_row, tgt_row = to_row(weight), to_row(scale), to_row(tgt)
    x_s1.recv()
    put(st2, y, merge(st1, ng))
    x_s2.start()
    x_c.start(nv // 2)
    x_s2.recv()
    top, tot, mom, pick = merge(st2, ny)
    lse = top + jnp.log(tot)
    inner = weight_row * (mom / tot - pick)
    missed = weight_row * (jnp.exp(jnp.minimum(pick - lse, 0.0)) - 1.0)
    put(st3, v, [scale_row, inner, lse, missed, weight_row * (lse - pick), weight_row, tgt_row])
    x_s3.start()
    x_act.start()
    x_s3.recv()
    x_c.recv()

    def logit_grads(k, loss):
        at = pl.ds(pl.multiple_of(k * rv, rv), rv)
        scale_k, inner_k, lse_k, missed_k, _, weight_k, tgt_k = (to_col(st3[k, i : i + 1, :]) for i in range(7))
        grown_k = ef[at, :].astype(F32)
        peak_k = grown_k[:, vc : vc + 1] + grown_k[:, vc + 1 : vc + 2] + grown_k[:, vc + 2 : vc + 3]
        prob = (weight_k * jnp.exp(jnp.minimum(peak_k - lse_k, 0.0))) * grown_k
        df[at, :] = jnp.where(valid, jnp.where(column == tgt_k, missed_k, prob), 0.0).astype(BF16)
        rowv[at, 0:1] = scale_k
        rowv[at, 1:2] = inner_k
        return loss + st3[k, 4:5, :]

    loss = lax.fori_loop(0, nv, logit_grads, jnp.zeros((1, 128), F32))
    in_use = lax.broadcasted_iota(jnp.int32, (1, 128), 1) < rv
    loss_ref[...] = jnp.sum(jnp.where(in_use, loss, 0.0), axis=1, keepdims=True) / rows

    hy = ny // 2

    def rows_of(core, i):
        lhs = jnp.concatenate(
            [
                df[pl.ds(pl.multiple_of(k * rv + core * rh, rh), rh), :]
                for k in range(i * hy, (i + 1) * hy)
            ],
            axis=0,
        )
        out = lax.dot_general(lhs, headp[...], (((1,), (0,)), ((), ())), preferred_element_type=F32)
        return out.reshape(hy, rh, width_part)

    def to_other(i):
        at = pl.ds(i * hy, hy)
        return to_core(po.at[at], rc.at[at], s_dc.at[0, i], s_dc.at[1, i])

    for i in range(2):
        po[i * hy : (i + 1) * hy] = rows_of(o, i).astype(BF16)
        to_other(i).start()
    for i in range(2):
        pm[i * hy : (i + 1) * hy] = rows_of(c, i)
    for i in range(2):
        to_other(i).wait_recv()

    wk = width_part // 8

    def pack0(k, _):
        both = pm[k] + rc[k].astype(F32)
        pm[k] = both
        last = [both[zz * 8 + 6 : zz * 8 + 8] for zz in range(nz)]
        q1[k] = stack(jnp.concatenate(last, axis=0)).astype(BF16)
        return 0

    lax.fori_loop(0, ny, pack0, 0)
    x_q1.start()
    rq1[y] = q1[y]

    def pack1(k, _):
        d1[k] = pm[k, :, :half].astype(BF16)
        return 0

    lax.fori_loop(0, ny, pack1, 0)
    x_d1.start()
    rd1[y] = d1[y]

    def pack2(k, _):
        for zz in range(nz):
            pair = jnp.concatenate(
                [pm[2 * k, zz * 8 : zz * 8 + 8, half:], pm[2 * k + 1, zz * 8 : zz * 8 + 8, half:]], axis=0
            )
            d2[zz, pl.ds(pl.multiple_of(k * 16, 16), 16), :] = pair.astype(BF16)
        return 0

    lax.fori_loop(0, ny // 2, pack2, 0)
    x_d2.start()
    rd2[z] = d2[z]

    x_q1.recv()
    line = rq1[0].astype(F32)
    for p in range(1, ny):
        line = line + rq1[p].astype(F32)
    rq2[z] = line
    x_q2.start()

    def norm(k, total):
        at = pl.ds(pl.multiple_of(k * rv, rv), rv)
        hg[at, :] = (hr[at, :].astype(F32) * rowv[at, 0:1] * gain_ref[...]).astype(BF16)
        mine = pl.ds(pl.multiple_of(k * rv + c * rh, rh), rh)
        return total + jnp.sum(pm[k] * hr[mine, :].astype(F32) * rowv[mine, 0:1], axis=0, keepdims=True)

    gain_part = lax.fori_loop(0, ny, norm, jnp.zeros((1, width_part), F32))
    for k in range(8):
        gg1[y, k : k + 1, :] = gain_part[:, k * wk : (k + 1) * wk]
    x_g1.start()

    mine = pl.ds(pl.multiple_of(y * rv + c * rh, rh), rh)
    of_last = lambda x: jnp.concatenate([x[zz * 8 + 6 : zz * 8 + 8] for zz in range(nz)], axis=0)
    h_last = of_last(hr[mine, :].astype(F32))
    scale_last = of_last(rowv[mine, 0:1])
    inner_last = of_last(rowv[mine, 1:2])
    x_q2.recv()
    line = rq2[0]
    for p in range(1, nz):
        line = line + rq2[p]
    grad_last = jnp.concatenate([line[: 2 * nz], line[2 * nz :]], axis=1)
    rows_last = scale_last * (grad_last * gain_ref[...]) - h_last * (
        scale_last * scale_last * inner_last / width
    )
    ls[c, y] = stack(rows_last).astype(BF16)

    def pass_on(p):
        ref = ls.at[c, p]
        return to_core(ref, ref, s_ec.at[0, p], s_ec.at[1, p])

    x_e.start()
    pass_on(y).start()

    wt = min(width_part, 256)
    for m in range(0, width_part, wt):
        part = lax.dot_general(
            df[...], hg[:, m : m + wt], (((0,), (0,)), ((), ())), preferred_element_type=F32
        )
        gheadv[:, m : m + wt] = part[:vc].astype(BF16)
    store_head = pltpu.make_async_copy(gheadv, ghead_ref, s_out.at[0])
    store_head.start()
    x_act.recv()

    def acts_in(p, _):
        tile = act[p].astype(F32)
        parts = [tile[zz * 4 + cc * 2 : zz * 4 + cc * 2 + 2] for cc in range(2) for zz in range(nz)]
        act[p] = jnp.concatenate(parts, axis=0).astype(BF16)
        return 0

    x_act.sent()
    lax.fori_loop(0, nv, acts_in, 0)

    x_d1.recv()
    sum1 = rd1[0].astype(F32)
    for p in range(1, ny):
        sum1 = sum1 + rd1[p].astype(F32)
    for zz in range(nz):
        d1b[zz] = stack(sum1[zz * 8 : zz * 8 + 8]).astype(BF16)
    x_d3.start()
    rd1b[z] = d1b[z]
    x_d2.recv()
    sum2 = rd2[0].astype(F32)
    for p in range(1, nz):
        sum2 = sum2 + rd2[p].astype(F32)
    for k in range(ny):
        d2b[k] = stack(sum2[k * 8 : k * 8 + 8]).astype(BF16)
    x_d4.start()
    rd2b[y] = d2b[y]
    x_g1.recv()
    gain_y = gg1[0]
    for p in range(1, ny):
        gain_y = gain_y + gg1[p]
    gg2[g] = gain_y
    x_g2.start()

    x_e.recv(lambda p: pass_on(p).start())

    def rows_out(j, _):
        p = nearest(j)
        ref = ls.at[o, p]
        to_core(ref, ref, s_ec.at[0, p], s_ec.at[1, p]).wait_recv()
        a, b = ls[0, p].astype(F32), ls[1, p].astype(F32)
        lr[p, :, :half] = jnp.concatenate([a[: 2 * nz], b[: 2 * nz]], axis=0).astype(BF16)
        lr[p, :, half:] = jnp.concatenate([a[2 * nz :], b[2 * nz :]], axis=0).astype(BF16)
        return 0

    lax.fori_loop(0, ny, rows_out, 0)
    tokens = ny * lr.shape[1]
    last = lr[...].reshape(tokens, width_part)
    load_down.wait()
    part = lax.dot_general(last, dwv[...], (((1,), (1,)), ((), ())), preferred_element_type=F32)
    tv = tokens // nv
    lanes_f = lax.broadcasted_iota(jnp.int32, (tv, fp.shape[2]), 1)
    for p in range(nv):
        fp[p] = to_fixed(part[p * tv : (p + 1) * tv], jnp.zeros((tv, 1), F32), lanes_f, ff)
    x_f.start()
    rf[v] = fp[v]
    acts = act[...].reshape(tokens, act.shape[2])
    down = lax.dot_general(acts, last, (((0,), (0,)), ((), ())), preferred_element_type=F32)
    gdownv[...] = down[:ff].astype(BF16)
    store_down = pltpu.make_async_copy(gdownv, gdown_ref, s_out.at[1])
    store_down.start()

    x_d3.recv()
    g1 = rd1b[0].astype(F32)
    for p in range(1, nz):
        g1 = g1 + rd1b[p].astype(F32)
    x_d4.recv()
    g2 = rd2b[0].astype(F32)
    for p in range(1, ny):
        g2 = g2 + rd2b[p].astype(F32)
    grad_own = jnp.concatenate([g1[:8], g1[8:], g2[:8], g2[8:]], axis=1)
    own_at = pl.ds(pl.multiple_of(y * rv + c * rh + z * 8, 8), 8)
    scale_own = rowv[own_at, 0:1]
    inner_own = rowv[own_at, 1:2]
    ghs[...] = scale_own * (grad_own * gain_ref[...]) - hown[...] * (
        scale_own * scale_own * inner_own / width
    )
    for e in range(EXITS):
        gh_ref[e] = ghs[2 * e : 2 * e + 2, :].astype(BF16)
    x_g2.recv()
    gain_all = gg2[0]
    for p in range(1, ng):
        gain_all = gain_all + gg2[p]
    for k in range(8):
        ggain_ref[:, k * wk : (k + 1) * wk] = gain_all[k : k + 1, :]

    x_f.recv()
    acc = from_fixed(rf[0], ff)[0]
    for p in range(1, nv):
        acc = acc + from_fixed(rf[p], ff)[0]
    for zz in range(nz):
        for cc in range(2):
            to = zz * 4 + cc * 2
            at = cc * 2 * nz + zz * 2
            gactv[to : to + 2, :] = acc[at : at + 2, :ff]
    gact_ref[...] = gactv[...].astype(BF16)

    each(nz, z, finish(own_z))
    each(ny, y, finish(own_y))
    lax.fori_loop(0, nz, lambda zz, _: (each(ny, y, finish(on_y(zz))), 0)[1], 0)
    lax.fori_loop(0, ny, lambda yy, _: (each(nz, z, finish(on_z(yy))), 0)[1], 0)
    lax.fori_loop(0, ny, lambda yy, _: (across(yy).wait_send(), 0)[1], 0)
    lax.fori_loop(0, ny, lambda p, _: (pass_on(p).wait_send(), 0)[1], 0)
    each(nv, v, lambda p, _: to_tokens(p).wait_send())
    x_s1.sent()
    x_s2.sent()
    x_s3.sent()
    x_c.sent()
    for i in range(2):
        to_other(i).wait_send()
    x_d1.sent()
    x_d2.sent()
    x_d3.sent()
    x_d4.sent()
    x_q1.sent()
    x_q2.sent()
    x_g1.sent()
    x_e.sent()
    x_g2.sent()
    x_f.sent()
    store_head.wait()
    store_down.wait()


def hand_on_kernel(n, *refs):
    ins, outs, held, sems = refs[:n], refs[n : 2 * n], refs[2 * n : 3 * n], refs[3 * n]
    load = [pltpu.make_async_copy(ins[i], held[i], sems.at[0, i]) for i in range(n)]
    store = [pltpu.make_async_copy(held[i], outs[i], sems.at[1, i]) for i in range(n)]
    for copy in load:
        copy.start()
    for i in range(n):
        load[i].wait()
        store[i].start()
    for copy in store:
        copy.wait()


def hand_on(arrays):
    n = len(arrays)
    hbm = pl.BlockSpec(memory_space=pl.ANY)
    return pl.pallas_call(
        functools.partial(hand_on_kernel, n),
        out_shape=tuple(jax.ShapeDtypeStruct(a.shape, a.dtype) for a in arrays),
        in_specs=[hbm] * n,
        out_specs=(hbm,) * n,
        scratch_shapes=[pltpu.VMEM(a.shape, a.dtype) for a in arrays] + [pltpu.SemaphoreType.DMA((2, n))],
        compiler_params=pltpu.CompilerParams(vmem_limit_bytes=56 * 1024 * 1024),
    )(*arrays)


def body(ny, nz, hidden, norm_gain, head, targets, scale_index, layer_act, down_weight):
    nv = lax.axis_size("vocab")
    exits, own_tokens, w = hidden.shape
    vc = head.shape[1]
    tok_v, ff = layer_act.shape
    fpad = -(-ff // 128) * 128
    ng = 2 * nz
    rv = OWN * ng
    rh = rv // 2
    rows = rv * ny
    half, q, wk = w // 2, w // 4, w // 8
    tok_y = own_tokens * ng
    vm = pltpu.VMEM
    sem = lambda *n: pltpu.SemaphoreType.DMA(n)
    dma = lambda n: sem(2, n)
    scratch = [
        vm((OWN, w), F32), vm((2, ny, nz, 2, 16, q), BF16),
        vm((nv, tok_v, fpad), BF16), vm((vc, w), BF16), vm((VP, w), BF16), vm((fpad, w), BF16),
        vm((vc, w), BF16), vm((ff, w), BF16), vm((rows, w), BF16), vm((rows, w), BF16),
        vm((nv, rv, VP), jnp.int16), vm((nv, rv, VP), jnp.int16),
        vm((ng, 8, 128), F32), vm((ny, 8, 128), F32), vm((nv, 8, 128), F32),
        vm((rows, VP), BF16), vm((rows, VP), BF16), vm((rows, 128), F32),
        vm((ny, rh, w), BF16), vm((ny, rh, w), F32), vm((ny, rh, w), BF16),
        vm((ny, rh, half), BF16), vm((nz, ny * 8, half), BF16),
        vm((ny, rh, half), BF16), vm((nz, ny * 8, half), BF16),
        vm((nz, 16, q), BF16), vm((ny, 16, q), BF16), vm((nz, 16, q), BF16), vm((ny, 16, q), BF16),
        vm((OWN, w), F32), vm((ny, 4 * nz, half), BF16), vm((ny, 4 * nz, half), BF16), vm((nz, 4 * nz, half), F32),
        vm((ny, 8, wk), F32), vm((ng, 8, wk), F32),
        vm((2, ny, 4 * nz, half), BF16), vm((ny, tok_y, w), BF16),
        vm((nv, tok_v, fpad), jnp.int16), vm((nv, tok_v, fpad), jnp.int16), vm((tok_v, ff), F32),
        dma(nv), sem(2), sem(2), sem(2, ny, nz), sem(nz), sem(nz, ny), sem(ny), sem(ny, nz), dma(ny),
        dma(nv), dma(ng), dma(ny), dma(nv), dma(nv),
        dma(2), dma(ny), dma(nz), dma(nz), dma(ny),
        dma(ny), dma(nz), dma(ny), dma(ny), dma(ng), dma(ny), dma(nv),
    ]
    spec = pl.BlockSpec(memory_space=vm)
    hbm = pl.BlockSpec(memory_space=pl.ANY)
    sds = jax.ShapeDtypeStruct
    results = pl.pallas_call(
        functools.partial(kernel, ny, nz, nv, vc),
        out_shape=(
            sds((1, 1), F32), sds(hidden.shape, BF16), sds((vc, w), BF16), sds((1, w), F32),
            sds(layer_act.shape, BF16), sds(down_weight.shape, BF16),
        ),
        in_specs=[spec, spec, hbm, spec, spec, spec, hbm],
        out_specs=(spec, spec, hbm, spec, spec, hbm),
        scratch_shapes=scratch,
        compiler_params=pltpu.CompilerParams(
            collective_id=0, has_side_effects=True, vmem_limit_bytes=56 * 1024 * 1024
        ),
    )(
        hidden, norm_gain.reshape(1, w), head.T, targets.reshape(1, -1), scale_index, layer_act, down_weight
    )
    loss, grad_hidden, grad_head, grad_gain, grad_act, grad_down = hand_on(results)
    return loss[0, 0], grad_hidden, grad_head.T, grad_gain.reshape(w), grad_act, grad_down


def solution(mesh, ny=8, nz=4):
    return jax.shard_map(
        functools.partial(body, ny, nz),
        mesh=mesh,
        in_specs=(
            P(None, "fsdp", "vocab"),
            P("vocab"),
            P("vocab", "fsdp"),
            P("vocab"),
            P(None, "vocab"),
            P("vocab", "fsdp"),
            P("fsdp", "vocab"),
        ),
        out_specs=(
            P(),
            P(None, "fsdp", "vocab"),
            P("vocab", "fsdp"),
            P("vocab"),
            P("vocab", "fsdp"),
            P("fsdp", "vocab"),
        ),
        check_vma=False,
    )
```
